32 devices in a mesh: dp: 8 (over z, y), tensor: 4 (over x, core).
Axes of the slice: x: 2, y: 2, z: 4, core: 2. Of those that a mesh axis runs over, the one named last changes fastest.
Arguments:
- tokens: bfloat16 [9600, 768], P('dp'), may hold values from -6 to 6
- lengths: int32 [8], P('dp'), may hold values from 576 to 1200, as said below
- gain_one: float32 [768], replicated, may hold values from 0.1 to 1.9
- gain_two: float32 [768], replicated, may hold values from 0.1 to 1.9
- w_qkv: bfloat16 [3, 768, 768], P(None, None, 'tensor'), may hold values from -0.21875 to 0.21875
- w_out: bfloat16 [768, 768], P('tensor'), may hold values from -2.5 to 2.5
- w_up: bfloat16 [768, 3072], P(None, 'tensor'), may hold values from -0.21875 to 0.21875
- w_down: bfloat16 [3072, 768], P('tensor'), may hold values from -0.109375 to 0.109375
- w_tap: bfloat16 [768, 256], P(None, 'tensor'), may hold values from -0.21875 to 0.21875
- w_conv: bfloat16 [4, 3, 3, 256, 256], P(None, None, None, None, 'tensor'), may hold values from -0.125 to 0.125
- cot_tokens: bfloat16 [9600, 768], P('dp'), may hold values from -6 to 6
- cot_joined: bfloat16 [8, 60, 80, 256], P('dp', None, None, 'tensor'), may hold values from -6 to 6
Outputs:
- out_tokens: bfloat16 [9600, 768], P('dp')
- joined: bfloat16 [8, 60, 80, 256], P('dp', None, None, 'tensor')
- grad_tokens: bfloat16 [9600, 768], P('dp')
- grad_qkv: float32 [3, 768, 768], P(None, None, 'tensor')
- grad_out: float32 [768, 768], P('tensor')
- grad_up: float32 [768, 3072], P(None, 'tensor')
- grad_down: float32 [3072, 768], P('tensor')
- grad_tap: float32 [768, 256], P(None, 'tensor')
- grad_conv: float32 [4, 3, 3, 256, 256], P(None, None, None, None, 'tensor')
- grad_gain_one: float32 [768], replicated
- grad_gain_two: float32 [768], replicated
The draws below stay inside these ranges and needn't reach their ends.
Inputs may be any that keep to these rules, and one draw needn't show every extreme that they name: `lengths`: every image holds 576 or 1200 patch tokens; both values occur in every draw.
All inputs are finite; a program needn't handle non-finite values.
Results may differ from the reference program's by a relative error of at most 0.028.
Values may be sent and summed in bfloat16 or wider, within the bound.
A program may use at most 192 MiB of HBM per device.

```python
import jax
import jax.numpy as jnp
from jax import lax

D = 768
HEADS = 12
HEAD_DIM = 64
FF = 3072
CH = 256
GH = 30
GW = 40
SH = 24
SW = 24
IMAGES = 8
TOKENS = 9600


def draw_lengths(key, part):
    key = jax.random.fold_in(key, 7)
    pick_key, order_key = jax.random.split(key)
    larger = jax.random.randint(pick_key, (IMAGES,), 0, 3) == 0
    base = jnp.where(larger, GH * GW, SH * SW).astype(jnp.int32)
    base = base.at[0].set(GH * GW).at[1].set(SH * SW)
    return base[jax.random.permutation(order_key, IMAGES)]


def steps_of(rng, extent, cuts, least, top_value):
    factor_of, own = 1.0, jax.random.fold_in(rng, 6)
    for axis_at, parts in cuts:
        heights = jnp.exp(jax.random.uniform(jax.random.fold_in(own, axis_at), (parts,), jnp.float32, least / len(cuts), top_value / len(cuts)))
        factor_of = factor_of * jnp.repeat(heights, extent[axis_at] // parts).reshape([-1 if axis == axis_at else 1 for axis in range(len(extent))])
    return factor_of


def scatter_about(key, shape, scale, bound, cuts=(), kind=jnp.bfloat16):
    drawn = scale * jax.random.normal(key, shape, jnp.float32)
    if cuts:
        drawn = drawn * steps_of(key, shape, cuts, -0.22, 0.18)
    return jnp.clip(drawn, -bound, bound).astype(kind)


def setup_inputs(seed: int = 0) -> dict:
    key_list = jax.random.split(jax.random.key(seed), 13)
    return {
        "tokens": scatter_about(key_list[0], (TOKENS, D), 1.0, 6.0, ((0, 8),)),
        "lengths": draw_lengths(jax.random.fold_in(key_list[12], 71), 0),
        "gain_one": jnp.clip(1.0 + 0.18 * jax.random.normal(key_list[2], (D,), jnp.float32), 0.1, 1.9),
        "gain_two": jnp.clip(1.0 + 0.18 * jax.random.normal(key_list[3], (D,), jnp.float32), 0.1, 1.9),
        "w_qkv": scatter_about(key_list[4], (3, D, D), D ** -0.5, 0.21875, ((2, 4),)),
        "w_out": scatter_about(key_list[5], (D, D), (max(D // 128, 1)) ** -0.5, 2.5, ((0, 4),)),
        "w_up": scatter_about(key_list[6], (D, FF), D ** -0.5, 0.21875, ((1, 4),)),
        "w_down": scatter_about(key_list[7], (FF, D), FF ** -0.5, 0.109375, ((0, 4),)),
        "w_tap": scatter_about(key_list[8], (D, CH), D ** -0.5, 0.21875, ((1, 4),)),
        "w_conv": scatter_about(key_list[9], (4, 3, 3, CH, CH), (9 * CH) ** -0.5, 0.125, ((4, 4),)),
        "cot_tokens": scatter_about(key_list[10], (TOKENS, D), 1.0, 6.0, ((0, 8),)),
        "cot_joined": scatter_about(key_list[11], (IMAGES, 2 * GH, 2 * GW, CH), 1.0, 6.0, ((0, 8), (3, 4))),
    }


highest = lax.Precision.HIGHEST

@jax.custom_vjp
def low(v):
    return lax.optimization_barrier(v.astype(jnp.bfloat16)).astype(jnp.float32)

@jax.custom_vjp
def low_back(v):
    return v

def low_keep(v):
    return (low(v), None)

def low_pass(kept, grad):
    return (grad,)

def back_keep(v):
    return (v, None)

def back_low(kept, grad):
    return (low(grad),)
low.defvjp(low_keep, low_pass)
low_back.defvjp(back_keep, back_low)

def grid_mask(lengths):
    larger = lengths == GH * GW
    height = jnp.where(larger, GH, SH).astype(jnp.int32)
    breadth = jnp.where(larger, GW, SW).astype(jnp.int32)
    down_index = jnp.arange(GH, dtype=jnp.int32)
    across_index = jnp.arange(GW, dtype=jnp.int32)
    inside = (down_index[None, :, None] < height[:, None, None]) & (across_index[None, None, :] < breadth[:, None, None])
    return jnp.where(inside, 1.0, 0.0).astype(jnp.float32)

def upsample_table(count):
    target = jnp.arange(2 * count, dtype=jnp.int32)
    source = jnp.arange(count, dtype=jnp.int32)
    nearest = target // 2
    further = jnp.clip(nearest + 2 * (target % 2) - 1, 0, count - 1)
    table = 0.75 * (source[None, :] == nearest[:, None]) + 0.25 * (source[None, :] == further[:, None])
    return table.astype(jnp.float32)

def layer_norm(values, gain):
    centred = values - lax.optimization_barrier(jnp.mean(values, axis=-1, keepdims=True))
    spread = lax.optimization_barrier(jnp.mean(centred * centred, axis=-1, keepdims=True))
    return centred * lax.rsqrt(spread + 1e-06) * gain

def convolve(field, weight):
    height, breadth = (field.shape[1], field.shape[2])
    padded = jnp.pad(field, ((0, 0), (1, 1), (1, 1), (0, 0)))
    total = jnp.zeros(field.shape[:3] + (weight.shape[3],), jnp.float32)
    for offset_row in range(3):
        for offset_col in range(3):
            window = padded[:, offset_row:offset_row + height, offset_col:offset_col + breadth, :]
            total = total + jnp.einsum('bhwc,co->bhwo', window, weight[offset_row, offset_col], precision=highest)
    return total

def attend(item):
    heads_block, key_mask = item
    queries, keys_part, values = (heads_block[:, 0], heads_block[:, 1], heads_block[:, 2])
    raw_scores = low_back(jnp.einsum('qhd,khd->hqk', queries, keys_part, precision=highest))
    scores = jnp.where(key_mask[None, None, :] > 0.5, raw_scores * HEAD_DIM ** (-0.5), -1e+30)
    maximum = lax.optimization_barrier(jnp.max(scores, axis=-1, keepdims=True))
    weights = jnp.exp(scores - maximum)
    probabilities = weights / lax.optimization_barrier(jnp.sum(weights, axis=-1, keepdims=True))
    return jnp.einsum('hqk,khd->qhd', low(probabilities), values, precision=highest)

def forward(tokens_in, gain_one, gain_two, w_qkv, w_out, w_up, w_down, w_tap, w_conv, token_mask, grid_cells):
    slots = GH * GW
    normed_one = low(layer_norm(tokens_in, gain_one))
    qkv = jnp.einsum('td,sde->tse', normed_one, w_qkv, precision=highest)
    qkv = low(low_back(qkv)).reshape(IMAGES, slots, 3, HEADS, HEAD_DIM)
    masks = token_mask.reshape(IMAGES, slots)
    mixed = lax.map(jax.checkpoint(attend), (qkv, masks)).reshape(IMAGES * slots, D)
    mixed = low(low_back(mixed))
    hidden_one = tokens_in + low_back(jnp.dot(mixed, w_out, precision=highest))
    normed_two = low(layer_norm(hidden_one, gain_two))
    pre_act = low_back(jnp.dot(normed_two, w_up, precision=highest))
    activation = low(jax.nn.gelu(pre_act, approximate=False))
    hidden_two = hidden_one + low_back(jnp.dot(activation, w_down, precision=highest))
    block_out = token_mask[:, None] * hidden_two
    field = low_back(jnp.dot(low(block_out), w_tap, precision=highest)).reshape(IMAGES, GH, GW, CH)
    cells = grid_cells[..., None]
    for unit in range(2):
        unit_in = low(jax.nn.gelu(field, approximate=False))
        first = cells * low_back(convolve(unit_in, w_conv[2 * unit]))
        mid_in = low(jax.nn.gelu(first, approximate=False))
        second = cells * low_back(convolve(mid_in, w_conv[2 * unit + 1]))
        field = field + second
    table_rows = upsample_table(GH)
    table_cols = upsample_table(GW)
    joined = jnp.einsum('ra,bacd->brcd', table_rows, field, precision=highest)
    joined = jnp.einsum('sc,brcd->brsd', table_cols, joined, precision=highest)
    return (block_out, joined)

def reference(tokens, lengths, gain_one, gain_two, w_qkv, w_out, w_up, w_down, w_tap, w_conv, cot_tokens, cot_joined):
    grid_cells = grid_mask(lengths)
    token_mask = grid_cells.reshape(IMAGES * GH * GW)

    def wrapped(tokens_in, gain_a, gain_b, qkv_weight, out_weight, up_weight, down_weight, tap_weight, conv_weight):
        return forward(tokens_in, gain_a, gain_b, qkv_weight, out_weight, up_weight, down_weight, tap_weight, conv_weight, token_mask, grid_cells)
    primals = (tokens.astype(jnp.float32), gain_one.astype(jnp.float32), gain_two.astype(jnp.float32), w_qkv.astype(jnp.float32), w_out.astype(jnp.float32), w_up.astype(jnp.float32), w_down.astype(jnp.float32), w_tap.astype(jnp.float32), w_conv.astype(jnp.float32))
    outputs, pullback = jax.vjp(wrapped, *primals)
    grads = pullback((cot_tokens.astype(jnp.float32), cot_joined.astype(jnp.float32)))
    return (outputs[0].astype(jnp.bfloat16), outputs[1].astype(jnp.bfloat16), grads[0].astype(jnp.bfloat16), grads[3], grads[4], grads[5], grads[6], grads[7], grads[8], grads[1], grads[2])
```

```python
import functools

import jax
import jax.numpy as jnp
from jax import lax
from jax.experimental import pallas as pl
from jax.experimental.pallas import tpu as pltpu
from jax.sharding import PartitionSpec as P

HEAD_DIM = 64
GH = 30
GW = 40
SH = 24
SW = 24
SLOTS = GH * GW
D = 768
CH = 256
BLOCK = 64
TAPS = 9
WIDE = TAPS * BLOCK
PART = 304
ROWS = 4 * PART
LANES = 1280
CHUNK = 256
SLOT = 128
F32 = jnp.float32
BF16 = jnp.bfloat16
MESH = pl.DeviceIdType.MESH
VMEM_LIMIT = 56 * 2**20

vmem = pl.BlockSpec(memory_space=pltpu.VMEM)
smem = pl.BlockSpec(memory_space=pltpu.SMEM)
anywhere = pl.BlockSpec(memory_space=pl.ANY)


def dot(a, b, dims=(1, 0)):
    return lax.dot_general(
        a, b, (((dims[0],), (dims[1],)), ((), ())), preferred_element_type=F32
    )


def gelu(v):
    return 0.5 * v * (1.0 + lax.erf(v * 0.7071067811865476))


def gelu_slope(v):
    return (
        0.5 * (1.0 + lax.erf(v * 0.7071067811865476))
        + v * jnp.exp(-0.5 * v * v) * 0.3989422804014327
    )


def norm(v):
    centred = v - jnp.mean(v, axis=-1, keepdims=True)
    spread = jnp.mean(centred * centred, axis=-1, keepdims=True)
    inverse = lax.rsqrt(spread + 1e-06)
    return centred * inverse, inverse


def norm_back(incoming, scaled, inverse, gain):
    weighted = incoming * gain
    inner = (
        weighted
        - jnp.mean(weighted, axis=-1, keepdims=True)
        - scaled * jnp.mean(weighted * scaled, axis=-1, keepdims=True)
    )
    return inverse * inner, jnp.sum(incoming * scaled, axis=0, keepdims=True)


def grid_place(shape, axis, offset):
    index = (lax.broadcasted_iota(jnp.int32, shape, axis) + offset).astype(F32)
    row = jnp.floor((index + 0.5) * (1.0 / GW))
    return row, index - GW * row


def cell_mask(shape, axis, offset, length):
    row, col = grid_place(shape, axis, offset)
    large = length == SLOTS
    height = jnp.where(large, float(GH), float(SH))
    breadth = jnp.where(large, float(GW), float(SW))
    return jnp.where((row < height) & (col < breadth), 1.0, 0.0)


class Peers:
    def __init__(self):
        self.dp = lax.axis_index("dp")
        self.t = lax.axis_index("tensor")
        self.sib = self.t + 1 - 2 * lax.rem(self.t, 2)
        self.xp = lax.rem(self.t + 2, 4)
        self.diag = lax.rem(self.sib + 2, 4)
        self.mate = self.dp + 1 - 2 * lax.rem(self.dp, 2)

    def greet(self, mate=False):
        barrier = pltpu.get_barrier_semaphore()
        others = [(self.dp, self.sib), (self.dp, self.xp)]
        if mate:
            others.append((self.mate, self.t))
        for other in others:
            pl.semaphore_signal(barrier, inc=1, device_id=other, device_id_type=MESH)
        pl.semaphore_wait(barrier, len(others))


class Links:
    def __init__(self, send, recv):
        self.send, self.recv, self.used = send, recv, 0

    def copy(self, src, dst, device):
        at = self.used
        self.used += 1
        return pltpu.make_async_remote_copy(
            src_ref=src,
            dst_ref=dst,
            send_sem=self.send.at[at],
            recv_sem=self.recv.at[at],
            device_id=device,
            device_id_type=MESH,
        )


class Gather:
    def __init__(self, links, peers, place):
        p = peers
        self.x = links.copy(place(p.t), place(p.t), (p.dp, p.xp))
        self.c = links.copy(place(p.t), place(p.t), (p.dp, p.sib))
        self.f = links.copy(place(p.xp), place(p.xp), (p.dp, p.sib))

    def start(self):
        self.x.start()
        self.c.start()

    def forward(self):
        self.x.wait_recv()
        self.f.start()

    def finish(self):
        self.c.wait_recv()
        self.f.wait_recv()
        self.x.wait_send()
        self.c.wait_send()
        self.f.wait_send()


class Scatter:
    def __init__(self, links, peers, out_c, out_x, in_c, in_x):
        p = peers
        self.p, self.out_c, self.out_x, self.in_c, self.in_x = p, out_c, out_x, in_c, in_x
        self.c = [links.copy(out_c.at[i], in_c.at[i], (p.dp, p.sib)) for i in range(2)]
        self.x = links.copy(out_x, in_x, (p.dp, p.xp))

    def run(self, part):
        p = self.p
        self.out_c[0] = part(p.diag).astype(BF16)
        self.c[0].start()
        mine = part(p.xp)
        self.c[0].wait_recv()
        self.out_x[...] = (mine + self.in_c[0].astype(F32)).astype(BF16)
        self.x.start()
        self.out_c[1] = part(p.sib).astype(BF16)
        self.c[1].start()
        mine = part(p.t)
        self.c[1].wait_recv()
        mine = mine + self.in_c[1].astype(F32)
        self.x.wait_recv()
        total = mine + self.in_x[...].astype(F32)
        self.c[0].wait_send()
        self.c[1].wait_send()
        self.x.wait_send()
        return total


def sems(count):
    return [pltpu.SemaphoreType.DMA((count,)), pltpu.SemaphoreType.DMA((count,))]


def part_at(ref, owner):
    return ref.at[pl.ds(pl.multiple_of(owner * PART, 16), PART), :]


def call(kernel, outs, ins, scratch, collective, flops, args):
    return pl.pallas_call(
        kernel,
        out_shape=[jax.ShapeDtypeStruct(*o) for o in outs],
        in_specs=ins,
        out_specs=[vmem] * len(outs),
        scratch_shapes=scratch,
        cost_estimate=pl.CostEstimate(
            flops=flops, bytes_accessed=20_000_000, transcendentals=0
        ),
        compiler_params=pltpu.CompilerParams(
            collective_id=collective,
            has_side_effects=True,
            vmem_limit_bytes=VMEM_LIMIT,
        )
        if collective is not None
        else pltpu.CompilerParams(vmem_limit_bytes=VMEM_LIMIT),
    )(*args)


def attend_kernel(
    length, tok_hbm, gain_one, gain_two, w_qkv, w_out, w_tap, w_conv,
    hidden, normed_two, q_tm, k_tm, v_tm, lse, mixed, normed_one, tap_all, conv_x,
    tok, mixed_all, out_all, v_cm, local, send, recv,
):
    p = Peers()
    links = Links(send, recv)
    bring = pltpu.make_async_copy(tok_hbm, tok.at[pl.ds(0, SLOTS), :], local.at[0])
    bring.start()
    tok[SLOTS:, :] = jnp.zeros((ROWS - SLOTS, D), BF16)
    p.greet()
    own_out = out_all.at[pl.ds(pl.multiple_of(p.t * 192, 64), 192), :]
    own_tap = tap_all.at[pl.ds(pl.multiple_of(p.t * 64, 64), 64), :]
    own_out[...] = w_out[...]
    own_tap[...] = w_tap[...]
    place_out = lambda t: out_all.at[pl.ds(pl.multiple_of(t * 192, 64), 192), :]
    place_tap = lambda t: tap_all.at[pl.ds(pl.multiple_of(t * 64, 64), 64), :]
    g_out = Gather(links, p, place_out)
    g_tap = Gather(links, p, place_tap)
    half = lax.rem(p.dp, 2) * 2
    c_conv = links.copy(w_conv.at[pl.ds(half, 2)], conv_x, (p.dp, p.xp))
    g_out.start()
    g_tap.start()
    c_conv.start()
    bring.wait()
    q_tm[:, ROWS:, :] = jnp.zeros((3, LANES - ROWS, SLOT), BF16)
    lane = lax.broadcasted_iota(jnp.int32, (PART, SLOT), 1)

    def project(i, carry):
        off = pl.multiple_of(i * PART, 16)
        rows = pl.ds(off, PART)
        scaled, _ = norm(tok[rows, :].astype(F32))
        normed = (scaled * gain_one[...]).astype(BF16)
        normed_one[rows, :] = normed
        bias = jnp.where(cell_mask((PART, SLOT), 0, off, length[0]) > 0.5, 0.0, -1e30)
        for h in range(3):
            q = dot(normed, w_qkv[:, h * SLOT : (h + 1) * SLOT]).astype(BF16).astype(F32)
            q_tm[h, rows, :] = jnp.where(lane == HEAD_DIM, 1.0, q * 0.125).astype(BF16)
            k = dot(normed, w_qkv[:, (3 + h) * SLOT : (4 + h) * SLOT])
            k_tm[h, rows, :] = jnp.where(lane == HEAD_DIM, bias, k).astype(BF16)
            v = dot(normed, w_qkv[:, (6 + h) * SLOT : (7 + h) * SLOT])
            v_tm[h, rows, :] = v.astype(BF16)
        return carry

    lax.fori_loop(0, 4, project, 0)
    gathers = []
    for h in range(3):
        v_cm[:, 0:ROWS] = v_tm[h].T

        def attend(c, carry):
            lanes = pl.ds(pl.multiple_of(c * CHUNK, CHUNK), CHUNK)
            s = dot(k_tm[h], q_tm[h, lanes, :], (1, 1))
            top = jnp.max(s, axis=0, keepdims=True)
            w = jnp.exp(s - top)
            total = jnp.sum(w, axis=0, keepdims=True)
            probs = (w * (1.0 / total)).astype(BF16)
            out = dot(v_cm[0:HEAD_DIM, 0:ROWS], probs).astype(BF16)
            lse[h : h + 1, lanes] = top + jnp.log(total)
            mixed[h * HEAD_DIM : (h + 1) * HEAD_DIM, lanes] = out
            own = pl.ds(pl.multiple_of(p.t * 192 + h * HEAD_DIM, 64), HEAD_DIM)
            mixed_all[own, lanes] = out
            return carry

        lax.fori_loop(0, LANES // CHUNK, attend, 0)
        place = lambda t, h=h: mixed_all.at[
            pl.ds(pl.multiple_of(t * 192 + h * HEAD_DIM, 64), HEAD_DIM), :
        ]
        g = Gather(links, p, place)
        g.start()
        gathers.append(g)
        if h == 0:
            g_out.forward()
            g_tap.forward()
        else:
            gathers[h - 1].forward()
    gathers[2].forward()
    for g in gathers:
        g.finish()
    g_out.finish()
    g_tap.finish()

    def finish(off, count):
        rows = pl.ds(off, count)
        branch = dot(mixed_all[:, rows], out_all[...], (0, 0))
        after = tok[rows, :].astype(F32) + branch
        hidden[rows, :] = after
        scaled, _ = norm(after)
        normed_two[rows, :] = (scaled * gain_two[...]).astype(BF16)

    lax.fori_loop(
        0, 4, lambda i, c: (finish(pl.multiple_of(i * CHUNK, CHUNK), CHUNK), c)[1], 0
    )
    finish(4 * CHUNK, ROWS - 4 * CHUNK)
    c_conv.wait_recv()
    c_conv.wait_send()


def attend_call(length, tokens, gain_one, gain_two, w_qkv, w_out, w_tap, w_conv):
    outs = [
        ((ROWS, D), F32),
        ((ROWS, D), BF16),
        ((3, LANES, SLOT), BF16),
        ((3, ROWS, SLOT), BF16),
        ((3, ROWS, SLOT), BF16),
        ((8, LANES), F32),
        ((192, LANES), BF16),
        ((ROWS, D), BF16),
        ((CH, D), BF16),
        ((2, CH, WIDE), BF16),
    ]
    scratch = [
        pltpu.VMEM((ROWS, D), BF16),
        pltpu.VMEM((D, LANES), BF16),
        pltpu.VMEM((D, D), BF16),
        pltpu.VMEM((SLOT, LANES), BF16),
        pltpu.SemaphoreType.DMA((1,)),
    ] + sems(16)
    return call(
        attend_kernel, outs, [smem, anywhere] + [vmem] * 6, scratch, 0, 8_000_000_000,
        (length, tokens, gain_one, gain_two, w_qkv, w_out, w_tap, w_conv),
    )


def mlp_kernel(
    length, normed_two, hidden, w_up, w_down, tap_all, conv_x,
    pre, act, out_own, field, conv_all,
    out_c, out_x, in_c, in_x, local, send, recv,
):
    p = Peers()
    links = Links(send, recv)
    p.greet(mate=True)
    half = lax.rem(p.dp, 2) * 2
    keep = pltpu.make_async_copy(conv_x, conv_all.at[pl.ds(half, 2)], local.at[0])
    keep.start()
    swap = links.copy(conv_x, conv_all.at[pl.ds(half, 2)], (p.mate, p.t))
    swap.start()

    def part(owner):
        rows = pl.ds(pl.multiple_of(owner * PART, 16), PART)
        value = dot(normed_two[rows, :], w_up[...])
        pre[rows, :] = value
        activation = gelu(value).astype(BF16)
        act[rows, :] = activation
        return dot(activation, w_down[...])

    total = Scatter(links, p, out_c, out_x, in_c, in_x).run(part)
    off = pl.multiple_of(p.t * PART, 16)
    rows = pl.ds(off, PART)
    mask = cell_mask((PART, D), 0, off, length[0])
    out = (mask * (hidden[rows, :] + total)).astype(BF16)
    out_own[...] = out
    field[rows, :] = dot(out, tap_all[...], (1, 1)).astype(BF16)
    g = Gather(links, p, lambda t: part_at(field, t))
    g.start()
    g.forward()
    g.finish()
    keep.wait()
    swap.wait_recv()
    swap.wait_send()


def mlp_call(length, normed_two, hidden, w_up, w_down, tap_all, conv_x):
    outs = [
        ((ROWS, D), F32),
        ((ROWS, D), BF16),
        ((PART, D), BF16),
        ((ROWS, CH), BF16),
        ((4, CH, WIDE), BF16),
    ]
    scratch = [
        pltpu.VMEM((2, PART, D), BF16),
        pltpu.VMEM((PART, D), BF16),
        pltpu.VMEM((2, PART, D), BF16),
        pltpu.VMEM((PART, D), BF16),
        pltpu.SemaphoreType.DMA((1,)),
    ] + sems(7)
    return call(
        mlp_kernel, outs, [smem] + [vmem] * 6, scratch, 1, 4_000_000_000,
        (length, normed_two, hidden, w_up, w_down, tap_all, conv_x),
    )


def conv_kernel(
    length, field, w_own, w_far, grad_own, out_own,
    result, tap_grad, grads, out_all,
    start_all, state, first, x_all, wide, flip, dcol, back, grad, grad_far, grad_near,
    back_out, back_in, send, recv,
):
    p = Peers()
    links = Links(send, recv)
    p.greet()
    weights = (w_own, w_far)
    block_of = (p.t, p.xp)
    at = lambda t: pl.ds(pl.multiple_of(t * BLOCK, BLOCK), BLOCK)

    near = out_all.at[pl.ds(pl.multiple_of(p.t * PART, 16), PART), :]
    near[...] = out_own[...]
    out_all[ROWS:, :] = jnp.zeros((LANES - ROWS, D), BF16)
    g_out = Gather(links, p, lambda t: part_at(out_all, t))
    grad_near[...] = grad_own[...].astype(BF16)
    c_grad = links.copy(grad_near, grad_far, (p.dp, p.xp))
    c_grad.start()
    g_out.start()

    def masks(count):
        _, col = grid_place((count, LANES), 1, 0)
        not_first = jnp.where(col > 0.5, 1.0, 0.0)
        not_last = jnp.where(col < GW - 1.5, 1.0, 0.0)
        return cell_mask((count, LANES), 1, 0, length[0]), not_first, not_last

    cells8, not_first8, not_last8 = masks(8)
    cells16, not_first16, not_last16 = masks(16)

    start_all[:, ROWS:] = jnp.zeros((CH, LANES - ROWS), F32)
    start_all[:, 0:ROWS] = field[...].astype(F32).T

    def open_rows(i, carry):
        rows = pl.ds(pl.multiple_of(i * 16, 16), 16)
        x_all[0, rows, :] = gelu(start_all[rows, :]).astype(BF16)
        return carry

    lax.fori_loop(0, CH // 16, open_rows, 0)
    for b in range(2):
        state[0, b] = start_all[at(block_of[b]), :]

    def convolve(index, b, use):
        flip[...] = weights[b][index].T

        def columns(c, carry):
            lanes = pl.ds(pl.multiple_of(c * CHUNK, CHUNK), CHUNK)
            wide[:, lanes] = dot(flip[...], x_all[index, :, lanes])
            return carry

        lax.fori_loop(0, LANES // CHUNK, columns, 0)

        def rows8(g, carry):
            total = jnp.zeros((8, LANES), F32)
            for q in range(3):
                tap = lambda r: wide[pl.ds(pl.multiple_of((r * 3 + q) * BLOCK + g * 8, 8), 8), :]
                three = (
                    tap(1)
                    + pltpu.roll(tap(0), GW, 1)
                    + pltpu.roll(tap(2), LANES - GW, 1)
                )
                if q == 0:
                    three = pltpu.roll(three, 1, 1) * not_first8
                if q == 2:
                    three = pltpu.roll(three, LANES - 1, 1) * not_last8
                total = total + three
            use(pl.ds(pl.multiple_of(g * 8, 8), 8), cells8 * total)
            return carry

        lax.fori_loop(0, BLOCK // 8, rows8, 0)

    def share(index):
        copies = [
            links.copy(x_all.at[index, at(t), :], x_all.at[index, at(t), :], (p.dp, p.sib))
            for t in block_of
        ]
        for c in copies:
            c.start()
        return copies

    def settle(copies):
        for c in copies:
            c.wait_recv()

    pending = []
    for unit in range(2):
        for b in range(2):
            def use_first(rows, value, b=b):
                first[unit, b, rows, :] = value

            convolve(2 * unit, b, use_first)

            def close(i, carry, b=b):
                rows = pl.ds(pl.multiple_of(i * 16, 16), 16)
                into = pl.ds(pl.multiple_of(block_of[b] * BLOCK + i * 16, 16), 16)
                x_all[2 * unit + 1, into, :] = gelu(first[unit, b, rows, :]).astype(BF16)
                return carry

            lax.fori_loop(0, BLOCK // 16, close, 0)
        copies = share(2 * unit + 1)
        pending += copies
        if unit == 0:
            g_out.forward()
        settle(copies)
        for b in range(2 - unit):
            def use_second(rows, value, b=b):
                if unit == 0:
                    state[1, b, rows, :] = state[0, b, rows, :] + value
                else:
                    result[rows, :] = state[1, b, rows, :] + value

            convolve(2 * unit + 1, b, use_second)
            if unit == 0:
                def close_two(i, carry, b=b):
                    rows = pl.ds(pl.multiple_of(i * 16, 16), 16)
                    into = pl.ds(pl.multiple_of(block_of[b] * BLOCK + i * 16, 16), 16)
                    x_all[2, into, :] = gelu(state[1, b, rows, :]).astype(BF16)
                    return carry

                lax.fori_loop(0, BLOCK // 16, close_two, 0)
        if unit == 0:
            copies = share(2)
            pending += copies
            settle(copies)

    c_grad.wait_recv()
    grad[0] = grad_own[...]
    grad[1] = grad_far[...].astype(F32)

    def spread(b, value_of):
        def rows16(i, carry):
            rows = pl.ds(pl.multiple_of(i * 16, 16), 16)
            value = value_of(rows).astype(BF16).astype(F32)
            for q in range(3):
                side = value
                if q == 0:
                    side = pltpu.roll(value, LANES - 1, 1) * not_last16
                if q == 2:
                    side = pltpu.roll(value, 1, 1) * not_first16
                for r in range(3):
                    moved = side
                    if r == 0:
                        moved = pltpu.roll(side, LANES - GW, 1)
                    if r == 2:
                        moved = pltpu.roll(side, GW, 1)
                    into = pl.ds(
                        pl.multiple_of((r * 3 + q) * BLOCK + i * 16, 16), 16
                    )
                    dcol[b, into, :] = moved.astype(BF16)
            return carry

        lax.fori_loop(0, BLOCK // 16, rows16, 0)

    def conv_back(index, turn):
        def columns(c, carry):
            lanes = pl.ds(pl.multiple_of(c * CHUNK, CHUNK), CHUNK)
            back[:, lanes] = dot(w_own[index], dcol[0, :, lanes]) + dot(
                w_far[index], dcol[1, :, lanes]
            )
            return carry

        lax.fori_loop(0, LANES // CHUNK, columns, 0)
        copies = []
        for b, t in enumerate((p.sib, p.diag)):
            back_out[turn, b] = back[at(t), :].astype(BF16)
            c = links.copy(back_out.at[turn, b], back_in.at[turn, b], (p.dp, p.sib))
            c.start()
            copies.append(c)
        grads[index] = dot(x_all[index], dcol[0], (1, 1))
        for c in copies:
            c.wait_recv()
        pending.extend(copies)

        def value(b, rows):
            far = pl.ds(
                pl.multiple_of(block_of[b] * BLOCK + rows.start, 16), 16
            )
            return back[far, :] + back_in[turn, b, rows, :].astype(F32)

        return value

    for turn, unit in enumerate((1, 0)):
        for b in range(2):
            spread(b, lambda rows, b=b: cells16 * grad[b, rows, :])
        d_mid = conv_back(2 * unit + 1, 2 * turn)
        for b in range(2):
            spread(
                b,
                lambda rows, b=b: cells16
                * d_mid(b, rows)
                * gelu_slope(first[unit, b, rows, :]),
            )
        d_in = conv_back(2 * unit, 2 * turn + 1)
        for b in range(2):
            def renew(i, carry, b=b):
                rows = pl.ds(pl.multiple_of(i * 16, 16), 16)
                fresh = grad[b, rows, :] + d_in(b, rows) * gelu_slope(state[unit, b, rows, :])
                grad[b, rows, :] = fresh
                if unit == 0:
                    into = pl.ds(pl.multiple_of(block_of[b] * BLOCK + i * 16, 16), 16)
                    _, _ = into, carry
                    inside = jnp.where(
                        lax.broadcasted_iota(jnp.int32, (16, LANES), 1) < SLOTS, fresh, 0.0
                    )
                    tap_grad[into, :] = inside.astype(BF16)
                return carry

            lax.fori_loop(0, BLOCK // 16, renew, 0)
    copies = [
        links.copy(tap_grad.at[at(t), :], tap_grad.at[at(t), :], (p.dp, p.sib))
        for t in block_of
    ]
    for c in copies:
        c.start()
    settle(copies)
    for c in pending + copies + [c_grad]:
        c.wait_send()
    g_out.finish()


def conv_call(length, field, w_own, w_far, grad_own, out_own):
    outs = [
        ((BLOCK, LANES), F32),
        ((CH, LANES), BF16),
        ((4, CH, WIDE), F32),
        ((LANES, D), BF16),
    ]
    scratch = [
        pltpu.VMEM((CH, LANES), F32),
        pltpu.VMEM((2, 2, BLOCK, LANES), F32),
        pltpu.VMEM((2, 2, BLOCK, LANES), F32),
        pltpu.VMEM((4, CH, LANES), BF16),
        pltpu.VMEM((WIDE, LANES), F32),
        pltpu.VMEM((WIDE, CH), BF16),
        pltpu.VMEM((2, WIDE, LANES), BF16),
        pltpu.VMEM((CH, LANES), F32),
        pltpu.VMEM((2, BLOCK, LANES), F32),
        pltpu.VMEM((BLOCK, LANES), BF16),
        pltpu.VMEM((BLOCK, LANES), BF16),
        pltpu.VMEM((4, 2, BLOCK, LANES), BF16),
        pltpu.VMEM((4, 2, BLOCK, LANES), BF16),
    ] + sems(20)
    return call(
        conv_kernel, outs, [smem] + [vmem] * 5, scratch, 2, 9_000_000_000,
        (length, field, w_own, w_far, grad_own, out_own),
    )


def mlp_back_kernel(
    length, tap_grad, tap_all, cot_hbm, pre, act, normed_two, w_up, w_down, hidden, gain_two,
    out_all,
    grad_hidden, branch, g_down, g_up, g_tap, g_gain,
    cot, tap_tm, d_mlp, d_pre, mine_block, out_c, out_x, in_c, in_x, local, send, recv,
):
    p = Peers()
    links = Links(send, recv)
    bring = pltpu.make_async_copy(cot_hbm, cot.at[pl.ds(0, SLOTS), :], local.at[0])
    bring.start()
    cot[SLOTS:, :] = jnp.zeros((ROWS - SLOTS, D), BF16)
    p.greet()
    tap_tm[...] = tap_grad[...].T
    bring.wait()

    def part(owner):
        off = pl.multiple_of(owner * PART, 16)
        rows = pl.ds(off, PART)
        block = cell_mask((PART, D), 0, off, length[0]) * (
            cot[rows, :].astype(F32) + dot(tap_tm[rows, :], tap_all[...])
        )
        mine_block[...] = block
        low = block.astype(BF16)
        d_mlp[rows, :] = low
        slope = (dot(low, w_down[...], (1, 1)) * gelu_slope(pre[rows, :])).astype(BF16)
        d_pre[rows, :] = slope
        return dot(slope, w_up[...], (1, 1))

    total = Scatter(links, p, out_c, out_x, in_c, in_x).run(part)
    rows = pl.ds(pl.multiple_of(p.t * PART, 16), PART)
    scaled, inverse = norm(hidden[rows, :])
    inner, gain_part = norm_back(total, scaled, inverse, gain_two[...])
    after = mine_block[...] + inner
    grad_hidden[...] = after
    g_gain[...] = gain_part
    branch[rows, :] = after.astype(BF16)
    g = Gather(links, p, lambda t: part_at(branch, t))
    g.start()
    g_down[...] = dot(act[...], d_mlp[...], (0, 0))
    g.forward()
    g_up[...] = dot(normed_two[...], d_pre[...], (0, 0))
    g_tap[...] = dot(
        tap_grad[pl.ds(pl.multiple_of(p.t * BLOCK, BLOCK), BLOCK), :], out_all[...]
    )
    g.finish()


def mlp_back_call(*args):
    outs = [
        ((PART, D), F32),
        ((ROWS, D), BF16),
        ((D, D), F32),
        ((D, D), F32),
        ((BLOCK, D), F32),
        ((1, D), F32),
    ]
    scratch = [
        pltpu.VMEM((ROWS, D), BF16),
        pltpu.VMEM((LANES, CH), BF16),
        pltpu.VMEM((ROWS, D), BF16),
        pltpu.VMEM((ROWS, D), BF16),
        pltpu.VMEM((PART, D), F32),
        pltpu.VMEM((2, PART, D), BF16),
        pltpu.VMEM((PART, D), BF16),
        pltpu.VMEM((2, PART, D), BF16),
        pltpu.VMEM((PART, D), BF16),
        pltpu.SemaphoreType.DMA((1,)),
    ] + sems(6)
    return call(
        mlp_back_kernel, outs, [smem, vmem, vmem, anywhere] + [vmem] * 8, scratch, 3,
        9_000_000_000, args,
    )


def attend_back_kernel(
    length, branch, grad_hidden, w_out, mixed, q_tm, k_tm, v_tm, lse, normed_one, w_qkv, tok_hbm,
    gain_one,
    grad_tok, g_qkv, g_out, g_gain,
    tok, d_mix, d_mix_cm, k_cm, acc_k, acc_v, d_all, out_c, out_x, in_c, in_x, local, send, recv,
):
    p = Peers()
    links = Links(send, recv)
    bring = pltpu.make_async_copy(tok_hbm, tok.at[pl.ds(0, SLOTS), :], local.at[0])
    bring.start()
    tok[SLOTS:, :] = jnp.zeros((ROWS - SLOTS, D), BF16)
    p.greet()
    d_mix[:, ROWS:, :] = jnp.zeros((3, LANES - ROWS, SLOT), BF16)
    d_mix_cm[:, ROWS:] = jnp.zeros((192, LANES - ROWS), F32)
    d_all[...] = jnp.zeros(d_all.shape, BF16)
    value = dot(w_out[...], branch[...], (1, 1))
    d_mix_cm[:, 0:ROWS] = value.astype(BF16).astype(F32)
    for h in range(3):
        mix = dot(branch[...], w_out[h * HEAD_DIM : (h + 1) * HEAD_DIM, :], (1, 1))
        d_mix[h, 0:ROWS, 0:HEAD_DIM] = mix.astype(BF16)
        d_mix[h, 0:ROWS, HEAD_DIM:] = jnp.zeros((ROWS, SLOT - HEAD_DIM), BF16)
    g_out[...] = dot(mixed[:, 0:ROWS], branch[...])
    for h in range(3):
        k_cm[:, 0:ROWS] = k_tm[h].T
        acc_k[...] = jnp.zeros(acc_k.shape, F32)
        acc_v[...] = jnp.zeros(acc_v.shape, F32)

        def attend(c, carry):
            lanes = pl.ds(pl.multiple_of(c * CHUNK, CHUNK), CHUNK)
            heads = slice(h * HEAD_DIM, (h + 1) * HEAD_DIM)
            q = q_tm[h, lanes, :]
            dm = d_mix[h, lanes, :]
            inner = jnp.sum(
                d_mix_cm[heads, lanes] * mixed[heads, lanes].astype(F32), axis=0, keepdims=True
            )
            probs = jnp.exp(dot(k_tm[h], q, (1, 1)) - lse[h : h + 1, lanes])
            d_probs = dot(v_tm[h], dm, (1, 1))
            d_raw = (probs * (d_probs - inner)).astype(BF16)
            acc_v[...] += dot(probs.astype(BF16), dm)
            acc_k[...] += dot(d_raw, q)
            d_q = dot(k_cm[0:HEAD_DIM, 0:ROWS], d_raw) * 0.125
            d_all[lanes, h * SLOT : h * SLOT + HEAD_DIM] = d_q.T.astype(BF16)
            return carry

        lax.fori_loop(0, LANES // CHUNK, attend, 0)
        d_all[0:ROWS, (3 + h) * SLOT : (4 + h) * SLOT] = acc_k[...].astype(BF16)
        d_all[0:ROWS, (6 + h) * SLOT : (7 + h) * SLOT] = acc_v[...].astype(BF16)

    def part(owner):
        rows = pl.ds(pl.multiple_of(owner * PART, 16), PART)
        return dot(d_all[rows, :], w_qkv[...], (1, 1))

    total = Scatter(links, p, out_c, out_x, in_c, in_x).run(part)
    bring.wait()
    rows = pl.ds(pl.multiple_of(p.t * PART, 16), PART)
    scaled, inverse = norm(tok[rows, :].astype(F32))
    inner, gain_part = norm_back(total, scaled, inverse, gain_one[...])
    g_gain[...] = gain_part
    grad_tok[rows, :] = (grad_hidden[...] + inner).astype(BF16)
    g = Gather(links, p, lambda t: part_at(grad_tok, t))
    g.start()
    g_qkv[...] = dot(normed_one[...], d_all[0:ROWS, :], (0, 0))
    g.forward()
    g.finish()


def attend_back_call(*args):
    outs = [
        ((ROWS, D), BF16),
        ((D, 9 * SLOT), F32),
        ((192, D), F32),
        ((1, D), F32),
    ]
    scratch = [
        pltpu.VMEM((ROWS, D), BF16),
        pltpu.VMEM((3, LANES, SLOT), BF16),
        pltpu.VMEM((192, LANES), F32),
        pltpu.VMEM((SLOT, LANES), BF16),
        pltpu.VMEM((ROWS, SLOT), F32),
        pltpu.VMEM((ROWS, SLOT), F32),
        pltpu.VMEM((LANES, 9 * SLOT), BF16),
        pltpu.VMEM((2, PART, D), BF16),
        pltpu.VMEM((PART, D), BF16),
        pltpu.VMEM((2, PART, D), BF16),
        pltpu.VMEM((PART, D), BF16),
        pltpu.SemaphoreType.DMA((1,)),
    ] + sems(6)
    return call(
        attend_back_kernel, outs, [smem] + [vmem] * 10 + [anywhere, vmem], scratch, 4,
        12_000_000_000, args,
    )


def lift_kernel(field, joined, grid, tall):
    grid[...] = field[...].T

    def row_pair(a, carry):
        def row(i):
            return grid[pl.ds(pl.multiple_of(i * GW, 8), GW), :]

        here = row(a)
        up = row(jnp.maximum(a - 1, 0))
        down = row(jnp.minimum(a + 1, GH - 1))
        for side, other in enumerate((up, down)):
            line = 0.75 * here + 0.25 * other
            left = jnp.concatenate([line[0:1], line[:-1]], axis=0)
            right = jnp.concatenate([line[1:], line[-1:]], axis=0)
            tall[pl.ds(0, GW, 2), :] = 0.75 * line + 0.25 * left
            tall[pl.ds(1, GW, 2), :] = 0.75 * line + 0.25 * right
            joined[2 * a + side] = tall[...].astype(BF16)
        return carry

    lax.fori_loop(0, GH, row_pair, 0)


def lift_call(field):
    return call(
        lift_kernel, [((2 * GH, 2 * GW, BLOCK), BF16)], [vmem],
        [pltpu.VMEM((LANES, BLOCK), F32), pltpu.VMEM((2 * GW, BLOCK), F32)],
        None, 100_000_000, (field,),
    )[0]


def lower_kernel(cot, grad, grid, tall):
    grid[SLOTS:, :] = jnp.zeros((LANES - SLOTS, SLOT), F32)

    def row(a, carry):
        def line(i):
            return cot[i].astype(F32)

        first, last = a == 0, a == GH - 1
        mid = 0.75 * (line(2 * a) + line(2 * a + 1))
        low = jnp.where(first, 0.25 * line(0), 0.25 * line(jnp.maximum(2 * a - 1, 0)))
        high = jnp.where(
            last, 0.25 * line(2 * GH - 1), 0.25 * line(jnp.minimum(2 * a + 2, 2 * GH - 1))
        )
        tall[:, 0:BLOCK] = mid + low + high
        even = tall[pl.ds(0, GW, 2), :]
        odd = tall[pl.ds(1, GW, 2), :]
        before = jnp.concatenate([even[0:1], odd[:-1]], axis=0)
        after = jnp.concatenate([even[1:], odd[-1:]], axis=0)
        grid[pl.ds(pl.multiple_of(a * GW, 8), GW), :] = 0.75 * (even + odd) + 0.25 * (
            before + after
        )
        return carry

    tall[...] = jnp.zeros(tall.shape, F32)
    lax.fori_loop(0, GH, row, 0)
    grad[...] = grid[...].T[0:BLOCK, :]


def lower_call(cot):
    return call(
        lower_kernel, [((BLOCK, LANES), F32)], [vmem],
        [pltpu.VMEM((LANES, SLOT), F32), pltpu.VMEM((2 * GW, SLOT), F32)],
        None, 100_000_000, (cot,),
    )[0]


def per_device(
    tokens, lengths, gain_one, gain_two, w_qkv, w_out, w_up, w_down, w_tap, w_conv,
    cot_tokens, cot_joined,
):
    gain_one = gain_one.reshape(1, D)
    gain_two = gain_two.reshape(1, D)
    heads = w_qkv.shape[2] // HEAD_DIM
    slots = jnp.pad(
        w_qkv.transpose(1, 0, 2).reshape(D, 3 * heads, HEAD_DIM),
        ((0, 0), (0, 0), (0, SLOT - HEAD_DIM)),
    ).reshape(D, 3 * heads * SLOT)
    tap_t = w_tap.T
    conv_w = w_conv.transpose(0, 3, 1, 2, 4).reshape(4, CH, WIDE)
    (
        hidden, normed_two, q_tm, k_tm, v_tm, lse, mixed, normed_one, tap_all, conv_x,
    ) = attend_call(lengths, tokens, gain_one, gain_two, slots, w_out, tap_t, conv_w)
    grad_own = lower_call(cot_joined[0])
    pre, act, out_own, field, conv_far = mlp_call(
        lengths, normed_two, hidden, w_up, w_down, tap_all, conv_x
    )
    result, tap_grad, g_conv, out_all = conv_call(
        lengths, field, conv_w, conv_far, grad_own, out_own
    )
    joined = lift_call(result)[None]
    grad_hidden, branch, g_down, g_up, g_tap, g_gain_two = mlp_back_call(
        lengths, tap_grad, tap_all, cot_tokens, pre, act, normed_two, w_up, w_down, hidden,
        gain_two, out_all,
    )
    grad_tok, g_qkv, g_out, g_gain_one = attend_back_call(
        lengths, branch, grad_hidden, w_out, mixed, q_tm, k_tm, v_tm, lse, normed_one, slots,
        tokens, gain_one,
    )

    def total(v):
        return lax.psum(v.astype(BF16), "dp").astype(F32)

    g_conv = total(g_conv).reshape(4, CH, 3, 3, BLOCK).transpose(0, 2, 3, 1, 4)
    g_tap = total(g_tap).T
    g_down = total(g_down)
    g_up = total(g_up)
    g_out = total(g_out)
    g_qkv = g_qkv.reshape(D, 3, heads, SLOT)[..., :HEAD_DIM].reshape(D, 3, heads * HEAD_DIM)
    g_qkv = total(g_qkv.transpose(1, 0, 2))
    gains = lax.psum(jnp.concatenate([g_gain_one, g_gain_two]), ("dp", "tensor"))
    return (
        out_all[:SLOTS], joined, grad_tok[:SLOTS], g_qkv, g_out, g_up, g_down, g_tap, g_conv,
        gains[0], gains[1],
    )


def solution(mesh):
    placed = (
        P("dp", None),
        P("dp"),
        P(),
        P(),
        P(None, None, "tensor"),
        P("tensor", None),
        P(None, "tensor"),
        P("tensor", None),
        P(None, "tensor"),
        P(None, None, None, None, "tensor"),
        P("dp", None),
        P("dp", None, None, "tensor"),
    )
    return jax.shard_map(
        per_device,
        mesh=mesh,
        in_specs=placed,
        out_specs=(
            P("dp", None),
            P("dp", None, None, "tensor"),
            P("dp", None),
            P(None, None, "tensor"),
            P("tensor", None),
            P(None, "tensor"),
            P("tensor", None),
            P(None, "tensor"),
            P(None, None, None, None, "tensor"),
            P(),
            P(),
        ),
        check_vma=False,
    )
```

```python
import functools

import jax
import jax.numpy as jnp
from jax import lax
from jax.experimental import pallas as pl
from jax.experimental.pallas import tpu as pltpu
from jax.sharding import PartitionSpec as P

HEAD_DIM = 64
GH = 30
GW = 40
SH = 24
SW = 24
SLOTS = GH * GW
D = 768
CH = 256
BLOCK = 64
TAPS = 9
WIDE = TAPS * BLOCK
PART = 304
ROWS = 4 * PART
LANES = 1280
CHUNK = 256
SLOT = 128
F32 = jnp.float32
BF16 = jnp.bfloat16
MESH = pl.DeviceIdType.MESH
VMEM_LIMIT = 56 * 2**20

vmem = pl.BlockSpec(memory_space=pltpu.VMEM)
smem = pl.BlockSpec(memory_space=pltpu.SMEM)
anywhere = pl.BlockSpec(memory_space=pl.ANY)


def dot(a, b, dims=(1, 0)):
    return lax.dot_general(
        a, b, (((dims[0],), (dims[1],)), ((), ())), preferred_element_type=F32
    )


def gelu(v):
    return 0.5 * v * (1.0 + lax.erf(v * 0.7071067811865476))


def gelu_and_slope(v):
    share = 0.5 * (1.0 + lax.erf(v * 0.7071067811865476))
    return v * share, share + v * jnp.exp(-0.5 * v * v) * 0.3989422804014327


def norm(v):
    centred = v - jnp.mean(v, axis=-1, keepdims=True)
    spread = jnp.mean(centred * centred, axis=-1, keepdims=True)
    inverse = lax.rsqrt(spread + 1e-06)
    return centred * inverse, inverse


def norm_back(incoming, scaled, inverse, gain):
    weighted = incoming * gain
    inner = (
        weighted
        - jnp.mean(weighted, axis=-1, keepdims=True)
        - scaled * jnp.mean(weighted * scaled, axis=-1, keepdims=True)
    )
    return inverse * inner, jnp.sum(incoming * scaled, axis=0, keepdims=True)


def grid_place(shape, axis, offset):
    index = (lax.broadcasted_iota(jnp.int32, shape, axis) + offset).astype(F32)
    row = jnp.floor((index + 0.5) * (1.0 / GW))
    return row, index - GW * row


def cell_mask(shape, axis, offset, length):
    row, col = grid_place(shape, axis, offset)
    large = length == SLOTS
    height = jnp.where(large, float(GH), float(SH))
    breadth = jnp.where(large, float(GW), float(SW))
    return jnp.where((row < height) & (col < breadth), 1.0, 0.0)


class Peers:
    def __init__(self):
        self.dp = lax.axis_index("dp")
        self.n = lax.axis_size("dp")
        self.t = lax.axis_index("tensor")
        self.sib = self.t + 1 - 2 * lax.rem(self.t, 2)
        self.xp = lax.rem(self.t + 2, 4)
        self.diag = lax.rem(self.sib + 2, 4)

    def bit(self, at):
        return lax.rem(self.dp // (1 << at), 2)

    def mate(self, at):
        return self.dp + (1 - 2 * self.bit(at)) * (1 << at)

    def bits(self):
        return self.n.bit_length() - 1

    def greet(self, bits=0):
        barrier = pltpu.get_barrier_semaphore()
        others = [(self.dp, self.sib), (self.dp, self.xp)]
        others += [(self.mate(at), self.t) for at in range(bits)]
        for other in others:
            pl.semaphore_signal(barrier, inc=1, device_id=other, device_id_type=MESH)
        pl.semaphore_wait(barrier, len(others))


class Links:
    def __init__(self, send, recv):
        self.send, self.recv, self.used = send, recv, 0

    def copy(self, src, dst, device):
        at = self.used
        self.used += 1
        return pltpu.make_async_remote_copy(
            src_ref=src,
            dst_ref=dst,
            send_sem=self.send.at[at],
            recv_sem=self.recv.at[at],
            device_id=device,
            device_id_type=MESH,
        )


class Gather:
    def __init__(self, links, peers, place):
        p = peers
        self.x = links.copy(place(p.t), place(p.t), (p.dp, p.xp))
        self.c = links.copy(place(p.t), place(p.t), (p.dp, p.sib))
        self.f = links.copy(place(p.xp), place(p.xp), (p.dp, p.sib))

    def start(self):
        self.x.start()
        self.c.start()

    def forward(self):
        self.x.wait_recv()
        self.f.start()

    def finish(self):
        self.c.wait_recv()
        self.f.wait_recv()
        self.x.wait_send()
        self.c.wait_send()
        self.f.wait_send()


PIECES = ((0, 160), (160, PART - 160))


class Scatter:
    def __init__(self, links, peers, out_c, out_x, in_c, in_x, mine):
        p = peers
        self.p, self.out_c, self.out_x, self.in_c, self.in_x = p, out_c, out_x, in_c, in_x
        self.mine = mine
        self.c = [links.copy(out_c.at[i], in_c.at[i], (p.dp, p.sib)) for i in range(2)]
        self.x = [
            links.copy(out_x.at[pl.ds(*piece), :], in_x.at[pl.ds(*piece), :], (p.dp, p.xp))
            for piece in PIECES
        ]

    def far(self, part):
        p = self.p
        self.out_c[0] = part(p.diag).astype(BF16)
        self.c[0].start()
        self.mine[...] = part(p.xp)
        self.c[0].wait_recv()
        for copy, piece in zip(self.x, PIECES):
            rows = pl.ds(*piece)
            self.out_x[rows, :] = (self.mine[rows, :] + self.in_c[0, rows, :].astype(F32)).astype(
                BF16
            )
            copy.start()

    def near(self, part):
        p = self.p
        self.out_c[1] = part(p.sib).astype(BF16)
        self.c[1].start()
        self.mine[...] = part(p.t)
        self.c[1].wait_recv()
        self.mine[...] += self.in_c[1].astype(F32)

    def piece(self, at):
        rows = pl.ds(*PIECES[at])
        self.x[at].wait_recv()
        return self.mine[rows, :] + self.in_x[rows, :].astype(F32)

    def finish(self):
        for copy in self.c + self.x:
            copy.wait_send()


class Halver:
    def __init__(self, links, peers, source, total, result, arrive, order=(0, 1, 2), after=0):
        p = self.p = peers
        self.links, self.source, self.total, self.result = links, source, total, result
        self.arrive, self.after = arrive, after
        self.rows = source.shape[0]
        base, size = 0, self.rows
        self.keep, self.give, self.to = [], [], []
        self.base = [base]
        for at in order:
            size //= 2
            mine = p.bit(at)
            self.give.append(pl.ds(pl.multiple_of(base + (1 - mine) * size, 16), size))
            base = base + mine * size
            self.base.append(base)
            self.keep.append(pl.ds(pl.multiple_of(base, 16), size))
            self.to.append((p.mate(at), p.t))
        self.sent, self.rs, self.ag = [], {}, {}
        self.slot = [0, self.rows // 2, 3 * self.rows // 4]

    def s(self, k):
        src = self.source if k == self.after else self.total
        land = pl.ds(self.slot[k], self.rows >> (k + 1))
        copy = self.links.copy(src.at[self.give[k], :], self.arrive.at[land, :], self.to[k])
        copy.start()
        self.rs[k] = (copy, src, land)
        self.sent.append(copy)

    def a(self, k):
        copy, src, land = self.rs[k]
        copy.wait_recv()
        keep = self.keep[k]
        self.total[keep, :] = (
            src[keep, :].astype(F32) + self.arrive[land, :].astype(F32)
        ).astype(BF16)
        if k == 2:
            size = self.rows >> 3
            for extra in range(3, self.p.bits()):
                start = 7 * size + (extra - 3) * size
                land = pl.ds(start, size)
                copy = self.links.copy(
                    self.total.at[keep, :], self.arrive.at[land, :], (self.p.mate(extra), self.p.t)
                )
                copy.start()
                copy.wait_recv()
                copy.wait_send()
                self.total[keep, :] = (
                    self.total[keep, :].astype(F32) + self.arrive[land, :].astype(F32)
                ).astype(BF16)

    def g(self, k):
        region = self.keep[k]
        if k == 2:
            src = self.source if self.after == 3 else self.total
            self.result[region, :] = src[region, :]
        copy = self.links.copy(self.result.at[region, :], self.result.at[region, :], self.to[k])
        copy.start()
        self.ag[k] = copy
        self.sent.append(copy)

    def w(self, k):
        self.ag[k].wait_recv()

    def finish(self):
        for copy in self.sent:
            copy.wait_send()

    def step(self, at):
        if at == 0:
            self.s(0)
        elif at < 3:
            if self.after < at:
                self.a(at - 1)
            self.s(at)
        elif at == 3:
            if self.after < 3:
                self.a(2)
            self.g(2)
        else:
            self.w(6 - at)
            if at < 6:
                self.g(5 - at)


def landing(rows, columns, bits):
    return pltpu.VMEM((rows + max(bits - 4, 0) * (rows // 8), columns), BF16)


class Doubler:
    def __init__(self, links, peers, outgoing, incoming):
        p = peers
        self.links, self.outgoing, self.incoming = links, outgoing, incoming
        self.to = [(p.dp, p.sib), (p.dp, p.xp)] + [(p.mate(at), p.t) for at in range(p.bits())]
        self.copies = []

    def start(self, value):
        self.value = value
        self.send()

    def send(self):
        at = len(self.copies)
        if at < len(self.to):
            self.outgoing[at] = self.value
            copy = self.links.copy(self.outgoing.at[at], self.incoming.at[at], self.to[at])
            copy.start()
            self.copies.append(copy)

    def step(self):
        at = len(self.copies) - 1
        self.copies[at].wait_recv()
        self.value = self.value + self.incoming[at]
        self.send()

    def finish(self):
        while len(self.copies) < len(self.to):
            self.step()
        self.copies[-1].wait_recv()
        self.value = self.value + self.incoming[len(self.to) - 1]
        for copy in self.copies:
            copy.wait_send()
        return self.value


def sems(count):
    return [pltpu.SemaphoreType.DMA((count,)), pltpu.SemaphoreType.DMA((count,))]


def part_at(ref, owner):
    return ref.at[pl.ds(pl.multiple_of(owner * PART, 16), PART), :]


def piece_at(ref, owner, piece):
    return ref.at[pl.ds(pl.multiple_of(owner * PART + piece[0], 16), piece[1]), :]


def upsample_table(count):
    shape = (2 * count, count)
    target = lax.broadcasted_iota(jnp.int32, shape, 0)
    source = lax.broadcasted_iota(jnp.int32, shape, 1)
    nearest = lax.shift_right_logical(target, 1)
    odd = target - 2 * nearest
    further = jnp.clip(nearest + 2 * odd - 1, 0, count - 1)
    return jnp.where(source == nearest, 0.75, 0.0) + jnp.where(source == further, 0.25, 0.0)


def split_dot(a, table):
    high = a.astype(BF16)
    low = (a - high.astype(F32)).astype(BF16)
    return dot(high, table) + dot(low, table)


def call(kernel, outs, ins, scratch, collective, flops, args):
    return pl.pallas_call(
        kernel,
        out_shape=[jax.ShapeDtypeStruct(*o) for o in outs],
        in_specs=ins,
        out_specs=[vmem] * len(outs),
        scratch_shapes=scratch,
        cost_estimate=pl.CostEstimate(
            flops=flops, bytes_accessed=20_000_000, transcendentals=0
        ),
        compiler_params=pltpu.CompilerParams(
            collective_id=collective,
            has_side_effects=True,
            vmem_limit_bytes=VMEM_LIMIT,
        )
        if collective is not None
        else pltpu.CompilerParams(vmem_limit_bytes=VMEM_LIMIT),
    )(*args)


def attend_kernel(
    length, tok_hbm, gain_one, gain_two, w_qkv, w_out, w_tap, w_conv,
    hidden_own, normed_two, q_cm, k_tm, v_tm, k_cm, lse, mixed, normed_one, tap_all, conv_x,
    tok, hidden, mixed_all, out_all, v_cm, local, send, recv,
):
    p = Peers()
    links = Links(send, recv)
    bring = pltpu.make_async_copy(tok_hbm, tok.at[pl.ds(0, SLOTS), :], local.at[0])
    bring.start()
    tok[SLOTS:, :] = jnp.zeros((LANES - SLOTS, D), BF16)
    place_out = lambda t: out_all.at[pl.ds(pl.multiple_of(t * 192, 64), 192), :]
    place_tap = lambda t: tap_all.at[pl.ds(pl.multiple_of(t * 64, 64), 64), :]
    place_out(p.t)[...] = w_out[...]
    place_tap(p.t)[...] = w_tap[...]
    p.greet()
    g_out = Gather(links, p, place_out)
    g_tap = Gather(links, p, place_tap)
    quarter = lax.rem(p.dp, 4)
    c_conv = links.copy(w_conv.at[quarter], conv_x, (p.dp, p.xp))
    g_out.start()
    g_tap.start()
    bring.wait()
    gain = gain_one[...].reshape(1, D)
    lane = lax.broadcasted_iota(jnp.int32, (CHUNK, SLOT), 1)
    one_row = jnp.where(
        lax.broadcasted_iota(jnp.int32, (HEAD_DIM, CHUNK), 0) == 0, 1.0, 0.0
    ).astype(BF16)

    def project(i, carry):
        off = pl.multiple_of(i * CHUNK, CHUNK)
        rows = pl.ds(off, CHUNK)
        scaled, _ = norm(tok[rows, :].astype(F32))
        normed = (scaled * gain).astype(BF16)
        normed_one[rows, :] = normed
        bias = jnp.where(cell_mask((CHUNK, SLOT), 0, off, length[0]) > 0.5, 0.0, -1e30)
        bias = jnp.where(lane == HEAD_DIM, bias, 0.0).astype(BF16)
        qkv = dot(w_qkv[...], normed, (1, 1)).astype(BF16)
        for h in range(3):
            near = slice(h * HEAD_DIM, (h + 1) * HEAD_DIM)
            q_cm[h, 0:HEAD_DIM, rows] = (qkv[near].astype(F32) * 0.125).astype(BF16)
            q_cm[h, HEAD_DIM:, rows] = one_row
            k = qkv[192 + h * HEAD_DIM : 192 + (h + 1) * HEAD_DIM]
            k_cm[near, rows] = k
            k_tm[h, rows, :] = bias
            k_tm[h, rows, 0:HEAD_DIM] = k.T
            v = qkv[384 + h * HEAD_DIM : 384 + (h + 1) * HEAD_DIM]
            v_cm[near, rows] = v
            v_tm[h, rows, :] = v.T
        return carry

    lax.fori_loop(0, LANES // CHUNK, project, 0)
    gathers = []
    for h in range(3):
        heads = slice(h * HEAD_DIM, (h + 1) * HEAD_DIM)

        def attend(c, carry):
            lanes = pl.ds(pl.multiple_of(c * CHUNK, CHUNK), CHUNK)
            s = dot(k_tm[h, 0:ROWS, :], q_cm[h, :, lanes])
            top = jnp.max(s, axis=0, keepdims=True)
            w = jnp.exp(s - top)
            total = jnp.sum(w, axis=0, keepdims=True)
            probs = (w * (1.0 / total)).astype(BF16)
            out = dot(v_cm[heads, 0:ROWS], probs).astype(BF16)
            lse[h : h + 1, lanes] = top + jnp.log(total)
            mixed[heads, lanes] = out
            own = pl.ds(pl.multiple_of(p.t * 192 + h * HEAD_DIM, 64), HEAD_DIM)
            mixed_all[own, lanes] = out
            return carry

        lax.fori_loop(0, LANES // CHUNK, attend, 0)
        place = lambda t, h=h: mixed_all.at[
            pl.ds(pl.multiple_of(t * 192 + h * HEAD_DIM, 64), HEAD_DIM), :
        ]
        g = Gather(links, p, place)
        g.start()
        gathers.append(g)
        if h == 0:
            g_out.forward()
            g_tap.forward()
        else:
            gathers[h - 1].forward()
    c_conv.start()
    gathers[2].forward()
    for g in gathers:
        g.finish()
    g_out.finish()
    g_tap.finish()
    gain_after = gain_two[...].reshape(1, D)

    def finish(i, carry):
        rows = pl.ds(pl.multiple_of(i * CHUNK, CHUNK), CHUNK)
        branch = dot(mixed_all[:, rows], out_all[...], (0, 0))
        after = tok[rows, :].astype(F32) + branch
        hidden[rows, :] = after
        scaled, _ = norm(after)
        normed_two[rows, :] = (scaled * gain_after).astype(BF16)
        return carry

    lax.fori_loop(0, LANES // CHUNK, finish, 0)
    hidden_own[...] = hidden[pl.ds(pl.multiple_of(p.t * PART, 16), PART), :]
    c_conv.wait_recv()
    c_conv.wait_send()


def attend_call(*args):
    outs = [
        ((PART, D), F32),
        ((LANES, D), BF16),
        ((3, SLOT, LANES), BF16),
        ((3, LANES, SLOT), BF16),
        ((3, LANES, HEAD_DIM), BF16),
        ((192, LANES), BF16),
        ((8, LANES), F32),
        ((192, LANES), BF16),
        ((LANES, D), BF16),
        ((CH, D), BF16),
        ((WIDE, CH), BF16),
    ]
    scratch = [
        pltpu.VMEM((LANES, D), BF16),
        pltpu.VMEM((LANES, D), F32),
        pltpu.VMEM((D, LANES), BF16),
        pltpu.VMEM((D, D), BF16),
        pltpu.VMEM((192, LANES), BF16),
        pltpu.SemaphoreType.DMA((1,)),
    ] + sems(16)
    return call(
        attend_kernel, outs, [smem, anywhere] + [vmem] * 6, scratch, 0, 8_000_000_000, args
    )


def lower(cot, grad, tall, table):
    grad[:, SLOTS:] = jnp.zeros((BLOCK, LANES - SLOTS), F32)
    for a in range(GH):
        mid = 0.75 * (cot[2 * a].astype(F32) + cot[2 * a + 1].astype(F32))
        before = cot[max(2 * a - 1, 0)].astype(F32)
        after = cot[min(2 * a + 2, 2 * GH - 1)].astype(F32)
        tall[a * BLOCK : (a + 1) * BLOCK, :] = mid + 0.25 * (before + after)
    for a in range(GH):
        grad[:, a * GW : (a + 1) * GW] = split_dot(tall[a * BLOCK : (a + 1) * BLOCK, :], table)


def mlp_kernel(
    length, normed_two, hidden_own, w_up, w_down, tap_all, conv_x, cot,
    slope, act, out_own, field, conv_all, grad_own,
    out_c, out_x, in_c, in_x, mine, tall, local, send, recv,
):
    p = Peers()
    links = Links(send, recv)
    p.greet(2)
    quarter = lax.rem(p.dp, 4)
    pair = quarter - lax.rem(quarter, 2)
    keep = pltpu.make_async_copy(conv_x, conv_all.at[quarter], local.at[0])
    keep.start()
    swap = links.copy(conv_x, conv_all.at[quarter], (p.mate(0), p.t))
    swap.start()

    def part(owner):
        rows = pl.ds(pl.multiple_of(owner * PART, 16), PART)
        activation, steep = gelu_and_slope(dot(normed_two[rows, :], w_up[...]))
        activation = activation.astype(BF16)
        slope[rows, :] = steep.astype(BF16)
        act[rows, :] = activation
        return dot(activation, w_down[...])

    sums = Scatter(links, p, out_c, out_x, in_c, in_x, mine)
    sums.far(part)
    keep.wait()
    swap.wait_recv()
    pairs = conv_all.at[pl.ds(pair, 2)]
    trade = links.copy(pairs, pairs, (p.mate(1), p.t))
    trade.start()
    sums.near(part)
    lower(cot, grad_own, tall, upsample_table(GW).astype(BF16))
    gathers = []
    for at, piece in enumerate(PIECES):
        total = sums.piece(at)
        off = pl.multiple_of(p.t * PART + piece[0], 16)
        mask = cell_mask((piece[1], D), 0, off, length[0])
        out = (mask * (hidden_own[pl.ds(*piece), :] + total)).astype(BF16)
        out_own[pl.ds(*piece), :] = out
        field[pl.ds(off, piece[1]), :] = dot(out, tap_all[...], (1, 1)).astype(BF16)
        g = Gather(links, p, lambda t: piece_at(field, t, piece))
        g.start()
        gathers.append(g)
    for g in gathers:
        g.forward()
    for g in gathers:
        g.finish()
    sums.finish()
    swap.wait_send()
    trade.wait_recv()
    trade.wait_send()


def mlp_call(*args):
    outs = [
        ((ROWS, D), BF16),
        ((ROWS, D), BF16),
        ((PART, D), BF16),
        ((ROWS, CH), BF16),
        ((4, WIDE, CH), BF16),
        ((BLOCK, LANES), F32),
    ]
    scratch = scatter_scratch() + [
        pltpu.VMEM((GH * BLOCK, 2 * GW), F32),
        pltpu.SemaphoreType.DMA((1,)),
    ] + sems(12)
    return call(mlp_kernel, outs, [smem] + [vmem] * 7, scratch, 1, 4_000_000_000, args)


def scatter_scratch():
    return [
        pltpu.VMEM((2, PART, D), BF16),
        pltpu.VMEM((PART, D), BF16),
        pltpu.VMEM((2, PART, D), BF16),
        pltpu.VMEM((PART, D), BF16),
        pltpu.VMEM((PART, D), F32),
    ]


def conv_kernel(
    length, field, w_own, w_far, grad_own, out_own,
    result, tap_grad, g_conv, t_conv, out_all,
    start_all, state, steep_first, steep_state, x_all, wide, flip, dcol, back, grad, grad_far,
    grad_near, back_out, back_in, arrive, send, recv,
):
    p = Peers()
    links = Links(send, recv)
    p.greet(3)
    weights = (w_own, w_far)
    block_of = (p.t, p.xp)
    at = lambda t: pl.ds(pl.multiple_of(t * BLOCK, BLOCK), BLOCK)

    part_at(out_all, p.t)[...] = out_own[...]
    out_all[ROWS:, :] = jnp.zeros((LANES - ROWS, D), BF16)
    g_out = Gather(links, p, lambda t: part_at(out_all, t))
    grad_near[...] = grad_own[...].astype(BF16)
    c_grad = links.copy(grad_near, grad_far, (p.dp, p.xp))
    c_grad.start()
    g_out.start()
    halvers = {
        j: Halver(links, p, g_conv.at[j], t_conv.at[j], None, arrive.at[j]) for j in (3, 2, 1)
    }

    def masks(count):
        _, col = grid_place((count, LANES), 1, 0)
        not_first = jnp.where(col > 0.5, 1.0, 0.0)
        not_last = jnp.where(col < GW - 1.5, 1.0, 0.0)
        return cell_mask((count, LANES), 1, 0, length[0]), not_first, not_last

    _, not_first8, not_last8 = masks(8)
    cells16, not_first16, not_last16 = masks(16)

    start_all[:, ROWS:] = jnp.zeros((CH, LANES - ROWS), F32)
    start_all[:, 0:ROWS] = field[...].astype(F32).T

    def rows_at(i):
        return pl.ds(pl.multiple_of(i * 16, 16), 16)

    def into_at(b, i):
        return pl.ds(pl.multiple_of(block_of[b] * BLOCK + i * 16, 16), 16)

    def open_rows(i, carry):
        x_all[0, rows_at(i), :] = gelu(start_all[rows_at(i), :]).astype(BF16)
        return carry

    lax.fori_loop(0, CH // 16, open_rows, 0)

    def convolve(index, b, use):
        for c in range(LANES // CHUNK):
            lanes = slice(c * CHUNK, (c + 1) * CHUNK)
            wide[:, lanes] = dot(weights[b][index], x_all[index, :, lanes])

        def rows16(i, carry):
            halves = []
            for half in range(2):
                total = None
                for q in range(3):
                    tap = lambda r: wide[
                        pl.ds(pl.multiple_of((r * 3 + q) * BLOCK + i * 16 + half * 8, 8), 8), :
                    ]
                    three = (
                        tap(1)
                        + pltpu.roll(tap(0), GW, 1)
                        + pltpu.roll(tap(2), LANES - GW, 1)
                    )
                    if q == 0:
                        three = pltpu.roll(three, 1, 1) * not_first8
                    if q == 2:
                        three = pltpu.roll(three, LANES - 1, 1) * not_last8
                    total = three if total is None else total + three
                halves.append(total)
            use(i, cells16 * jnp.concatenate(halves, axis=0))
            return carry

        lax.fori_loop(0, BLOCK // 16, rows16, 0)

    def share(index):
        copies = [
            links.copy(x_all.at[index, at(t), :], x_all.at[index, at(t), :], (p.dp, p.sib))
            for t in block_of
        ]
        for c in copies:
            c.start()
        return copies

    def settle(copies):
        for c in copies:
            c.wait_recv()

    pending = []
    for unit in range(2):
        for b in range(2):
            def use_first(i, value, b=b):
                low, steep = gelu_and_slope(value)
                x_all[2 * unit + 1, into_at(b, i), :] = low.astype(BF16)
                steep_first[unit, b, rows_at(i), :] = steep

            convolve(2 * unit, b, use_first)
        copies = share(2 * unit + 1)
        pending += copies
        if unit == 0:
            g_out.forward()
            for b in range(2):
                def opening(i, carry, b=b):
                    value = start_all[into_at(b, i), :]
                    state[b, rows_at(i), :] = value
                    steep_state[0, b, rows_at(i), :] = gelu_and_slope(value)[1]
                    return carry

                lax.fori_loop(0, BLOCK // 16, opening, 0)
        settle(copies)
        for b in range(2 - unit):
            def use_second(i, value, b=b):
                fresh = state[b, rows_at(i), :] + value
                if unit == 0:
                    low, steep = gelu_and_slope(fresh)
                    state[b, rows_at(i), :] = fresh
                    x_all[2, into_at(b, i), :] = low.astype(BF16)
                    steep_state[1, b, rows_at(i), :] = steep
                else:
                    result[rows_at(i), :] = fresh

            convolve(2 * unit + 1, b, use_second)
        if unit == 0:
            copies = share(2)
            pending += copies
            settle(copies)

    c_grad.wait_recv()
    grad[0] = grad_own[...]
    grad[1] = grad_far[...].astype(F32)

    def spread(b, value_of):
        def rows16(i, carry):
            value = value_of(rows_at(i)).astype(BF16).astype(F32)
            for q in range(3):
                side = value
                if q == 0:
                    side = pltpu.roll(value, LANES - 1, 1) * not_last16
                if q == 2:
                    side = pltpu.roll(value, 1, 1) * not_first16
                for r in range(3):
                    moved = side
                    if r == 0:
                        moved = pltpu.roll(side, LANES - GW, 1)
                    if r == 2:
                        moved = pltpu.roll(side, GW, 1)
                    into = pl.ds(pl.multiple_of((r * 3 + q) * BLOCK + i * 16, 16), 16)
                    dcol[b, into, :] = moved.astype(BF16)
            return carry

        lax.fori_loop(0, BLOCK // 16, rows16, 0)

    def conv_back(index, turn, between):
        flip[0] = w_own[index].T
        flip[1] = w_far[index].T
        for c in range(LANES // CHUNK):
            lanes = slice(c * CHUNK, (c + 1) * CHUNK)
            back[:, lanes] = dot(flip[0], dcol[0, :, lanes]) + dot(flip[1], dcol[1, :, lanes])
        copies = []
        for b, t in enumerate((p.sib, p.diag)):
            back_out[turn, b] = back[at(t), :].astype(BF16)
            c = links.copy(back_out.at[turn, b], back_in.at[turn, b], (p.dp, p.sib))
            c.start()
            copies.append(c)
        weight_grad = dot(dcol[0], x_all[index], (1, 1)).astype(BF16)
        g_conv[index, 0:WIDE, :] = weight_grad[:, 0:SLOT]
        g_conv[index, WIDE:, :] = weight_grad[:, SLOT:]
        between()
        for c in copies:
            c.wait_recv()
        pending.extend(copies)

        def value(b, rows):
            far = pl.ds(pl.multiple_of(block_of[b] * BLOCK + rows.start, 16), 16)
            return back[far, :] + back_in[turn, b, rows, :].astype(F32)

        return value

    def between(turn):
        def act():
            if turn == 0:
                halvers[3].s(0)
            if turn == 1:
                halvers[3].a(0)
                halvers[3].s(1)
                halvers[2].s(0)
            if turn == 2:
                halvers[3].a(1)
                halvers[3].s(2)
                halvers[2].a(0)
                halvers[2].s(1)
                halvers[1].s(0)

        return act

    inside16 = jnp.where(
        lax.broadcasted_iota(jnp.int32, (16, LANES), 1) < SLOTS, 1.0, 0.0
    )
    for turn, unit in enumerate((1, 0)):
        for b in range(2):
            spread(b, lambda rows, b=b: cells16 * grad[b, rows, :])
        d_mid = conv_back(2 * unit + 1, 2 * turn, between(2 * turn))
        for b in range(2):
            spread(
                b,
                lambda rows, b=b: cells16 * d_mid(b, rows) * steep_first[unit, b, rows, :],
            )
        d_in = conv_back(2 * unit, 2 * turn + 1, between(2 * turn + 1))
        for b in range(2):
            def renew(i, carry, b=b):
                rows = rows_at(i)
                fresh = grad[b, rows, :] + d_in(b, rows) * steep_state[unit, b, rows, :]
                if unit == 1:
                    grad[b, rows, :] = fresh
                else:
                    tap_grad[into_at(b, i), :] = (inside16 * fresh).astype(BF16)
                return carry

            lax.fori_loop(0, BLOCK // 16, renew, 0)
    copies = [
        links.copy(tap_grad.at[at(t), :], tap_grad.at[at(t), :], (p.dp, p.sib))
        for t in block_of
    ]
    for c in copies:
        c.start()
    halvers[3].a(2)
    halvers[2].a(1)
    halvers[1].a(0)
    settle(copies)
    for c in pending + copies + [c_grad]:
        c.wait_send()
    for h in halvers.values():
        h.finish()
    g_out.finish()


FLAT = (2 * WIDE, SLOT)


def conv_call(bits, *args):
    outs = [
        ((BLOCK, LANES), F32),
        ((CH, LANES), BF16),
        ((4,) + FLAT, BF16),
        ((4,) + FLAT, BF16),
        ((LANES, D), BF16),
    ]
    scratch = [
        pltpu.VMEM((CH, LANES), F32),
        pltpu.VMEM((2, BLOCK, LANES), F32),
        pltpu.VMEM((2, 2, BLOCK, LANES), F32),
        pltpu.VMEM((2, 2, BLOCK, LANES), F32),
        pltpu.VMEM((4, CH, LANES), BF16),
        pltpu.VMEM((WIDE, LANES), F32),
        pltpu.VMEM((2, CH, WIDE), BF16),
        pltpu.VMEM((2, WIDE, LANES), BF16),
        pltpu.VMEM((CH, LANES), F32),
        pltpu.VMEM((2, BLOCK, LANES), F32),
        pltpu.VMEM((BLOCK, LANES), BF16),
        pltpu.VMEM((BLOCK, LANES), BF16),
        pltpu.VMEM((4, 2, BLOCK, LANES), BF16),
        pltpu.VMEM((4, 2, BLOCK, LANES), BF16),
        pltpu.VMEM((4,) + landing(*FLAT, bits).shape, BF16),
    ] + sems(40)
    return call(conv_kernel, outs, [smem] + [vmem] * 5, scratch, 2, 9_000_000_000, args)


def lift(field, joined, table):
    for a in range(GH):
        here = field[:, a * GW : (a + 1) * GW]
        up, down = max(a - 1, 0), min(a + 1, GH - 1)
        for side, other in enumerate((up, down)):
            line = 0.75 * here + 0.25 * field[:, other * GW : (other + 1) * GW]
            joined[2 * a + side] = split_dot(line, table).astype(BF16)


def mlp_back_kernel(
    length, tap_grad, tap_all, cot_hbm, slope, act, normed_two, w_up, w_down, hidden_own, gain_two,
    out_all, field, g_conv, t_conv,
    grad_hidden, branch, t_down, t_up, g_tap, g_gain, joined, conv_sum,
    cot, tap_tm, d_mlp, d_pre, mine_block, out_c, out_x, in_c, in_x, mine,
    low_down, low_up, conv_run, conv_res, conv_arrive, arrive, local, send, recv,
):
    p = Peers()
    links = Links(send, recv)
    bring = pltpu.make_async_copy(cot_hbm, cot.at[pl.ds(0, SLOTS), :], local.at[0])
    bring.start()
    cot[SLOTS:, :] = jnp.zeros((ROWS - SLOTS, D), BF16)
    p.greet(3)
    conv = {
        j: Halver(
            links, p, (g_conv if j == 0 else t_conv).at[j], conv_run.at[j], conv_res.at[j],
            conv_arrive.at[j], after=j,
        )
        for j in range(4)
    }
    h_up = Halver(links, p, low_up, t_up, None, arrive.at[0])
    h_down = Halver(links, p, low_down, t_down, None, arrive.at[1], order=(1, 0, 2))

    def tick(at):
        for j in (3, 2, 1, 0):
            if j <= at + j <= 6:
                conv[j].step(at + j)

    tick(0)
    tap_tm[...] = tap_grad[...].T
    bring.wait()

    def part(owner):
        off = pl.multiple_of(owner * PART, 16)
        rows = pl.ds(off, PART)
        block = cell_mask((PART, D), 0, off, length[0]) * (
            cot[rows, :].astype(F32) + dot(tap_tm[rows, :], tap_all[...])
        )
        mine_block[...] = block
        low = block.astype(BF16)
        d_mlp[rows, :] = low
        steep = (dot(low, w_down[...], (1, 1)) * slope[rows, :].astype(F32)).astype(BF16)
        d_pre[rows, :] = steep
        return dot(steep, w_up[...], (1, 1))

    sums = Scatter(links, p, out_c, out_x, in_c, in_x, mine)
    sums.far(part)
    tick(1)
    sums.near(part)
    tick(2)
    low_up[...] = dot(normed_two[0:ROWS, :], d_pre[...], (0, 0)).astype(BF16)
    h_up.s(0)
    low_down[...] = dot(act[...], d_mlp[...], (0, 0)).astype(BF16)
    h_down.s(0)
    tick(3)
    gain = gain_two[...].reshape(1, D)
    gathers = []
    gain_part = jnp.zeros((1, D), F32)
    for at, piece in enumerate(PIECES):
        rows = pl.ds(*piece)
        total = sums.piece(at)
        scaled, inverse = norm(hidden_own[rows, :])
        inner, add = norm_back(total, scaled, inverse, gain)
        after = mine_block[rows, :] + inner
        grad_hidden[rows, :] = after
        gain_part = gain_part + add
        branch[pl.ds(pl.multiple_of(p.t * PART + piece[0], 16), piece[1]), :] = after.astype(BF16)
        g = Gather(links, p, lambda t: piece_at(branch, t, piece))
        g.start()
        gathers.append(g)
    g_gain[...] = gain_part
    tick(4)
    lift(field, joined, upsample_table(GW).T.astype(BF16))
    tick(5)
    g_tap[...] = dot(
        tap_grad[pl.ds(pl.multiple_of(p.t * BLOCK, BLOCK), BLOCK), :], out_all[...]
    ).astype(BF16)
    gathers[0].forward()
    tick(6)
    for j in range(4):
        for side in range(2):
            conv_sum[j, :, side * SLOT : (side + 1) * SLOT] = conv_res[
                j, side * WIDE : (side + 1) * WIDE, :
            ].astype(F32)
    gathers[1].forward()
    h_up.a(0)
    h_down.a(0)
    for g in gathers:
        g.finish()
    sums.finish()
    for h in list(conv.values()) + [h_up, h_down]:
        h.finish()


def mlp_back_call(bits, *args):
    outs = [
        ((PART, D), F32),
        ((ROWS, D), BF16),
        ((D, D), BF16),
        ((D, D), BF16),
        ((BLOCK, D), BF16),
        ((1, D), F32),
        ((2 * GH, BLOCK, 2 * GW), BF16),
        ((4, WIDE, CH), F32),
    ]
    scratch = [
        pltpu.VMEM((ROWS, D), BF16),
        pltpu.VMEM((LANES, CH), BF16),
        pltpu.VMEM((ROWS, D), BF16),
        pltpu.VMEM((ROWS, D), BF16),
        pltpu.VMEM((PART, D), F32),
    ] + scatter_scratch() + [
        pltpu.VMEM((D, D), BF16),
        pltpu.VMEM((D, D), BF16),
        pltpu.VMEM((4,) + FLAT, BF16),
        pltpu.VMEM((4,) + FLAT, BF16),
        pltpu.VMEM((4,) + landing(*FLAT, bits).shape, BF16),
        pltpu.VMEM((2,) + landing(D, D, bits).shape, BF16),
        pltpu.SemaphoreType.DMA((1,)),
    ] + sems(60)
    return call(
        mlp_back_kernel, outs, [smem, vmem, vmem, anywhere] + [vmem] * 11, scratch, 3,
        9_000_000_000, args,
    )


def attend_back_kernel(
    length, branch, grad_hidden, w_out, mixed, q_cm, k_tm, v_tm, k_cm, lse, normed_one, w_qkv,
    tok_hbm, gain_one, up_in, down_in, tap_in, gain_in,
    grad_tok, qkv_sum, out_sum, up_sum, down_sum, tap_sum, gain_sum,
    tok, d_mix, acc_k, acc_v, d_cm, d_tm, w_by_head, out_c, out_x, in_c, in_x, mine,
    ot, ot_run, ot_res, ot_arrive, up_run, up_res, up_arrive, down_run, down_res, down_arrive,
    head, head_run, head_res, head_arrive, gain_out, gain_arrive, local, send, recv,
):
    p = Peers()
    links = Links(send, recv)
    bring = pltpu.make_async_copy(tok_hbm, tok.at[pl.ds(0, SLOTS), :], local.at[0])
    bring.start()
    tok[SLOTS:, :] = jnp.zeros((ROWS - SLOTS, D), BF16)
    p.greet(p.bits())
    h_up = Halver(links, p, up_in, up_run, up_res, up_arrive, after=1)
    h_down = Halver(links, p, down_in, down_run, down_res, down_arrive, order=(1, 0, 2), after=1)
    h_ot = Halver(links, p, ot, ot_run, ot_res, ot_arrive, order=(1, 0, 2))
    h_head = [
        Halver(links, p, head.at[h], head_run.at[h], head_res.at[h], head_arrive.at[h])
        for h in range(3)
    ]
    gains = Doubler(links, p, gain_out, gain_arrive)
    done = {id(h): 0 for h in [h_ot] + h_head}
    done[id(h_up)] = done[id(h_down)] = 1

    def tick(*halvers):
        for h in halvers:
            if done[id(h)] < 7:
                h.step(done[id(h)])
                done[id(h)] += 1

    tick(h_up, h_down)
    d_mix[:, ROWS:] = jnp.zeros((192, LANES - ROWS), BF16)
    d_cm[...] = jnp.zeros(d_cm.shape, BF16)
    ot[0:192, :] = dot(mixed[:, 0:ROWS], branch[...]).astype(BF16)
    ot[192:, :] = tap_in[...]
    tick(h_ot)
    d_mix[:, 0:ROWS] = dot(w_out[...], branch[...], (1, 1)).astype(BF16)
    for h in range(3):
        for part in range(3):
            w_by_head[h * 192 + part * 64 : h * 192 + part * 64 + 64, :] = w_qkv[
                part * 192 + h * 64 : part * 192 + h * 64 + 64, :
            ]
    for h in range(3):
        heads = slice(h * HEAD_DIM, (h + 1) * HEAD_DIM)
        acc_k[...] = jnp.zeros(acc_k.shape, F32)
        acc_v[...] = jnp.zeros(acc_v.shape, F32)

        def attend(c, carry):
            lanes = pl.ds(pl.multiple_of(c * CHUNK, CHUNK), CHUNK)
            dm = d_mix[heads, lanes]
            inner = jnp.sum(
                dm.astype(F32) * mixed[heads, lanes].astype(F32), axis=0, keepdims=True
            )
            probs = jnp.exp(
                dot(k_tm[h, 0:ROWS, :], q_cm[h, :, lanes]) - lse[h : h + 1, lanes]
            )
            d_probs = dot(v_tm[h, 0:ROWS, :], dm)
            d_raw = (probs * (d_probs - inner)).astype(BF16)
            acc_v[...] += dot(probs.astype(BF16), dm, (1, 1))
            acc_k[...] += dot(d_raw, q_cm[h, 0:HEAD_DIM, lanes], (1, 1))
            d_q = dot(k_cm[heads, 0:ROWS], d_raw) * 0.125
            d_cm[h * 192 : h * 192 + 64, lanes] = d_q.astype(BF16)
            return carry

        lax.fori_loop(0, 2, attend, 0)
        tick(h_up, h_down, h_ot, *h_head[:h])
        lax.fori_loop(2, LANES // CHUNK, attend, 0)
        d_cm[h * 192 + 64 : h * 192 + 128, 0:ROWS] = acc_k[...].T.astype(BF16)
        d_cm[h * 192 + 128 : h * 192 + 192, 0:ROWS] = acc_v[...].T.astype(BF16)
        three = dot(d_cm[h * 192 : (h + 1) * 192, :], normed_one[...]).astype(BF16)
        head[h, 0:192, :] = three[:, 0:384]
        head[h, 192:, :] = three[:, 384:]
        tick(h_up, h_down, h_ot, *h_head[: h + 1])
    d_tm[...] = d_cm[...].T

    def part(owner):
        rows = pl.ds(pl.multiple_of(owner * PART, 16), PART)
        return dot(d_tm[rows, :], w_by_head[...])

    sums = Scatter(links, p, out_c, out_x, in_c, in_x, mine)
    sums.far(part)
    tick(h_up, h_down, h_ot, *h_head)
    sums.near(part)
    tick(h_up, h_down, h_ot, *h_head)
    bring.wait()
    gain = gain_one[...].reshape(1, D)
    gathers = []
    gain_part = jnp.zeros((1, D), F32)
    for at, piece in enumerate(PIECES):
        rows = pl.ds(*piece)
        place = pl.ds(pl.multiple_of(p.t * PART + piece[0], 16), piece[1])
        total = sums.piece(at)
        scaled, inverse = norm(tok[place, :].astype(F32))
        inner, add = norm_back(total, scaled, inverse, gain)
        gain_part = gain_part + add
        grad_tok[place, :] = (grad_hidden[rows, :] + inner).astype(BF16)
        g = Gather(links, p, lambda t: piece_at(grad_tok, t, piece))
        g.start()
        gathers.append(g)
        tick(h_up, h_down, h_ot, *h_head)
    row = lax.broadcasted_iota(jnp.int32, (8, D), 0)
    gains.start(
        jnp.where(row == 0, gain_part, 0.0) + jnp.where(row == 1, gain_in[...], 0.0)
    )
    for h in (h_up, h_down, h_ot):
        while done[id(h)] < 7:
            tick(h)
    up_sum[...] = up_res[...].astype(F32)
    down_sum[...] = down_res[...].astype(F32)
    out_sum[...] = ot_res[0:192, :].astype(F32)
    tap_sum[...] = ot_res[192:, :].astype(F32)
    gathers[0].forward()
    gains.step()
    while any(done[id(h)] < 7 for h in h_head):
        tick(*h_head)
        if len(gains.copies) < len(gains.to):
            gains.step()
    gathers[1].forward()
    for h in range(3):
        for part_at_ in range(3):
            for side in range(2):
                rows = side * 192 + part_at_ * 64
                qkv_sum[
                    part_at_ * 192 + h * 64 : part_at_ * 192 + h * 64 + 64,
                    side * 384 : (side + 1) * 384,
                ] = head_res[h, rows : rows + 64, :].astype(F32)
    gain_sum[...] = gains.finish()
    for g in gathers:
        g.finish()
    sums.finish()
    for h in [h_up, h_down, h_ot] + h_head:
        h.finish()


def attend_back_call(bits, *args):
    outs = [
        ((ROWS, D), BF16),
        ((3 * 192, D), F32),
        ((192, D), F32),
        ((D, D), F32),
        ((D, D), F32),
        ((BLOCK, D), F32),
        ((8, D), F32),
    ]

    def reducing(rows, columns, count=None):
        lead = () if count is None else (count,)
        return [
            pltpu.VMEM(lead + (rows, columns), BF16),
            pltpu.VMEM(lead + (rows, columns), BF16),
            pltpu.VMEM(lead + landing(rows, columns, bits).shape, BF16),
        ]

    scratch = [
        pltpu.VMEM((ROWS, D), BF16),
        pltpu.VMEM((192, LANES), BF16),
        pltpu.VMEM((ROWS, HEAD_DIM), F32),
        pltpu.VMEM((ROWS, HEAD_DIM), F32),
        pltpu.VMEM((3 * 192, LANES), BF16),
        pltpu.VMEM((LANES, 3 * 192), BF16),
        pltpu.VMEM((3 * 192, D), BF16),
    ] + scatter_scratch() + [
        pltpu.VMEM((256, D), BF16),
        *reducing(256, D),
        *reducing(D, D),
        *reducing(D, D),
        pltpu.VMEM((3, 384, 384), BF16),
        *reducing(384, 384, 3),
        pltpu.VMEM((2 + bits, 8, D), F32),
        pltpu.VMEM((2 + bits, 8, D), F32),
        pltpu.SemaphoreType.DMA((1,)),
    ] + sems(90)
    return call(
        attend_back_kernel, outs, [smem] + [vmem] * 11 + [anywhere] + [vmem] * 5, scratch, 4,
        12_000_000_000, args,
    )


def per_device(
    bits, tokens, lengths, gain_one, gain_two, w_qkv, w_out, w_up, w_down, w_tap, w_conv,
    cot_tokens, cot_joined,
):
    w_heads = w_qkv.transpose(0, 2, 1).reshape(3 * 192, D)
    conv_w = w_conv.transpose(0, 1, 2, 4, 3).reshape(4, WIDE, CH)
    (
        hidden_own, normed_two, q_cm, k_tm, v_tm, k_cm, lse, mixed, normed_one, tap_all, conv_x,
    ) = attend_call(lengths, tokens, gain_one, gain_two, w_heads, w_out, w_tap.T, conv_w)
    slope, act, out_own, field, conv_far, grad_own = mlp_call(
        lengths, normed_two, hidden_own, w_up, w_down, tap_all, conv_x,
        cot_joined[0].transpose(0, 2, 1),
    )
    result, tap_grad, g_conv, t_conv, out_all = conv_call(
        bits, lengths, field, conv_w, conv_far, grad_own, out_own
    )
    grad_hidden, branch, t_down, t_up, g_tap, gain_part, joined, conv_sum = mlp_back_call(
        bits, lengths, tap_grad, tap_all, cot_tokens, slope, act, normed_two, w_up, w_down,
        hidden_own, gain_two, out_all, result, g_conv, t_conv,
    )
    grad_tok, qkv_sum, out_sum, up_sum, down_sum, tap_sum, gain_sum = attend_back_call(
        bits, lengths, branch, grad_hidden, w_out, mixed, q_cm, k_tm, v_tm, k_cm, lse, normed_one,
        w_heads, tokens, gain_one, t_up, t_down, g_tap, gain_part,
    )
    return (
        out_all[:SLOTS],
        joined.transpose(0, 2, 1)[None],
        grad_tok[:SLOTS],
        qkv_sum.reshape(3, 192, D).transpose(0, 2, 1),
        out_sum,
        up_sum,
        down_sum,
        tap_sum.T,
        conv_sum.reshape(4, 3, 3, BLOCK, CH).transpose(0, 1, 2, 4, 3),
        gain_sum[0],
        gain_sum[1],
    )


def solution(mesh):
    placed = (
        P("dp", None),
        P("dp"),
        P(),
        P(),
        P(None, None, "tensor"),
        P("tensor", None),
        P(None, "tensor"),
        P("tensor", None),
        P(None, "tensor"),
        P(None, None, None, None, "tensor"),
        P("dp", None),
        P("dp", None, None, "tensor"),
    )
    return jax.shard_map(
        functools.partial(per_device, mesh.shape["dp"].bit_length() - 1),
        mesh=mesh,
        in_specs=placed,
        out_specs=(
            P("dp", None),
            P("dp", None, None, "tensor"),
            P("dp", None),
            P(None, None, "tensor"),
            P("tensor", None),
            P(None, "tensor"),
            P("tensor", None),
            P(None, "tensor"),
            P(None, None, None, None, "tensor"),
            P(),
            P(),
        ),
        check_vma=False,
    )
```

```python
import functools

import jax
import jax.numpy as jnp
from jax import lax
from jax.experimental import pallas as pl
from jax.experimental.pallas import tpu as pltpu
from jax.sharding import PartitionSpec as P

HEAD_DIM = 64
GH = 30
GW = 40
SH = 24
SW = 24
SLOTS = GH * GW
D = 768
CH = 256
BLOCK = 64
TAPS = 9
WIDE = TAPS * BLOCK
PART = 304
ROWS = 4 * PART
LANES = 1280
CHUNK = 256
SLOT = 128
F32 = jnp.float32
BF16 = jnp.bfloat16
MESH = pl.DeviceIdType.MESH
VMEM_LIMIT = 60 * 2**20

vmem = pl.BlockSpec(memory_space=pltpu.VMEM)
smem = pl.BlockSpec(memory_space=pltpu.SMEM)
anywhere = pl.BlockSpec(memory_space=pl.ANY)


def dot(a, b, dims=(1, 0)):
    return lax.dot_general(
        a, b, (((dims[0],), (dims[1],)), ((), ())), preferred_element_type=F32
    )


def gelu(v):
    return 0.5 * v * (1.0 + lax.erf(v * 0.7071067811865476))


def gelu_and_slope(v):
    share = 0.5 * (1.0 + lax.erf(v * 0.7071067811865476))
    return v * share, share + v * jnp.exp(-0.5 * v * v) * 0.3989422804014327


def norm(v):
    centred = v - jnp.mean(v, axis=-1, keepdims=True)
    spread = jnp.mean(centred * centred, axis=-1, keepdims=True)
    inverse = lax.rsqrt(spread + 1e-06)
    return centred * inverse, inverse


def norm_back(incoming, scaled, inverse, gain):
    weighted = incoming * gain
    inner = (
        weighted
        - jnp.mean(weighted, axis=-1, keepdims=True)
        - scaled * jnp.mean(weighted * scaled, axis=-1, keepdims=True)
    )
    return inverse * inner, jnp.sum(incoming * scaled, axis=0, keepdims=True)


def grid_place(shape, axis, offset):
    index = (lax.broadcasted_iota(jnp.int32, shape, axis) + offset).astype(F32)
    row = jnp.floor((index + 0.5) * (1.0 / GW))
    return row, index - GW * row


def cell_mask(shape, axis, offset, length):
    row, col = grid_place(shape, axis, offset)
    large = length == SLOTS
    height = jnp.where(large, float(GH), float(SH))
    breadth = jnp.where(large, float(GW), float(SW))
    return jnp.where((row < height) & (col < breadth), 1.0, 0.0)


class Peers:
    def __init__(self):
        self.dp = lax.axis_index("dp")
        self.n = lax.axis_size("dp")
        self.t = lax.axis_index("tensor")
        self.sib = self.t + 1 - 2 * lax.rem(self.t, 2)
        self.xp = lax.rem(self.t + 2, 4)
        self.diag = lax.rem(self.sib + 2, 4)

    def bit(self, at):
        return lax.rem(self.dp // (1 << at), 2)

    def mate(self, at):
        return self.dp + (1 - 2 * self.bit(at)) * (1 << at)

    def bits(self):
        return self.n.bit_length() - 1

    def greet(self, bits=0):
        barrier = pltpu.get_barrier_semaphore()
        others = [(self.dp, self.sib), (self.dp, self.xp)]
        others += [(self.mate(at), self.t) for at in range(bits)]
        for other in others:
            pl.semaphore_signal(barrier, inc=1, device_id=other, device_id_type=MESH)
        pl.semaphore_wait(barrier, len(others))


class Links:
    def __init__(self, send, recv):
        self.send, self.recv, self.used = send, recv, 0

    def copy(self, src, dst, device):
        at = self.used
        self.used += 1
        return pltpu.make_async_remote_copy(
            src_ref=src,
            dst_ref=dst,
            send_sem=self.send.at[at],
            recv_sem=self.recv.at[at],
            device_id=device,
            device_id_type=MESH,
        )


class Gather:
    def __init__(self, links, peers, place):
        p = peers
        self.x = links.copy(place(p.t), place(p.t), (p.dp, p.xp))
        self.c = links.copy(place(p.t), place(p.t), (p.dp, p.sib))
        self.f = links.copy(place(p.xp), place(p.xp), (p.dp, p.sib))

    def start(self, clock=None, size=0):
        self.x.start()
        self.c.start()
        if clock is not None:
            clock.later(clock.flight("x", size), self.forward)

    def forward(self):
        self.x.wait_recv()
        self.f.start()

    def finish(self):
        self.c.wait_recv()
        self.f.wait_recv()
        self.x.wait_send()
        self.c.wait_send()
        self.f.wait_send()


PIECES = ((0, 160), (160, PART - 160))


class Scatter:
    def __init__(self, links, peers, out_c, out_x, in_c, in_x, mine):
        p = peers
        self.p, self.out_c, self.out_x, self.in_c, self.in_x = p, out_c, out_x, in_c, in_x
        self.mine = mine
        self.c = [links.copy(out_c.at[i], in_c.at[i], (p.dp, p.sib)) for i in range(2)]
        self.x = [
            links.copy(out_x.at[pl.ds(*piece), :], in_x.at[pl.ds(*piece), :], (p.dp, p.xp))
            for piece in PIECES
        ]

    def far(self, part):
        p = self.p
        self.out_c[0] = part(p.diag).astype(BF16)
        self.c[0].start()
        self.mine[...] = part(p.xp)
        self.c[0].wait_recv()
        for copy, piece in zip(self.x, PIECES):
            rows = pl.ds(*piece)
            self.out_x[rows, :] = (self.mine[rows, :] + self.in_c[0, rows, :].astype(F32)).astype(
                BF16
            )
            copy.start()

    def near(self, part):
        p = self.p
        self.out_c[1] = part(p.sib).astype(BF16)
        self.c[1].start()
        self.mine[...] = part(p.t)
        self.c[1].wait_recv()
        self.mine[...] += self.in_c[1].astype(F32)

    def piece(self, at):
        rows = pl.ds(*PIECES[at])
        self.x[at].wait_recv()
        return self.mine[rows, :] + self.in_x[rows, :].astype(F32)

    def finish(self):
        for copy in self.c + self.x:
            copy.wait_send()


class Clock:
    def __init__(self):
        self.now, self.free, self.queue, self.count = 0.0, {}, [], 0

    def flight(self, axis, size):
        start = max(self.now, self.free.get(axis, 0.0))
        took = size / {"core": 400e3, "zz": 23e3}.get(axis, 46e3)
        self.free[axis] = start + took
        return start + took + (1.0 if axis == "core" else 2.6)

    def later(self, when, act):
        self.queue.append((when, self.count, act))
        self.count += 1

    def work(self, took):
        self.now += took
        while self.queue and min(self.queue)[0] <= self.now:
            first = min(self.queue)
            self.queue.remove(first)
            first[2]()

    def drain(self):
        while self.queue:
            self.work(max(min(self.queue)[0] - self.now, 0.0))


AXES = ("y", "z", "zz")


class Halver:
    def __init__(self, links, peers, clock, array, arrive, result, order=(0, 1, 2), after=0):
        p = self.p = peers
        self.links, self.clock, self.array, self.arrive = links, clock, array, arrive
        self.result = result
        self.rows, self.columns = array.shape
        self.order, self.at = order, after
        self.fresh = after
        base, size = 0, self.rows
        self.keep, self.give, self.to = [], [], []
        for at in order:
            size //= 2
            mine = p.bit(at)
            self.give.append(pl.ds(pl.multiple_of(base + (1 - mine) * size, 16), size))
            base = base + mine * size
            self.keep.append(pl.ds(pl.multiple_of(base, 16), size))
            self.to.append((p.mate(at), p.t))
        self.sent, self.rs, self.ag = [], {}, {}
        self.slot = [0, self.rows // 2, 3 * self.rows // 4]

    def send(self, k, copy):
        copy.start()
        self.sent.append(copy)
        size = (self.rows >> (k + 1)) * self.columns * 2
        self.clock.later(self.clock.flight(AXES[self.order[k]], size), self.step)

    def s(self, k):
        land = pl.ds(self.slot[k], self.rows >> (k + 1))
        copy = self.links.copy(self.array.at[self.give[k], :], self.arrive.at[land, :], self.to[k])
        self.rs[k] = (copy, land)
        self.send(k, copy)

    def add(self, land, keep):
        self.array[keep, :] = (
            self.array[keep, :].astype(F32) + self.arrive[land, :].astype(F32)
        ).astype(BF16)

    def a(self, k):
        copy, land = self.rs[k]
        copy.wait_recv()
        keep = self.keep[k]
        self.add(land, keep)
        if k == 2:
            size = self.rows >> 3
            for extra in range(3, self.p.bits()):
                land = pl.ds((4 + extra) * size, size)
                copy = self.links.copy(
                    self.array.at[keep, :], self.arrive.at[land, :], (self.p.mate(extra), self.p.t)
                )
                copy.start()
                copy.wait_recv()
                copy.wait_send()
                self.add(land, keep)

    def g(self, k):
        region = self.keep[k]
        if k == 2:
            self.result[region, :] = self.array[region, :]
        copy = self.links.copy(self.result.at[region, :], self.result.at[region, :], self.to[k])
        self.ag[k] = copy
        self.send(k, copy)

    def step(self, last=7):
        at = self.at
        if at and at <= 3 and at > self.fresh:
            self.a(at - 1)
        if at < 3:
            self.s(at)
        elif at == 3:
            self.g(2)
        else:
            self.ag[6 - at].wait_recv()
            if at < 6:
                self.g(5 - at)
        self.at += 1

    def finish(self):
        for copy in self.sent:
            copy.wait_send()


def landing(rows, columns, bits):
    return pltpu.VMEM((rows + max(bits - 4, 0) * (rows // 8), columns), BF16)


class Doubler:
    def __init__(self, links, peers, outgoing, incoming):
        p = peers
        self.links, self.outgoing, self.incoming = links, outgoing, incoming
        self.to = [(p.dp, p.sib), (p.dp, p.xp)] + [(p.mate(at), p.t) for at in range(p.bits())]
        self.copies = []

    def start(self, value):
        self.value = value
        self.send()

    def send(self):
        at = len(self.copies)
        if at < len(self.to):
            self.outgoing[at] = self.value
            copy = self.links.copy(self.outgoing.at[at], self.incoming.at[at], self.to[at])
            copy.start()
            self.copies.append(copy)

    def step(self):
        at = len(self.copies) - 1
        self.copies[at].wait_recv()
        self.value = self.value + self.incoming[at]
        self.send()

    def finish(self):
        while len(self.copies) < len(self.to):
            self.step()
        self.copies[-1].wait_recv()
        self.value = self.value + self.incoming[len(self.to) - 1]
        for copy in self.copies:
            copy.wait_send()
        return self.value


def sems(count):
    return [pltpu.SemaphoreType.DMA((count,)), pltpu.SemaphoreType.DMA((count,))]


def part_at(ref, owner):
    return ref.at[pl.ds(pl.multiple_of(owner * PART, 16), PART), :]


def piece_at(ref, owner, piece):
    return ref.at[pl.ds(pl.multiple_of(owner * PART + piece[0], 16), piece[1]), :]


def upsample_table(count):
    shape = (2 * count, count)
    target = lax.broadcasted_iota(jnp.int32, shape, 0)
    source = lax.broadcasted_iota(jnp.int32, shape, 1)
    nearest = lax.shift_right_logical(target, 1)
    odd = target - 2 * nearest
    further = jnp.clip(nearest + 2 * odd - 1, 0, count - 1)
    return jnp.where(source == nearest, 0.75, 0.0) + jnp.where(source == further, 0.25, 0.0)


def split_dot(a, table):
    high = a.astype(BF16)
    low = (a - high.astype(F32)).astype(BF16)
    return dot(high, table) + dot(low, table)


def call(kernel, outs, ins, scratch, collective, flops, args):
    return pl.pallas_call(
        kernel,
        out_shape=[jax.ShapeDtypeStruct(*o) for o in outs],
        in_specs=ins,
        out_specs=[vmem] * len(outs),
        scratch_shapes=scratch,
        cost_estimate=pl.CostEstimate(
            flops=flops, bytes_accessed=20_000_000, transcendentals=0
        ),
        compiler_params=pltpu.CompilerParams(
            collective_id=collective,
            has_side_effects=True,
            vmem_limit_bytes=VMEM_LIMIT,
        )
        if collective is not None
        else pltpu.CompilerParams(vmem_limit_bytes=VMEM_LIMIT),
    )(*args)


def attend_kernel(
    length, tok_hbm, gain_one, gain_two, w_qkv, w_out, w_tap, w_conv,
    hidden_own, normed_two, q_cm, k_tm, v_tm, k_cm, lse, mixed, normed_one, tap_all, conv_x,
    tok, hidden, mixed_all, out_all, v_cm, local, send, recv,
):
    p = Peers()
    links = Links(send, recv)
    bring = pltpu.make_async_copy(tok_hbm, tok.at[pl.ds(0, SLOTS), :], local.at[0])
    bring.start()
    tok[SLOTS:, :] = jnp.zeros((LANES - SLOTS, D), BF16)
    place_out = lambda t: out_all.at[pl.ds(pl.multiple_of(t * 192, 64), 192), :]
    place_tap = lambda t: tap_all.at[pl.ds(pl.multiple_of(t * 64, 64), 64), :]
    place_out(p.t)[...] = w_out[...]
    place_tap(p.t)[...] = w_tap[...]
    p.greet()
    g_out = Gather(links, p, place_out)
    g_tap = Gather(links, p, place_tap)
    quarter = lax.rem(p.dp, 4)
    c_conv = links.copy(w_conv.at[quarter], conv_x, (p.dp, p.xp))
    g_out.start()
    g_tap.start()
    bring.wait()
    gain = gain_one[...].reshape(1, D)
    lane = lax.broadcasted_iota(jnp.int32, (CHUNK, SLOT), 1)
    one_row = jnp.where(
        lax.broadcasted_iota(jnp.int32, (HEAD_DIM, CHUNK), 0) == 0, 1.0, 0.0
    ).astype(BF16)

    def project(i, carry):
        off = pl.multiple_of(i * CHUNK, CHUNK)
        rows = pl.ds(off, CHUNK)
        scaled, _ = norm(tok[rows, :].astype(F32))
        normed = (scaled * gain).astype(BF16)
        normed_one[rows, :] = normed
        bias = jnp.where(cell_mask((CHUNK, SLOT), 0, off, length[0]) > 0.5, 0.0, -1e30)
        bias = jnp.where(lane == HEAD_DIM, bias, 0.0).astype(BF16)
        qkv = dot(w_qkv[...], normed, (1, 1)).astype(BF16)
        for h in range(3):
            near = slice(h * HEAD_DIM, (h + 1) * HEAD_DIM)
            q_cm[h, 0:HEAD_DIM, rows] = (qkv[near].astype(F32) * 0.125).astype(BF16)
            q_cm[h, HEAD_DIM:, rows] = one_row
            k = qkv[192 + h * HEAD_DIM : 192 + (h + 1) * HEAD_DIM]
            k_cm[near, rows] = k
            k_tm[h, rows, :] = bias
            k_tm[h, rows, 0:HEAD_DIM] = k.T
            v = qkv[384 + h * HEAD_DIM : 384 + (h + 1) * HEAD_DIM]
            v_cm[near, rows] = v
            v_tm[h, rows, :] = v.T
        return carry

    lax.fori_loop(0, LANES // CHUNK, project, 0)
    gathers = []
    for h in range(3):
        heads = slice(h * HEAD_DIM, (h + 1) * HEAD_DIM)

        def attend(c, carry):
            lanes = pl.ds(pl.multiple_of(c * CHUNK, CHUNK), CHUNK)
            s = dot(k_tm[h, 0:ROWS, :], q_cm[h, :, lanes])
            top = jnp.max(s, axis=0, keepdims=True)
            w = jnp.exp(s - top)
            total = jnp.sum(w, axis=0, keepdims=True)
            probs = (w * (1.0 / total)).astype(BF16)
            out = dot(v_cm[heads, 0:ROWS], probs).astype(BF16)
            lse[h : h + 1, lanes] = top + jnp.log(total)
            mixed[heads, lanes] = out
            own = pl.ds(pl.multiple_of(p.t * 192 + h * HEAD_DIM, 64), HEAD_DIM)
            mixed_all[own, lanes] = out
            return carry

        lax.fori_loop(0, LANES // CHUNK, attend, 0)
        place = lambda t, h=h: mixed_all.at[
            pl.ds(pl.multiple_of(t * 192 + h * HEAD_DIM, 64), HEAD_DIM), :
        ]
        g = Gather(links, p, place)
        g.start()
        gathers.append(g)
        if h == 0:
            g_out.forward()
            g_tap.forward()
        else:
            gathers[h - 1].forward()
    c_conv.start()
    gathers[2].forward()
    for g in gathers:
        g.finish()
    g_out.finish()
    g_tap.finish()
    gain_after = gain_two[...].reshape(1, D)

    def finish(i, carry):
        rows = pl.ds(pl.multiple_of(i * CHUNK, CHUNK), CHUNK)
        branch = dot(mixed_all[:, rows], out_all[...], (0, 0))
        after = tok[rows, :].astype(F32) + branch
        hidden[rows, :] = after
        scaled, _ = norm(after)
        normed_two[rows, :] = (scaled * gain_after).astype(BF16)
        return carry

    lax.fori_loop(0, LANES // CHUNK, finish, 0)
    hidden_own[...] = hidden[pl.ds(pl.multiple_of(p.t * PART, 16), PART), :]
    c_conv.wait_recv()
    c_conv.wait_send()


def attend_call(*args):
    outs = [
        ((PART, D), F32),
        ((LANES, D), BF16),
        ((3, SLOT, LANES), BF16),
        ((3, LANES, SLOT), BF16),
        ((3, LANES, HEAD_DIM), BF16),
        ((192, LANES), BF16),
        ((8, LANES), F32),
        ((192, LANES), BF16),
        ((LANES, D), BF16),
        ((CH, D), BF16),
        ((WIDE, CH), BF16),
    ]
    scratch = [
        pltpu.VMEM((LANES, D), BF16),
        pltpu.VMEM((LANES, D), F32),
        pltpu.VMEM((D, LANES), BF16),
        pltpu.VMEM((D, D), BF16),
        pltpu.VMEM((192, LANES), BF16),
        pltpu.SemaphoreType.DMA((1,)),
    ] + sems(16)
    return call(
        attend_kernel, outs, [smem, anywhere] + [vmem] * 6, scratch, 0, 8_000_000_000, args
    )


def lower(cot, grad, tall, table):
    grad[:, SLOTS:] = jnp.zeros((BLOCK, LANES - SLOTS), F32)
    for a in range(GH):
        mid = 0.75 * (cot[2 * a].astype(F32) + cot[2 * a + 1].astype(F32))
        before = cot[max(2 * a - 1, 0)].astype(F32)
        after = cot[min(2 * a + 2, 2 * GH - 1)].astype(F32)
        tall[a * BLOCK : (a + 1) * BLOCK, :] = mid + 0.25 * (before + after)
    for a in range(GH):
        grad[:, a * GW : (a + 1) * GW] = split_dot(tall[a * BLOCK : (a + 1) * BLOCK, :], table)


def mlp_kernel(
    length, normed_two, hidden_own, w_up, w_down, tap_all, conv_x, cot,
    slope, act, out_own, field, conv_all, grad_own,
    out_c, out_x, in_c, in_x, mine, tall, local, send, recv,
):
    p = Peers()
    links = Links(send, recv)
    p.greet(2)
    quarter = lax.rem(p.dp, 4)
    pair = quarter - lax.rem(quarter, 2)
    keep = pltpu.make_async_copy(conv_x, conv_all.at[quarter], local.at[0])
    keep.start()
    swap = links.copy(conv_x, conv_all.at[quarter], (p.mate(0), p.t))
    swap.start()

    def part(owner):
        rows = pl.ds(pl.multiple_of(owner * PART, 16), PART)
        activation, steep = gelu_and_slope(dot(normed_two[rows, :], w_up[...]))
        activation = activation.astype(BF16)
        slope[rows, :] = steep.astype(BF16)
        act[rows, :] = activation
        return dot(activation, w_down[...])

    sums = Scatter(links, p, out_c, out_x, in_c, in_x, mine)
    sums.far(part)
    keep.wait()
    swap.wait_recv()
    pairs = conv_all.at[pl.ds(pair, 2)]
    trade = links.copy(pairs, pairs, (p.mate(1), p.t))
    trade.start()
    sums.near(part)
    lower(cot, grad_own, tall, upsample_table(GW).astype(BF16))
    gathers = []
    for at, piece in enumerate(PIECES):
        total = sums.piece(at)
        off = pl.multiple_of(p.t * PART + piece[0], 16)
        mask = cell_mask((piece[1], D), 0, off, length[0])
        out = (mask * (hidden_own[pl.ds(*piece), :] + total)).astype(BF16)
        out_own[pl.ds(*piece), :] = out
        field[pl.ds(off, piece[1]), :] = dot(out, tap_all[...], (1, 1)).astype(BF16)
        g = Gather(links, p, lambda t: piece_at(field, t, piece))
        g.start()
        gathers.append(g)
    for g in gathers:
        g.forward()
    for g in gathers:
        g.finish()
    sums.finish()
    swap.wait_send()
    trade.wait_recv()
    trade.wait_send()


def mlp_call(*args):
    outs = [
        ((ROWS, D), BF16),
        ((ROWS, D), BF16),
        ((PART, D), BF16),
        ((ROWS, CH), BF16),
        ((4, WIDE, CH), BF16),
        ((BLOCK, LANES), F32),
    ]
    scratch = scatter_scratch() + [
        pltpu.VMEM((GH * BLOCK, 2 * GW), F32),
        pltpu.SemaphoreType.DMA((1,)),
    ] + sems(12)
    return call(mlp_kernel, outs, [smem] + [vmem] * 7, scratch, 1, 4_000_000_000, args)


def scatter_scratch():
    return [
        pltpu.VMEM((2, PART, D), BF16),
        pltpu.VMEM((PART, D), BF16),
        pltpu.VMEM((2, PART, D), BF16),
        pltpu.VMEM((PART, D), BF16),
        pltpu.VMEM((PART, D), F32),
    ]


def conv_kernel(
    length, field, w_own, w_far, grad_own, out_own,
    result, tap_grad, g_conv, out_all,
    start_all, state, steep_first, steep_state, x_all, wide, flip, dcol, back, grad, grad_far,
    grad_near, back_out, back_in, arrive, send, recv,
):
    p = Peers()
    links = Links(send, recv)
    p.greet(3)
    weights = (w_own, w_far)
    block_of = (p.t, p.xp)
    at = lambda t: pl.ds(pl.multiple_of(t * BLOCK, BLOCK), BLOCK)

    part_at(out_all, p.t)[...] = out_own[...]
    out_all[ROWS:, :] = jnp.zeros((LANES - ROWS, D), BF16)
    g_out = Gather(links, p, lambda t: part_at(out_all, t))
    grad_near[...] = grad_own[...].astype(BF16)
    c_grad = links.copy(grad_near, grad_far, (p.dp, p.xp))
    c_grad.start()
    g_out.start()
    halvers = {
        j: Halver(links, p, Clock(), g_conv.at[j], arrive.at[j], None, ORDERS[j]) for j in (3, 2, 1)
    }

    def masks(count):
        _, col = grid_place((count, LANES), 1, 0)
        not_first = jnp.where(col > 0.5, 1.0, 0.0)
        not_last = jnp.where(col < GW - 1.5, 1.0, 0.0)
        return cell_mask((count, LANES), 1, 0, length[0]), not_first, not_last

    _, not_first8, not_last8 = masks(8)
    cells16, not_first16, not_last16 = masks(16)

    start_all[:, ROWS:] = jnp.zeros((CH, LANES - ROWS), F32)
    start_all[:, 0:ROWS] = field[...].astype(F32).T

    def rows_at(i):
        return pl.ds(pl.multiple_of(i * 16, 16), 16)

    def into_at(b, i):
        return pl.ds(pl.multiple_of(block_of[b] * BLOCK + i * 16, 16), 16)

    def open_rows(i, carry):
        x_all[0, rows_at(i), :] = gelu(start_all[rows_at(i), :]).astype(BF16)
        return carry

    lax.fori_loop(0, CH // 16, open_rows, 0)

    def convolve(index, b, use):
        for c in range(LANES // CHUNK):
            lanes = slice(c * CHUNK, (c + 1) * CHUNK)
            wide[:, lanes] = dot(weights[b][index], x_all[index, :, lanes])

        def rows16(i, carry):
            halves = []
            for half in range(2):
                total = None
                for q in range(3):
                    tap = lambda r: wide[
                        pl.ds(pl.multiple_of((r * 3 + q) * BLOCK + i * 16 + half * 8, 8), 8), :
                    ]
                    three = (
                        tap(1)
                        + pltpu.roll(tap(0), GW, 1)
                        + pltpu.roll(tap(2), LANES - GW, 1)
                    )
                    if q == 0:
                        three = pltpu.roll(three, 1, 1) * not_first8
                    if q == 2:
                        three = pltpu.roll(three, LANES - 1, 1) * not_last8
                    total = three if total is None else total + three
                halves.append(total)
            use(i, cells16 * jnp.concatenate(halves, axis=0))
            return carry

        lax.fori_loop(0, BLOCK // 16, rows16, 0)

    def share(index):
        copies = [
            links.copy(x_all.at[index, at(t), :], x_all.at[index, at(t), :], (p.dp, p.sib))
            for t in block_of
        ]
        for c in copies:
            c.start()
        return copies

    def settle(copies):
        for c in copies:
            c.wait_recv()

    pending = []
    for unit in range(2):
        for b in range(2):
            def use_first(i, value, b=b):
                low, steep = gelu_and_slope(value)
                x_all[2 * unit + 1, into_at(b, i), :] = low.astype(BF16)
                steep_first[unit, b, rows_at(i), :] = steep

            convolve(2 * unit, b, use_first)
        copies = share(2 * unit + 1)
        pending += copies
        if unit == 0:
            g_out.forward()
            for b in range(2):
                def opening(i, carry, b=b):
                    value = start_all[into_at(b, i), :]
                    state[b, rows_at(i), :] = value
                    steep_state[0, b, rows_at(i), :] = gelu_and_slope(value)[1]
                    return carry

                lax.fori_loop(0, BLOCK // 16, opening, 0)
        settle(copies)
        for b in range(2 - unit):
            def use_second(i, value, b=b):
                fresh = state[b, rows_at(i), :] + value
                if unit == 0:
                    low, steep = gelu_and_slope(fresh)
                    state[b, rows_at(i), :] = fresh
                    x_all[2, into_at(b, i), :] = low.astype(BF16)
                    steep_state[1, b, rows_at(i), :] = steep
                else:
                    result[rows_at(i), :] = fresh

            convolve(2 * unit + 1, b, use_second)
        if unit == 0:
            copies = share(2)
            pending += copies
            settle(copies)

    c_grad.wait_recv()
    grad[0] = grad_own[...]
    grad[1] = grad_far[...].astype(F32)

    def spread(b, value_of):
        def rows16(i, carry):
            value = value_of(rows_at(i)).astype(BF16).astype(F32)
            for q in range(3):
                side = value
                if q == 0:
                    side = pltpu.roll(value, LANES - 1, 1) * not_last16
                if q == 2:
                    side = pltpu.roll(value, 1, 1) * not_first16
                for r in range(3):
                    moved = side
                    if r == 0:
                        moved = pltpu.roll(side, LANES - GW, 1)
                    if r == 2:
                        moved = pltpu.roll(side, GW, 1)
                    into = pl.ds(pl.multiple_of((r * 3 + q) * BLOCK + i * 16, 16), 16)
                    dcol[b, into, :] = moved.astype(BF16)
            return carry

        lax.fori_loop(0, BLOCK // 16, rows16, 0)

    def conv_back(index, turn, between):
        flip[0] = w_own[index].T
        flip[1] = w_far[index].T
        for c in range(LANES // CHUNK):
            lanes = slice(c * CHUNK, (c + 1) * CHUNK)
            back[:, lanes] = dot(flip[0], dcol[0, :, lanes]) + dot(flip[1], dcol[1, :, lanes])
        copies = []
        for b, t in enumerate((p.sib, p.diag)):
            back_out[turn, b] = back[at(t), :].astype(BF16)
            c = links.copy(back_out.at[turn, b], back_in.at[turn, b], (p.dp, p.sib))
            c.start()
            copies.append(c)
        weight_grad = dot(dcol[0], x_all[index], (1, 1)).astype(BF16)
        g_conv[index, 0:WIDE, :] = weight_grad[:, 0:SLOT]
        g_conv[index, WIDE:, :] = weight_grad[:, SLOT:]
        between()
        for c in copies:
            c.wait_recv()
        pending.extend(copies)

        def value(b, rows):
            far = pl.ds(pl.multiple_of(block_of[b] * BLOCK + rows.start, 16), 16)
            return back[far, :] + back_in[turn, b, rows, :].astype(F32)

        return value

    def between(turn):
        def act():
            if turn == 0:
                halvers[3].s(0)
            if turn == 1:
                halvers[3].a(0)
                halvers[3].s(1)
                halvers[2].s(0)
            if turn == 2:
                halvers[3].a(1)
                halvers[3].s(2)
                halvers[2].a(0)
                halvers[2].s(1)
                halvers[1].s(0)

        return act

    inside16 = jnp.where(
        lax.broadcasted_iota(jnp.int32, (16, LANES), 1) < SLOTS, 1.0, 0.0
    )
    for turn, unit in enumerate((1, 0)):
        for b in range(2):
            spread(b, lambda rows, b=b: cells16 * grad[b, rows, :])
        d_mid = conv_back(2 * unit + 1, 2 * turn, between(2 * turn))
        for b in range(2):
            spread(
                b,
                lambda rows, b=b: cells16 * d_mid(b, rows) * steep_first[unit, b, rows, :],
            )
        d_in = conv_back(2 * unit, 2 * turn + 1, between(2 * turn + 1))
        for b in range(2):
            def renew(i, carry, b=b):
                rows = rows_at(i)
                fresh = grad[b, rows, :] + d_in(b, rows) * steep_state[unit, b, rows, :]
                if unit == 1:
                    grad[b, rows, :] = fresh
                else:
                    tap_grad[into_at(b, i), :] = (inside16 * fresh).astype(BF16)
                return carry

            lax.fori_loop(0, BLOCK // 16, renew, 0)
    copies = [
        links.copy(tap_grad.at[at(t), :], tap_grad.at[at(t), :], (p.dp, p.sib))
        for t in block_of
    ]
    for c in copies:
        c.start()
    halvers[3].a(2)
    halvers[2].a(1)
    halvers[1].a(0)
    settle(copies)
    for c in pending + copies + [c_grad]:
        c.wait_send()
    for h in halvers.values():
        h.finish()
    g_out.finish()


FLAT = (2 * WIDE, SLOT)
ORDERS = ((0, 1, 2), (1, 0, 2), (0, 1, 2), (1, 0, 2))


def conv_call(bits, *args):
    outs = [
        ((BLOCK, LANES), F32),
        ((CH, LANES), BF16),
        ((4,) + FLAT, BF16),
        ((LANES, D), BF16),
    ]
    scratch = [
        pltpu.VMEM((CH, LANES), F32),
        pltpu.VMEM((2, BLOCK, LANES), F32),
        pltpu.VMEM((2, 2, BLOCK, LANES), F32),
        pltpu.VMEM((2, 2, BLOCK, LANES), F32),
        pltpu.VMEM((4, CH, LANES), BF16),
        pltpu.VMEM((WIDE, LANES), F32),
        pltpu.VMEM((2, CH, WIDE), BF16),
        pltpu.VMEM((2, WIDE, LANES), BF16),
        pltpu.VMEM((CH, LANES), F32),
        pltpu.VMEM((2, BLOCK, LANES), F32),
        pltpu.VMEM((BLOCK, LANES), BF16),
        pltpu.VMEM((BLOCK, LANES), BF16),
        pltpu.VMEM((4, 2, BLOCK, LANES), BF16),
        pltpu.VMEM((4, 2, BLOCK, LANES), BF16),
        pltpu.VMEM((4,) + landing(*FLAT, bits).shape, BF16),
    ] + sems(40)
    return call(conv_kernel, outs, [smem] + [vmem] * 5, scratch, 2, 9_000_000_000, args)


def lift(field, joined, table, grid_rows):
    for a in grid_rows:
        here = field[:, a * GW : (a + 1) * GW]
        up, down = max(a - 1, 0), min(a + 1, GH - 1)
        for side, other in enumerate((up, down)):
            line = 0.75 * here + 0.25 * field[:, other * GW : (other + 1) * GW]
            joined[2 * a + side] = split_dot(line, table).astype(BF16)


def back_kernel(
    length, tap_grad, tap_all, cot_hbm, slope, act, normed_two, w_up, w_down, hidden_own, gain_two,
    out_all, field, conv_hbm,
    w_out, mixed, q_cm, k_tm, v_tm, k_cm, lse, normed_one, w_qkv, tok_hbm, gain_one,
    joined, grad_tok, conv, up, down, ot, head, gain_sum,
    tok, tap_tm, d_mlp, d_pre, mine_block, grad_hidden, branch, out_c, out_x, in_c, in_x, mine,
    conv_part, up_part, down_part, ot_part, head_part,
    conv_arrive, up_arrive, down_arrive, ot_arrive, head_arrive, gain_out, gain_arrive,
    d_mix, acc_k, acc_v, d_cm, d_tm, w_by_head, local, send, recv,
):
    p = Peers()
    links = Links(send, recv)
    clock = Clock()
    bring_conv = pltpu.make_async_copy(conv_hbm, conv_part, local.at[1])
    bring_conv.start()
    bring = pltpu.make_async_copy(cot_hbm, tok.at[pl.ds(0, SLOTS), :], local.at[0])
    bring.start()
    tok[SLOTS:, :] = jnp.zeros((ROWS - SLOTS, D), BF16)
    bring_conv.wait()
    p.greet(p.bits())

    def halver(array, arrive, result, order=(0, 1, 2), after=0):
        made = Halver(links, p, clock, array, arrive, result, order, after)
        halvers.append(made)
        return made

    halvers = []
    for j in (3, 2, 1, 0):
        halver(conv_part.at[j], conv_arrive.at[j], conv.at[j], ORDERS[j], j).step()
    half = D // 2
    h_up = [
        halver(up_part.at[i], up_arrive.at[i], up.at[i], ((0, 1, 2), (1, 0, 2))[i])
        for i in range(2)
    ]
    h_down = [
        halver(down_part.at[i], down_arrive.at[i], down.at[i], ((0, 1, 2), (1, 0, 2))[i])
        for i in range(2)
    ]
    h_ot = halver(ot_part, ot_arrive, ot, (1, 0, 2))
    h_head = [
        halver(head_part.at[h], head_arrive.at[h], head.at[h], ((0, 1, 2), (1, 0, 2), (0, 1, 2))[h])
        for h in range(3)
    ]
    gains = Doubler(links, p, gain_out, gain_arrive)

    tap_tm[...] = tap_grad[...].T
    bring.wait()

    def part(owner):
        off = pl.multiple_of(owner * PART, 16)
        rows = pl.ds(off, PART)
        block = cell_mask((PART, D), 0, off, length[0]) * (
            tok[rows, :].astype(F32) + dot(tap_tm[rows, :], tap_all[...])
        )
        mine_block[...] = block
        low = block.astype(BF16)
        d_mlp[rows, :] = low
        steep = (dot(low, w_down[...], (1, 1)) * slope[rows, :].astype(F32)).astype(BF16)
        d_pre[rows, :] = steep
        return dot(steep, w_up[...], (1, 1))

    sums = Scatter(links, p, out_c, out_x, in_c, in_x, mine)
    sums.far(part)
    clock.work(5.0)
    sums.near(part)
    clock.work(5.0)
    for i in range(2):
        cols = slice(i * half, (i + 1) * half)
        up_part[i] = dot(normed_two[0:ROWS, cols], d_pre[...], (0, 0)).astype(BF16)
        h_up[i].step()
        clock.work(1.2)
    for i in range(2):
        cols = slice(i * half, (i + 1) * half)
        down_part[i] = dot(act[:, cols], d_mlp[...], (0, 0)).astype(BF16)
        h_down[i].step()
        clock.work(1.2)
    gain = gain_two[...].reshape(1, D)
    gathers = []
    gain_part_two = jnp.zeros((1, D), F32)
    for at, piece in enumerate(PIECES):
        rows = pl.ds(*piece)
        total = sums.piece(at)
        clock.now = max(clock.now, (14.0, 19.0)[at])
        scaled, inverse = norm(hidden_own[rows, :])
        inner, add = norm_back(total, scaled, inverse, gain)
        after = mine_block[rows, :] + inner
        grad_hidden[rows, :] = after
        gain_part_two = gain_part_two + add
        branch[pl.ds(pl.multiple_of(p.t * PART + piece[0], 16), piece[1]), :] = after.astype(BF16)
        g = Gather(links, p, lambda t: piece_at(branch, t, piece))
        g.start(clock, piece[1] * D * 2)
        gathers.append(g)
        clock.work(1.0)
    sums.finish()
    bring = pltpu.make_async_copy(tok_hbm, tok.at[pl.ds(0, SLOTS), :], local.at[0])
    bring.start()
    table = upsample_table(GW).T.astype(BF16)
    for quarter in range(5):
        lift(field, joined, table, range(quarter * 6, quarter * 6 + 6))
        clock.work(0.6)
    ot_part[192:, :] = dot(
        tap_grad[pl.ds(pl.multiple_of(p.t * BLOCK, BLOCK), BLOCK), :], out_all[...]
    ).astype(BF16)
    for h in range(3):
        for part_at_ in range(3):
            w_by_head[h * 192 + part_at_ * 64 : h * 192 + part_at_ * 64 + 64, :] = w_qkv[
                part_at_ * 192 + h * 64 : part_at_ * 192 + h * 64 + 64, :
            ]
    d_mix[:, ROWS:] = jnp.zeros((192, LANES - ROWS), BF16)
    d_cm[:, ROWS:] = jnp.zeros((3 * 192, LANES - ROWS), BF16)
    clock.work(1.0)
    while any(act.__self__ in gathers for _, _, act in clock.queue if hasattr(act, "__self__")):
        clock.work(0.5)
    for g in gathers:
        g.finish()
    clock.work(1.0)
    ot_part[0:192, :] = dot(mixed[:, 0:ROWS], branch[...]).astype(BF16)
    h_ot.step()
    d_mix[:, 0:ROWS] = dot(w_out[...], branch[...], (1, 1)).astype(BF16)
    clock.work(1.5)
    for h in range(3):
        heads = slice(h * HEAD_DIM, (h + 1) * HEAD_DIM)
        for c in range(LANES // CHUNK):
            lanes = slice(c * CHUNK, (c + 1) * CHUNK)
            dm = d_mix[heads, lanes]
            inner = jnp.sum(
                dm.astype(F32) * mixed[heads, lanes].astype(F32), axis=0, keepdims=True
            )
            probs = jnp.exp(
                dot(k_tm[h, 0:ROWS, :], q_cm[h, :, lanes]) - lse[h : h + 1, lanes]
            )
            d_probs = dot(v_tm[h, 0:ROWS, :], dm)
            d_raw = (probs * (d_probs - inner)).astype(BF16)
            d_v = dot(probs.astype(BF16), dm, (1, 1))
            d_k = dot(d_raw, q_cm[h, 0:HEAD_DIM, lanes], (1, 1))
            acc_v[...] = d_v if c == 0 else acc_v[...] + d_v
            acc_k[...] = d_k if c == 0 else acc_k[...] + d_k
            d_q = dot(k_cm[heads, 0:ROWS], d_raw) * 0.125
            d_cm[h * 192 : h * 192 + 64, lanes] = d_q.astype(BF16)
            clock.work(1.6)
        d_cm[h * 192 + 64 : h * 192 + 128, 0:ROWS] = acc_k[...].T.astype(BF16)
        d_cm[h * 192 + 128 : h * 192 + 192, 0:ROWS] = acc_v[...].T.astype(BF16)
        three = dot(d_cm[h * 192 : (h + 1) * 192, :], normed_one[...]).astype(BF16)
        head_part[h, 0:192, :] = three[:, 0:384]
        head_part[h, 192:, :] = three[:, 384:]
        h_head[h].step()
        clock.work(1.0)
    d_tm[...] = d_cm[...].T
    bring.wait()

    def part_two(owner):
        rows = pl.ds(pl.multiple_of(owner * PART, 16), PART)
        return dot(d_tm[rows, :], w_by_head[...])

    sums = Scatter(links, p, out_c, out_x, in_c, in_x, mine)
    sums.far(part_two)
    clock.work(2.0)
    sums.near(part_two)
    clock.work(2.0)
    began = clock.now
    gain = gain_one[...].reshape(1, D)
    gathers = []
    gain_part = jnp.zeros((1, D), F32)
    for at, piece in enumerate(PIECES):
        while clock.now < began + (4.0, 9.0)[at]:
            clock.work(1.0)
        rows = pl.ds(*piece)
        place = pl.ds(pl.multiple_of(p.t * PART + piece[0], 16), piece[1])
        total = sums.piece(at)
        scaled, inverse = norm(tok[place, :].astype(F32))
        inner, add = norm_back(total, scaled, inverse, gain)
        gain_part = gain_part + add
        grad_tok[place, :] = (grad_hidden[rows, :] + inner).astype(BF16)
        g = Gather(links, p, lambda t: piece_at(grad_tok, t, piece))
        g.start(clock, piece[1] * D * 2)
        gathers.append(g)
        clock.work(1.0)
    row = lax.broadcasted_iota(jnp.int32, (8, D), 0)
    gains.start(jnp.where(row == 0, gain_part, 0.0) + jnp.where(row == 1, gain_part_two, 0.0))

    def turn():
        gains.step()
        if len(gains.copies) < len(gains.to):
            clock.later(clock.now + 3.0, turn)

    clock.later(clock.now + 3.0, turn)
    clock.drain()
    gain_sum[...] = gains.finish()
    for g in gathers:
        g.finish()
    sums.finish()
    for h in halvers:
        h.finish()


def back_call(bits, *args):
    outs = [
        ((2 * GH, BLOCK, 2 * GW), BF16),
        ((ROWS, D), BF16),
        ((4,) + FLAT, BF16),
        ((2, D // 2, D), BF16),
        ((2, D // 2, D), BF16),
        ((256, D), BF16),
        ((3, 384, 384), BF16),
        ((8, D), F32),
    ]
    room = lambda lead, rows, columns: pltpu.VMEM(
        lead + landing(rows, columns, bits).shape, BF16
    )
    scratch = [
        pltpu.VMEM((ROWS, D), BF16),
        pltpu.VMEM((LANES, CH), BF16),
        pltpu.VMEM((ROWS, D), BF16),
        pltpu.VMEM((ROWS, D), BF16),
        pltpu.VMEM((PART, D), F32),
        pltpu.VMEM((PART, D), F32),
        pltpu.VMEM((ROWS, D), BF16),
    ] + scatter_scratch() + [
        pltpu.VMEM((4,) + FLAT, BF16),
        pltpu.VMEM((2, D // 2, D), BF16),
        pltpu.VMEM((2, D // 2, D), BF16),
        pltpu.VMEM((256, D), BF16),
        pltpu.VMEM((3, 384, 384), BF16),
        room((4,), *FLAT),
        room((2,), D // 2, D),
        room((2,), D // 2, D),
        room((), 256, D),
        room((3,), 384, 384),
        pltpu.VMEM((2 + bits, 8, D), F32),
        pltpu.VMEM((2 + bits, 8, D), F32),
        pltpu.VMEM((192, LANES), BF16),
        pltpu.VMEM((ROWS, HEAD_DIM), F32),
        pltpu.VMEM((ROWS, HEAD_DIM), F32),
        pltpu.VMEM((3 * 192, LANES), BF16),
        pltpu.VMEM((LANES, 3 * 192), BF16),
        pltpu.VMEM((3 * 192, D), BF16),
        pltpu.SemaphoreType.DMA((2,)),
    ] + sems(130)
    return call(
        back_kernel, outs,
        [smem, vmem, vmem, anywhere] + [vmem] * 9 + [anywhere] + [vmem] * 9 + [anywhere, vmem],
        scratch, 3, 20_000_000_000, args,
    )


def write_kernel(
    out_all, grad_tok, conv, up, down, ot, head,
    out_tokens, grad_tokens, conv_sum, up_sum, down_sum, out_sum, tap_sum, qkv_sum,
):
    out_tokens[...] = out_all[0:SLOTS, :]
    grad_tokens[...] = grad_tok[0:SLOTS, :]
    for j in range(4):
        for side in range(2):
            conv_sum[j, :, side * SLOT : (side + 1) * SLOT] = conv[
                j, side * WIDE : (side + 1) * WIDE, :
            ].astype(F32)
    for i in range(2):
        rows = slice(i * (D // 2), (i + 1) * (D // 2))
        up_sum[rows, :] = up[i].astype(F32)
        down_sum[rows, :] = down[i].astype(F32)
    out_sum[...] = ot[0:192, :].astype(F32)
    tap_sum[...] = ot[192:, :].astype(F32)
    for h in range(3):
        for part in range(3):
            for side in range(2):
                rows = side * 192 + part * 64
                qkv_sum[
                    part * 192 + h * 64 : part * 192 + h * 64 + 64, side * 384 : (side + 1) * 384
                ] = head[h, rows : rows + 64, :].astype(F32)


def write_call(*args):
    outs = [
        ((SLOTS, D), BF16),
        ((SLOTS, D), BF16),
        ((4, WIDE, CH), F32),
        ((D, D), F32),
        ((D, D), F32),
        ((192, D), F32),
        ((BLOCK, D), F32),
        ((3 * 192, D), F32),
    ]
    return call(write_kernel, outs, [vmem] * 7, [], None, 1_000_000, args)


def per_device(
    bits, tokens, lengths, gain_one, gain_two, w_qkv, w_out, w_up, w_down, w_tap, w_conv,
    cot_tokens, cot_joined,
):
    w_heads = w_qkv.transpose(0, 2, 1).reshape(3 * 192, D)
    conv_w = w_conv.transpose(0, 1, 2, 4, 3).reshape(4, WIDE, CH)
    (
        hidden_own, normed_two, q_cm, k_tm, v_tm, k_cm, lse, mixed, normed_one, tap_all, conv_x,
    ) = attend_call(lengths, tokens, gain_one, gain_two, w_heads, w_out, w_tap.T, conv_w)
    slope, act, out_own, field, conv_far, grad_own = mlp_call(
        lengths, normed_two, hidden_own, w_up, w_down, tap_all, conv_x,
        cot_joined[0].transpose(0, 2, 1),
    )
    result, tap_grad, g_conv, out_all = conv_call(
        bits, lengths, field, conv_w, conv_far, grad_own, out_own
    )
    joined, grad_tok, conv, up, down, ot, head, gain_sum = back_call(
        bits, lengths, tap_grad, tap_all, cot_tokens, slope, act, normed_two, w_up, w_down,
        hidden_own, gain_two, out_all, result, g_conv,
        w_out, mixed, q_cm, k_tm, v_tm, k_cm, lse, normed_one, w_heads, tokens, gain_one,
    )
    (
        out_tokens, grad_tokens, conv_sum, up_sum, down_sum, out_sum, tap_sum, qkv_sum,
    ) = write_call(out_all, grad_tok, conv, up, down, ot, head)
    return (
        out_tokens,
        joined.transpose(0, 2, 1)[None],
        grad_tokens,
        qkv_sum.reshape(3, 192, D).transpose(0, 2, 1),
        out_sum,
        up_sum,
        down_sum,
        tap_sum.T,
        conv_sum.reshape(4, 3, 3, BLOCK, CH).transpose(0, 1, 2, 4, 3),
        gain_sum[0],
        gain_sum[1],
    )


def solution(mesh):
    placed = (
        P("dp", None),
        P("dp"),
        P(),
        P(),
        P(None, None, "tensor"),
        P("tensor", None),
        P(None, "tensor"),
        P("tensor", None),
        P(None, "tensor"),
        P(None, None, None, None, "tensor"),
        P("dp", None),
        P("dp", None, None, "tensor"),
    )
    return jax.shard_map(
        functools.partial(per_device, mesh.shape["dp"].bit_length() - 1),
        mesh=mesh,
        in_specs=placed,
        out_specs=(
            P("dp", None),
            P("dp", None, None, "tensor"),
            P("dp", None),
            P(None, None, "tensor"),
            P("tensor", None),
            P(None, "tensor"),
            P("tensor", None),
            P(None, "tensor"),
            P(None, None, None, None, "tensor"),
            P(),
            P(),
        ),
        check_vma=False,
    )
```

```python
import functools

import jax
import jax.numpy as jnp
from jax import lax
from jax.experimental import pallas as pl
from jax.experimental.pallas import tpu as pltpu
from jax.sharding import PartitionSpec as P

HEAD_DIM = 64
GH = 30
GW = 40
SH = 24
SW = 24
SLOTS = GH * GW
D = 768
CH = 256
BLOCK = 64
TAPS = 9
WIDE = TAPS * BLOCK
PART = 304
ROWS = 4 * PART
LANES = 1280
CHUNK = 256
SLOT = 128
F32 = jnp.float32
BF16 = jnp.bfloat16
MESH = pl.DeviceIdType.MESH
VMEM_LIMIT = 60 * 2**20

vmem = pl.BlockSpec(memory_space=pltpu.VMEM)
smem = pl.BlockSpec(memory_space=pltpu.SMEM)
anywhere = pl.BlockSpec(memory_space=pl.ANY)


def dot(a, b, dims=(1, 0)):
    return lax.dot_general(
        a, b, (((dims[0],), (dims[1],)), ((), ())), preferred_element_type=F32
    )


def gelu(v):
    return 0.5 * v * (1.0 + lax.erf(v * 0.7071067811865476))


def gelu_and_slope(v):
    share = 0.5 * (1.0 + lax.erf(v * 0.7071067811865476))
    return v * share, share + v * jnp.exp(-0.5 * v * v) * 0.3989422804014327


def norm(v):
    centred = v - jnp.mean(v, axis=-1, keepdims=True)
    spread = jnp.mean(centred * centred, axis=-1, keepdims=True)
    inverse = lax.rsqrt(spread + 1e-06)
    return centred * inverse, inverse


def norm_back(incoming, scaled, inverse, gain):
    weighted = incoming * gain
    inner = (
        weighted
        - jnp.mean(weighted, axis=-1, keepdims=True)
        - scaled * jnp.mean(weighted * scaled, axis=-1, keepdims=True)
    )
    return inverse * inner, jnp.sum(incoming * scaled, axis=0, keepdims=True)


def grid_place(shape, axis, offset):
    index = (lax.broadcasted_iota(jnp.int32, shape, axis) + offset).astype(F32)
    row = jnp.floor((index + 0.5) * (1.0 / GW))
    return row, index - GW * row


def cell_mask(shape, axis, offset, length):
    row, col = grid_place(shape, axis, offset)
    large = length == SLOTS
    height = jnp.where(large, float(GH), float(SH))
    breadth = jnp.where(large, float(GW), float(SW))
    return jnp.where((row < height) & (col < breadth), 1.0, 0.0)


class Peers:
    def __init__(self):
        self.dp = lax.axis_index("dp")
        self.n = lax.axis_size("dp")
        self.t = lax.axis_index("tensor")
        self.sib = self.t + 1 - 2 * lax.rem(self.t, 2)
        self.xp = lax.rem(self.t + 2, 4)
        self.diag = lax.rem(self.sib + 2, 4)

    def bit(self, at):
        return lax.rem(self.dp // (1 << at), 2)

    def mate(self, at):
        return self.dp + (1 - 2 * self.bit(at)) * (1 << at)

    def bits(self):
        return self.n.bit_length() - 1

    def greet(self, bits=0):
        barrier = pltpu.get_barrier_semaphore()
        others = [(self.dp, self.sib), (self.dp, self.xp)]
        if bits >= 3:
            low = lax.rem(self.dp, 8)
            others += [
                (self.dp + lax.rem(low + k, 8) - low, self.t) for k in range(1, 8)
            ]
            bits_from = 3
        else:
            bits_from = 0
        others += [(self.mate(at), self.t) for at in range(bits_from, bits)]
        for other in others:
            pl.semaphore_signal(barrier, inc=1, device_id=other, device_id_type=MESH)
        pl.semaphore_wait(barrier, len(others))


class Links:
    def __init__(self, send, recv):
        self.send, self.recv, self.used = send, recv, 0

    def copy(self, src, dst, device):
        at = self.used
        self.used += 1
        return pltpu.make_async_remote_copy(
            src_ref=src,
            dst_ref=dst,
            send_sem=self.send.at[at],
            recv_sem=self.recv.at[at],
            device_id=device,
            device_id_type=MESH,
        )


class Gather:
    def __init__(self, links, peers, place):
        p = peers
        self.x = links.copy(place(p.t), place(p.t), (p.dp, p.xp))
        self.c = links.copy(place(p.t), place(p.t), (p.dp, p.sib))
        self.f = links.copy(place(p.xp), place(p.xp), (p.dp, p.sib))

    def start(self, clock=None, size=0):
        self.x.start()
        self.c.start()
        if clock is not None:
            clock.later(clock.flight("x", size), self.forward)

    def forward(self):
        self.x.wait_recv()
        self.f.start()

    def finish(self):
        self.c.wait_recv()
        self.f.wait_recv()
        self.x.wait_send()
        self.c.wait_send()
        self.f.wait_send()


PIECES = ((0, 160), (160, PART - 160))


class Scatter:
    def __init__(self, links, peers, out_c, out_x, in_c, in_x, mine):
        p = peers
        self.p, self.out_c, self.out_x, self.in_c, self.in_x = p, out_c, out_x, in_c, in_x
        self.mine = mine
        self.c = [links.copy(out_c.at[i], in_c.at[i], (p.dp, p.sib)) for i in range(2)]
        self.x = [
            links.copy(out_x.at[pl.ds(*piece), :], in_x.at[pl.ds(*piece), :], (p.dp, p.xp))
            for piece in PIECES
        ]

    def far(self, part, clock=None, cost=0.0):
        p = self.p
        self.lands = []
        self.out_c[0] = part(p.diag).astype(BF16)
        self.c[0].start()
        self.mine[...] = part(p.xp)
        if clock is not None:
            clock.work(cost)
            clock.until(clock.flight("core", PART * D * 2))
        self.c[0].wait_recv()
        for copy, piece in zip(self.x, PIECES):
            rows = pl.ds(*piece)
            self.out_x[rows, :] = (self.mine[rows, :] + self.in_c[0, rows, :].astype(F32)).astype(
                BF16
            )
            copy.start()
            if clock is not None:
                self.lands.append(clock.flight("x", piece[1] * D * 2))

    def near(self, part, clock=None, cost=0.0):
        p = self.p
        self.out_c[1] = part(p.sib).astype(BF16)
        self.c[1].start()
        self.mine[...] = part(p.t)
        if clock is not None:
            clock.work(cost)
            clock.until(clock.flight("core", PART * D * 2))
        self.c[1].wait_recv()
        self.mine[...] += self.in_c[1].astype(F32)

    def piece(self, at, clock=None):
        rows = pl.ds(*PIECES[at])
        if clock is not None:
            clock.until(self.lands[at])
        self.x[at].wait_recv()
        return self.mine[rows, :] + self.in_x[rows, :].astype(F32)

    def finish(self):
        for copy in self.c + self.x:
            copy.wait_send()


class Clock:
    RATES = {"core": 400e3, "zz": 23e3, "z4": 11.6e3, "all": 5.8e3}

    def __init__(self):
        self.now, self.free, self.queue, self.count = 0.0, {}, [], 0

    def flight(self, axis, size):
        took = size / self.RATES.get(axis, 46e3)
        lines = {"zz": ("zz", "z"), "z4": ("z", "zz"), "all": ("y", "z", "zz")}.get(axis, (axis,))
        start = max(self.now, self.free.get(lines[0], 0.0))
        for line in lines:
            part = 0.5 * took if (axis, line) in (("zz", "z"), ("all", "y")) else took
            self.free[line] = max(self.now, self.free.get(line, 0.0)) + part
        return start + took + (1.0 if axis == "core" else 4.0)

    def later(self, when, act):
        self.queue.append((when, self.count, act))
        self.count += 1

    def work(self, took):
        self.now += took
        while self.queue and min(self.queue)[0] <= self.now:
            first = min(self.queue)
            self.queue.remove(first)
            first[2]()

    def until(self, when):
        while self.queue and min(self.queue)[0] <= when:
            self.work(max(min(self.queue)[0] - self.now, 0.0))
        self.now = max(self.now, when)

    def drain(self):
        while self.queue:
            self.work(max(min(self.queue)[0] - self.now, 0.0))


Y, Z, ZZ, Z4, ALL = ("y", 0, 2), ("z", 1, 2), ("zz", 2, 2), ("z4", 1, 4), ("all", 0, 8)


class Halver:
    def __init__(self, links, peers, clock, array, arrive, result, stages, after=0):
        p = self.p = peers
        self.links, self.clock, self.array, self.arrive = links, clock, array, arrive
        self.result, self.stages = result, stages
        self.rows, self.columns = array.shape
        self.at = self.fresh = after
        base, size, slot = 0, self.rows, 0
        self.keep, self.give, self.land, self.to = [], [], [], []
        for _, low, count in stages:
            size //= count
            mine = lax.rem(p.dp // (1 << low), count)
            give, land, to = [], [], []
            for k in range(1, count):
                other = lax.rem(mine + k, count)
                give.append(pl.ds(pl.multiple_of(base + other * size, 16), size))
                land.append(pl.ds(slot, size))
                to.append((p.dp + (other - mine) * (1 << low), p.t))
                slot += size
            base = base + mine * size
            self.give.append(give)
            self.land.append(land)
            self.to.append(to)
            self.keep.append(pl.ds(pl.multiple_of(base, 16), size))
        self.size, self.slot = size, slot
        self.sent, self.rs, self.ag = [], {}, {}

    def send(self, k, copies):
        for copy in copies:
            copy.start()
        self.sent.extend(copies)
        size = self.keep[k].size * self.columns * 2
        self.clock.later(self.clock.flight(self.stages[k][0], size), self.step)

    def s(self, k):
        self.rs[k] = [
            self.links.copy(self.array.at[give, :], self.arrive.at[land, :], to)
            for give, land, to in zip(self.give[k], self.land[k], self.to[k])
        ]
        self.send(k, self.rs[k])

    def add(self, lands, keep):
        total = self.array[keep, :].astype(F32)
        for land in lands:
            total = total + self.arrive[land, :].astype(F32)
        self.array[keep, :] = total.astype(BF16)

    def a(self, k):
        for copy in self.rs[k]:
            copy.wait_recv()
        self.add(self.land[k], self.keep[k])
        if k == len(self.stages) - 1:
            for extra in range(3, self.p.bits()):
                land = pl.ds(self.slot + (extra - 3) * self.size, self.size)
                copy = self.links.copy(
                    self.array.at[self.keep[k], :], self.arrive.at[land, :],
                    (self.p.mate(extra), self.p.t),
                )
                copy.start()
                copy.wait_recv()
                copy.wait_send()
                self.add([land], self.keep[k])

    def g(self, k):
        region = self.keep[k]
        if k == len(self.stages) - 1:
            self.result[region, :] = self.array[region, :]
        self.ag[k] = [
            self.links.copy(self.result.at[region, :], self.result.at[region, :], to)
            for to in self.to[k]
        ]
        self.send(k, self.ag[k])

    def step(self):
        at, last = self.at, len(self.stages)
        if at <= last:
            if at > self.fresh:
                self.a(at - 1)
                self.fresh = at
            if at < last:
                self.s(at)
            elif self.result is None:
                return
            else:
                self.g(last - 1)
        else:
            k = 2 * last - at
            for copy in self.ag[k].copy():
                copy.wait_recv()
            if k:
                self.g(k - 1)
        self.at += 1

    def done(self):
        return self.at > 2 * len(self.stages)

    def level(self):
        if self.at > self.fresh:
            self.a(self.at - 1)
            self.fresh = self.at
        return self.fresh

    def finish(self):
        for copy in self.sent:
            copy.wait_send()


class Fetch:
    def __init__(self, links, peers, clock, source, place, size, after=None):
        p = self.p = peers
        self.clock, self.size, self.after = clock, size, after
        quarter = lax.rem(p.dp, 4)
        pair = quarter - lax.rem(quarter, 2)
        self.x = links.copy(source(quarter), place(p.t, quarter, 1), (p.dp, p.xp))
        mine = place(p.xp, quarter, 1)
        self.one = links.copy(mine, mine, (p.mate(0), p.t))
        both = place(p.xp, pair, 2)
        self.two = links.copy(both, both, (p.mate(1), p.t))

    def start(self):
        self.x.start()
        self.clock.later(self.clock.flight("x", self.size), self.swap)

    def swap(self):
        self.x.wait_recv()
        self.one.start()
        self.clock.later(self.clock.flight("y", self.size), self.trade)

    def trade(self):
        self.one.wait_recv()
        self.two.start()
        self.clock.later(self.clock.flight("z", 2 * self.size), self.end)

    def end(self):
        self.two.wait_recv()
        if self.after is not None:
            self.after()

    def finish(self):
        self.x.wait_send()
        self.one.wait_send()
        self.two.wait_send()


def landing(rows, columns, bits):
    return pltpu.VMEM((rows + max(bits - 4, 0) * (rows // 8), columns), BF16)


class Doubler:
    def __init__(self, links, peers, outgoing, incoming):
        p = peers
        self.links, self.outgoing, self.incoming = links, outgoing, incoming
        self.to = [(p.dp, p.sib), (p.dp, p.xp)] + [(p.mate(at), p.t) for at in range(p.bits())]
        self.copies = []

    def start(self, value):
        self.value = value
        self.send()

    def send(self):
        at = len(self.copies)
        if at < len(self.to):
            self.outgoing[at] = self.value
            copy = self.links.copy(self.outgoing.at[at], self.incoming.at[at], self.to[at])
            copy.start()
            self.copies.append(copy)

    def step(self):
        at = len(self.copies) - 1
        self.copies[at].wait_recv()
        self.value = self.value + self.incoming[at]
        self.send()

    def finish(self):
        while len(self.copies) < len(self.to):
            self.step()
        self.copies[-1].wait_recv()
        self.value = self.value + self.incoming[len(self.to) - 1]
        for copy in self.copies:
            copy.wait_send()
        return self.value


def sems(count):
    return [pltpu.SemaphoreType.DMA((count,)), pltpu.SemaphoreType.DMA((count,))]


def part_at(ref, owner):
    return ref.at[pl.ds(pl.multiple_of(owner * PART, 16), PART), :]


def piece_at(ref, owner, piece):
    return ref.at[pl.ds(pl.multiple_of(owner * PART + piece[0], 16), piece[1]), :]


def upsample_table(count):
    shape = (2 * count, count)
    target = lax.broadcasted_iota(jnp.int32, shape, 0)
    source = lax.broadcasted_iota(jnp.int32, shape, 1)
    nearest = lax.shift_right_logical(target, 1)
    odd = target - 2 * nearest
    further = jnp.clip(nearest + 2 * odd - 1, 0, count - 1)
    return jnp.where(source == nearest, 0.75, 0.0) + jnp.where(source == further, 0.25, 0.0)


def split_dot(a, table):
    high = a.astype(BF16)
    low = (a - high.astype(F32)).astype(BF16)
    return dot(high, table) + dot(low, table)


def call(kernel, outs, ins, scratch, collective, flops, args, places=None):
    return pl.pallas_call(
        kernel,
        out_shape=[jax.ShapeDtypeStruct(*o) for o in outs],
        in_specs=ins,
        out_specs=places or [vmem] * len(outs),
        scratch_shapes=scratch,
        cost_estimate=pl.CostEstimate(
            flops=flops, bytes_accessed=20_000_000, transcendentals=0
        ),
        compiler_params=pltpu.CompilerParams(
            collective_id=collective,
            has_side_effects=True,
            vmem_limit_bytes=VMEM_LIMIT,
        )
        if collective is not None
        else pltpu.CompilerParams(vmem_limit_bytes=VMEM_LIMIT),
    )(*args)


def front_kernel(
    levels, length, tok_hbm, gain_one, gain_two, w_qkv, w_out, w_tap, w_conv, w_up_hbm, w_down_hbm,
    cot_field_hbm, cot_hbm,
    hidden_own_, normed_two_, q_cm_, k_tm_, v_tm_, k_cm_, lse_, mixed_, normed_one_, slope_, act_,
    tap_all, out_own, field, conv_all, grad_own, down_part,
    hidden_own, normed_two, q_cm, k_tm, v_tm, k_cm, lse, mixed, normed_one, slope, act, down_arrive,
    tok, hidden, mixed_all, out_all, out_heads, v_cm, w_up, w_down, cot_field, cot,
    out_c, out_x, in_c, in_x, mine, tall, local, send, recv,
):
    p = Peers()
    links = Links(send, recv)
    bring = pltpu.make_async_copy(tok_hbm, tok.at[pl.ds(0, SLOTS), :], local.at[0])
    bring.start()
    late = [
        pltpu.make_async_copy(w_up_hbm, w_up, local.at[1]),
        pltpu.make_async_copy(w_down_hbm, w_down, local.at[2]),
        pltpu.make_async_copy(cot_field_hbm, cot_field, local.at[3]),
        pltpu.make_async_copy(cot_hbm, cot.at[pl.ds(0, SLOTS), :], local.at[4]),
    ]
    tok[SLOTS:, :] = jnp.zeros((LANES - SLOTS, D), BF16)
    cot[SLOTS:, :] = jnp.zeros((ROWS - SLOTS, D), BF16)
    place_out = lambda t: out_all.at[pl.ds(pl.multiple_of(t * 192, 64), 192), :]
    place_tap = lambda t: tap_all.at[pl.ds(pl.multiple_of(t * 64, 64), 64), :]
    place_out(p.t)[...] = w_out[...]
    place_tap(p.t)[...] = w_tap[...]
    clock = Clock()
    p.greet(p.bits())
    c_near = [links.copy(place(p.t), place(p.t), (p.dp, p.sib)) for place in (place_out, place_tap)]
    c_far = [links.copy(place(p.xp), place(p.xp), (p.dp, p.sib)) for place in (place_out, place_tap)]
    f_out = Fetch(
        links, p, clock, lambda q: w_out.at[pl.ds(pl.multiple_of(q * 48, 16), 48), :],
        lambda t, q, n: out_all.at[pl.ds(pl.multiple_of(t * 192 + q * 48, 16), n * 48), :],
        48 * D * 2, c_far[0].start,
    )
    f_tap = Fetch(
        links, p, clock, lambda q: w_tap.at[pl.ds(pl.multiple_of(q * 16, 16), 16), :],
        lambda t, q, n: tap_all.at[pl.ds(pl.multiple_of(t * 64 + q * 16, 16), n * 16), :],
        16 * D * 2, c_far[1].start,
    )
    f_conv = Fetch(
        links, p, clock, lambda q: w_conv.at[pl.ds(q, 1)],
        lambda t, q, n: conv_all.at[pl.ds(q, n)], WIDE * CH * 2,
    )
    f_out.start()
    f_tap.start()
    f_conv.start()
    for c in c_near:
        c.start()
    writes = []

    def write(*arrays):
        for src, dst in arrays:
            copy = pltpu.make_async_copy(src, dst, local.at[5 + len(writes)])
            copy.start()
            writes.append(copy)

    bring.wait()
    for copy in late:
        copy.start()
    gain = gain_one[...].reshape(1, D)
    lane = lax.broadcasted_iota(jnp.int32, (CHUNK, SLOT), 1)
    one_row = jnp.where(
        lax.broadcasted_iota(jnp.int32, (HEAD_DIM, CHUNK), 0) == 0, 1.0, 0.0
    ).astype(BF16)

    def project(i, carry):
        off = pl.multiple_of(i * CHUNK, CHUNK)
        rows = pl.ds(off, CHUNK)
        scaled, _ = norm(tok[rows, :].astype(F32))
        normed = (scaled * gain).astype(BF16)
        normed_one[rows, :] = normed
        bias = jnp.where(cell_mask((CHUNK, SLOT), 0, off, length[0]) > 0.5, 0.0, -1e30)
        bias = jnp.where(lane == HEAD_DIM, bias, 0.0).astype(BF16)
        qkv = dot(w_qkv[...], normed, (1, 1)).astype(BF16)
        for h in range(3):
            near = slice(h * HEAD_DIM, (h + 1) * HEAD_DIM)
            q_cm[h, 0:HEAD_DIM, rows] = (qkv[near].astype(F32) * 0.125).astype(BF16)
            q_cm[h, HEAD_DIM:, rows] = one_row
            k = qkv[192 + h * HEAD_DIM : 192 + (h + 1) * HEAD_DIM]
            k_cm[near, rows] = k
            k_tm[h, rows, :] = bias
            k_tm[h, rows, 0:HEAD_DIM] = k.T
            v = qkv[384 + h * HEAD_DIM : 384 + (h + 1) * HEAD_DIM]
            v_cm[h, 0:HEAD_DIM, rows] = v
            v_cm[h, HEAD_DIM:, rows] = one_row[0:16]
            v_tm[h, rows, :] = v.T
        return carry

    lax.fori_loop(0, LANES // CHUNK, project, 0)
    write((q_cm, q_cm_), (k_tm, k_tm_), (v_tm, v_tm_), (k_cm, k_cm_), (normed_one, normed_one_))
    clock.work(4.0)
    chunks = [(h, c) for h in range(3) for c in range(LANES // CHUNK)]

    def scores(h, c):
        return dot(k_tm[h, 0:ROWS, :], q_cm[h, :, c * CHUNK : (c + 1) * CHUNK])

    def mixed_at(t, h, lanes):
        return mixed_all.at[
            pl.ds(pl.multiple_of(h * CH + t * HEAD_DIM, HEAD_DIM), HEAD_DIM), lanes
        ]

    def gather(h, lanes):
        g = Gather(links, p, lambda t: mixed_at(t, h, lanes))
        g.start(clock, (lanes.stop - lanes.start) * HEAD_DIM * 2)
        gathers.append(g)

    gathers = []
    ahead = scores(0, 0)
    for at, (h, c) in enumerate(chunks):
        s = ahead
        if at + 1 < len(chunks):
            ahead = scores(*chunks[at + 1])
        heads = slice(h * HEAD_DIM, (h + 1) * HEAD_DIM)
        lanes = slice(c * CHUNK, (c + 1) * CHUNK)
        top = jnp.max(s, axis=0, keepdims=True)
        out = dot(v_cm[h, :, 0:ROWS], jnp.exp(s - top).astype(BF16))
        total = out[HEAD_DIM : HEAD_DIM + 1]
        out = (out[0:HEAD_DIM] * (1.0 / total)).astype(BF16)
        lse[h : h + 1, lanes] = top + jnp.log(total)
        mixed[heads, lanes] = out
        mixed_at(p.t, h, lanes)[...] = out
        if c == 4:
            gather(h, slice(0 if h < 2 else 4 * CHUNK, LANES))
        elif h == 2 and c % 2:
            gather(h, slice((c - 1) * CHUNK, (c + 1) * CHUNK))
        clock.work(0.6)
    write((lse, lse_), (mixed, mixed_))
    while any(act_[2] in waited for act_ in clock.queue for waited in ((f_out.swap, f_out.trade, f_out.end, f_tap.swap, f_tap.trade, f_tap.end, gathers[0].forward, gathers[1].forward),)):
        clock.work(0.3)
    for c in c_near + c_far:
        c.wait_recv()
    for far in range(4):
        for k in range(3):
            out_heads[k * CH + far * HEAD_DIM : k * CH + (far + 1) * HEAD_DIM, :] = out_all[
                far * 192 + k * HEAD_DIM : far * 192 + (k + 1) * HEAD_DIM, :
            ]
    gathers[0].finish()
    gathers[1].finish()
    clock.work(0.5)

    def begin(i, carry):
        rows = pl.ds(pl.multiple_of(i * CHUNK, CHUNK), CHUNK)
        branch = dot(mixed_all[0 : 2 * CH, rows], out_heads[0 : 2 * CH, :], (0, 0))
        hidden[rows, :] = tok[rows, :].astype(F32) + branch
        return carry

    lax.fori_loop(0, LANES // CHUNK, begin, 0)
    clock.work(2.0)
    while any(act_[2] in [g.forward for g in gathers] for act_ in clock.queue):
        clock.work(0.3)
    for g in gathers[2:]:
        g.finish()
    gain_after = gain_two[...].reshape(1, D)

    def finish(i, carry):
        rows = pl.ds(pl.multiple_of(i * CHUNK, CHUNK), CHUNK)
        after = hidden[rows, :] + dot(
            mixed_all[2 * CH : 3 * CH, rows], out_heads[2 * CH : 3 * CH, :], (0, 0)
        )
        hidden[rows, :] = after
        scaled, _ = norm(after)
        normed_two[rows, :] = (scaled * gain_after).astype(BF16)
        return carry

    lax.fori_loop(0, LANES // CHUNK, finish, 0)
    hidden_own[...] = hidden[pl.ds(pl.multiple_of(p.t * PART, 16), PART), :]
    write((hidden_own, hidden_own_), (normed_two, normed_two_))
    clock.work(2.5)
    for copy in late:
        copy.wait()

    def part(owner):
        rows = pl.ds(pl.multiple_of(owner * PART, 16), PART)
        activation, steep = gelu_and_slope(dot(normed_two[rows, :], w_up[...]))
        activation = activation.astype(BF16)
        slope[rows, :] = steep.astype(BF16)
        act[rows, :] = activation
        return dot(activation, w_down[...])

    sums = Scatter(links, p, out_c, out_x, in_c, in_x, mine)
    sums.far(part, clock, 1.7)
    sums.near(part, clock, 1.7)
    write((slope, slope_), (act, act_))
    h_down = [
        Halver(links, p, clock, down_part.at[i], down_arrive.at[i], None, (Y, Z, ZZ))
        for i in range(2)
    ]
    for i in range(4):
        rows = slice(i * PART, (i + 1) * PART)
        cot[rows, :] = (
            cell_mask((PART, D), 0, i * PART, length[0]) * cot[rows, :].astype(F32)
        ).astype(BF16)
    for i in range(2):
        cols = slice(i * (D // 2), (i + 1) * (D // 2))
        down_part[i] = dot(act[:, cols], cot[...], (0, 0)).astype(BF16)
        h_down[i].step()
        clock.work(0.8)
    lower(cot_field, grad_own, tall, upsample_table(GW).astype(BF16))
    gathers = []
    for at, piece in enumerate(PIECES):
        total = sums.piece(at, clock)
        off = pl.multiple_of(p.t * PART + piece[0], 16)
        mask = cell_mask((piece[1], D), 0, off, length[0])
        out = (mask * (hidden_own[pl.ds(*piece), :] + total)).astype(BF16)
        out_own[pl.ds(*piece), :] = out
        field[pl.ds(off, piece[1]), :] = dot(out, tap_all[...], (1, 1)).astype(BF16)
        g = Gather(links, p, lambda t: piece_at(field, t, piece))
        g.start(clock, piece[1] * CH * 2)
        gathers.append(g)
        clock.work(0.5)
    while any(act_[2] in [g.forward for g in gathers] for act_ in clock.queue):
        clock.work(0.3)
    while any(act_[2] in (f_conv.swap, f_conv.trade, f_conv.end) for act_ in clock.queue):
        clock.work(0.3)
    for g in gathers:
        g.finish()
    levels["down"] = [h.level() for h in h_down]
    sums.finish()
    for c in c_near + c_far:
        c.wait_send()
    for f in (f_out, f_tap, f_conv):
        f.finish()
    for h in h_down:
        h.finish()
    for copy in writes:
        copy.wait()


def front_call(bits, levels, *args):
    kept = [
        ((PART, D), F32),
        ((LANES, D), BF16),
        ((3, SLOT, LANES), BF16),
        ((3, LANES, SLOT), BF16),
        ((3, LANES, HEAD_DIM), BF16),
        ((192, LANES), BF16),
        ((8, LANES), F32),
        ((192, LANES), BF16),
        ((LANES, D), BF16),
        ((ROWS, D), BF16),
        ((ROWS, D), BF16),
    ]
    outs = kept + [
        ((CH, D), BF16),
        ((PART, D), BF16),
        ((ROWS, CH), BF16),
        ((4, WIDE, CH), BF16),
        ((BLOCK, LANES), F32),
        ((2, D // 2, D), BF16),
    ]
    scratch = [pltpu.VMEM(*k) for k in kept] + [
        pltpu.VMEM((2,) + landing(D // 2, D, bits).shape, BF16),
        pltpu.VMEM((LANES, D), BF16),
        pltpu.VMEM((LANES, D), F32),
        pltpu.VMEM((D, LANES), BF16),
        pltpu.VMEM((D, D), BF16),
        pltpu.VMEM((D, D), BF16),
        pltpu.VMEM((3, HEAD_DIM + 16, LANES), BF16),
        pltpu.VMEM((D, D), BF16),
        pltpu.VMEM((D, D), BF16),
        pltpu.VMEM((2 * GH, BLOCK, 2 * GW), BF16),
        pltpu.VMEM((ROWS, D), BF16),
    ] + scatter_scratch() + [
        pltpu.VMEM((GH * BLOCK, 2 * GW), F32),
        pltpu.SemaphoreType.DMA((5 + len(kept),)),
    ] + sems(70)
    return call(
        functools.partial(front_kernel, levels), outs,
        [smem, anywhere] + [vmem] * 5 + [anywhere] * 5, scratch, 0, 14_000_000_000, args,
        [anywhere] * len(kept) + [vmem] * 6,
    )


def lower(cot, grad, tall, table):
    grad[:, SLOTS:] = jnp.zeros((BLOCK, LANES - SLOTS), F32)
    for a in range(GH):
        mid = 0.75 * (cot[2 * a].astype(F32) + cot[2 * a + 1].astype(F32))
        before = cot[max(2 * a - 1, 0)].astype(F32)
        after = cot[min(2 * a + 2, 2 * GH - 1)].astype(F32)
        tall[a * BLOCK : (a + 1) * BLOCK, :] = mid + 0.25 * (before + after)
    for a in range(GH):
        grad[:, a * GW : (a + 1) * GW] = split_dot(tall[a * BLOCK : (a + 1) * BLOCK, :], table)


def scatter_scratch():
    return [
        pltpu.VMEM((2, PART, D), BF16),
        pltpu.VMEM((PART, D), BF16),
        pltpu.VMEM((2, PART, D), BF16),
        pltpu.VMEM((PART, D), BF16),
        pltpu.VMEM((PART, D), F32),
    ]


def conv_kernel(
    levels, length, field, w_own, w_far, grad_own, out_own, down_hbm,
    result, tap_grad, g_conv, out_all, down,
    start_all, state, steep_first, steep_state, x_all, wide, flip, dcol, back, grad, grad_far,
    grad_near, back_out, back_in, arrive, down_part, down_arrive, local, send, recv,
):
    p = Peers()
    links = Links(send, recv)
    clock = Clock()
    bring = pltpu.make_async_copy(down_hbm, down_part, local.at[0])
    bring.start()
    bring.wait()
    p.greet(p.bits())
    weights = (w_own, w_far)
    block_of = (p.t, p.xp)
    at = lambda t: pl.ds(pl.multiple_of(t * BLOCK, BLOCK), BLOCK)

    part_at(out_all, p.t)[...] = out_own[...]
    out_all[ROWS:, :] = jnp.zeros((LANES - ROWS, D), BF16)
    g_out = Gather(links, p, lambda t: part_at(out_all, t))
    grad_near[...] = grad_own[...].astype(BF16)
    c_grad = links.copy(grad_near, grad_far, (p.dp, p.xp))
    c_grad.start()
    halvers = {
        j: Halver(links, p, clock, g_conv.at[j], arrive.at[j], None, ORDERS[j]) for j in (3, 2, 1)
    }
    h_down = [
        Halver(
            links, p, clock, down_part.at[i], down_arrive.at[i], down.at[i], (Y, Z, ZZ),
            levels["down"][i],
        )
        for i in range(2)
    ]
    for h in h_down:
        h.step()

    def masks(count):
        _, col = grid_place((count, LANES), 1, 0)
        not_first = jnp.where(col > 0.5, 1.0, 0.0)
        not_last = jnp.where(col < GW - 1.5, 1.0, 0.0)
        return cell_mask((count, LANES), 1, 0, length[0]), not_first, not_last

    _, not_first8, not_last8 = masks(8)
    cells16, not_first16, not_last16 = masks(16)
    not_first16, not_last16 = not_first16.astype(BF16), not_last16.astype(BF16)

    start_all[:, ROWS:] = jnp.zeros((CH, LANES - ROWS), F32)
    start_all[:, 0:ROWS] = field[...].astype(F32).T

    def rows_at(i):
        return pl.ds(pl.multiple_of(i * 16, 16), 16)

    def into_at(b, i):
        return pl.ds(pl.multiple_of(block_of[b] * BLOCK + i * 16, 16), 16)

    def open_rows(i, carry):
        x_all[0, rows_at(i), :] = gelu(start_all[rows_at(i), :]).astype(BF16)
        return carry

    lax.fori_loop(0, CH // 16, open_rows, 0)
    clock.work(2.0)

    def convolve(index, b, use):
        for c in range(LANES // CHUNK):
            lanes = slice(c * CHUNK, (c + 1) * CHUNK)
            wide[:, lanes] = dot(weights[b][index], x_all[index, :, lanes])

        def rows16(i, carry):
            halves = []
            for half in range(2):
                total = None
                for q in range(3):
                    tap = lambda r: wide[
                        pl.ds(pl.multiple_of((r * 3 + q) * BLOCK + i * 16 + half * 8, 8), 8), :
                    ]
                    three = (
                        tap(1)
                        + pltpu.roll(tap(0), GW, 1)
                        + pltpu.roll(tap(2), LANES - GW, 1)
                    )
                    if q == 0:
                        three = pltpu.roll(three, 1, 1) * not_first8
                    if q == 2:
                        three = pltpu.roll(three, LANES - 1, 1) * not_last8
                    total = three if total is None else total + three
                halves.append(total)
            use(i, cells16 * jnp.concatenate(halves, axis=0))
            return carry

        lax.fori_loop(0, BLOCK // 16, rows16, 0)
        clock.work(2.2)

    pending = []

    def share(array, b):
        place = array.at[at(block_of[b]), :]
        copy = links.copy(place, place, (p.dp, p.sib))
        copy.start()
        pending.append(copy)
        return copy

    def settle(copies):
        for c in copies:
            c.wait_recv()
        clock.work(1.0)

    def first_conv(unit):
        copies = []
        for b in range(2):
            def use(i, value, b=b):
                low, steep = gelu_and_slope(value)
                x_all[2 * unit + 1, into_at(b, i), :] = low.astype(BF16)
                steep_first[unit, b, rows_at(i), :] = steep

            convolve(2 * unit, b, use)
            copies.append(share(x_all.at[2 * unit + 1], b))
        return copies

    def spread(turn, b, value_of):
        def rows16(i, carry):
            value = value_of(i).astype(BF16)
            for q in range(3):
                side = value
                if q == 0:
                    side = pltpu.roll(value, LANES - 1, 1) * not_last16
                if q == 2:
                    side = pltpu.roll(value, 1, 1) * not_first16
                for r in range(3):
                    moved = side
                    if r == 0:
                        moved = pltpu.roll(side, LANES - GW, 1)
                    if r == 2:
                        moved = pltpu.roll(side, GW, 1)
                    into = pl.ds(pl.multiple_of((r * 3 + q) * BLOCK + i * 16, 16), 16)
                    dcol[turn % 2, b, into, :] = moved
            return carry

        lax.fori_loop(0, BLOCK // 16, rows16, 0)
        clock.work(0.8)

    def conv_back(turn):
        index = 3 - turn
        flip[0] = w_own[index].T
        flip[1] = w_far[index].T
        for c in range(LANES // CHUNK):
            lanes = slice(c * CHUNK, (c + 1) * CHUNK)
            back[:, lanes] = dot(flip[0], dcol[turn % 2, 0, :, lanes]) + dot(
                flip[1], dcol[turn % 2, 1, :, lanes]
            )
        copies = []
        for b, t in enumerate((p.sib, p.diag)):
            back_out[turn, b] = back[at(t), :].astype(BF16)
            c = links.copy(back_out.at[turn, b], back_in.at[turn, b], (p.dp, p.sib))
            c.start()
            copies.append(c)
        pending.extend(copies)
        clock.work(1.3)
        return copies

    def summed(turn, b, i):
        return back[into_at(b, i), :] + back_in[turn, b, rows_at(i), :].astype(F32)

    def weight_grad(turn):
        index = 3 - turn
        found = dot(dcol[turn % 2, 0], x_all[index], (1, 1)).astype(BF16)
        g_conv[index, 0:WIDE, :] = found[:, 0:SLOT]
        g_conv[index, WIDE:, :] = found[:, SLOT:]

    coming = first_conv(0)
    for b in range(2):
        def opening(i, carry, b=b):
            value = start_all[into_at(b, i), :]
            state[b, rows_at(i), :] = value
            steep_state[0, b, rows_at(i), :] = gelu_and_slope(value)[1]
            return carry

        lax.fori_loop(0, BLOCK // 16, opening, 0)
    clock.work(1.0)
    c_grad.wait_recv()
    g_out.start()
    grad[0] = grad_own[...]
    grad[1] = grad_far[...].astype(F32)
    for b in range(2):
        spread(0, b, lambda i, b=b: cells16 * grad[b, rows_at(i), :])
    settle(coming)
    coming = []
    for b in range(2):
        def use_second(i, value, b=b):
            fresh = state[b, rows_at(i), :] + value
            low, steep = gelu_and_slope(fresh)
            state[b, rows_at(i), :] = fresh
            x_all[2, into_at(b, i), :] = low.astype(BF16)
            steep_state[1, b, rows_at(i), :] = steep

        convolve(1, b, use_second)
        coming.append(share(x_all.at[2], b))
    backs = conv_back(0)
    settle(coming)
    coming = first_conv(1)
    settle(backs)
    for b in range(2):
        spread(
            1, b, lambda i, b=b: cells16 * summed(0, b, i) * steep_first[1, b, rows_at(i), :]
        )
    settle(coming)
    backs = conv_back(1)
    weight_grad(0)
    halvers[3].step()

    def use_last(i, value):
        result[rows_at(i), :] = state[0, rows_at(i), :] + value

    convolve(3, 0, use_last)
    weight_grad(1)
    halvers[2].step()
    clock.work(0.8)
    settle(backs)
    for b in range(2):
        def renewed(i, b=b):
            fresh = grad[b, rows_at(i), :] + summed(1, b, i) * steep_state[1, b, rows_at(i), :]
            grad[b, rows_at(i), :] = fresh
            return cells16 * fresh

        spread(2, b, renewed)
    backs = conv_back(2)
    weight_grad(2)
    halvers[1].step()
    clock.work(0.5)
    g_out.forward()
    settle(backs)
    for b in range(2):
        spread(
            3, b, lambda i, b=b: cells16 * summed(2, b, i) * steep_first[0, b, rows_at(i), :]
        )
    backs = conv_back(3)
    weight_grad(3)
    clock.work(0.5)
    inside16 = jnp.where(
        lax.broadcasted_iota(jnp.int32, (16, LANES), 1) < SLOTS, 1.0, 0.0
    )
    settle(backs)
    coming = []
    for b in range(2):
        def close(i, carry, b=b):
            fresh = grad[b, rows_at(i), :] + summed(3, b, i) * steep_state[0, b, rows_at(i), :]
            tap_grad[into_at(b, i), :] = (inside16 * fresh).astype(BF16)
            return carry

        lax.fori_loop(0, BLOCK // 16, close, 0)
        coming.append(share(tap_grad, b))
    settle(coming)
    while not all(h.done() for h in h_down):
        clock.work(0.5)
    levels[0] = 0
    for j, h in halvers.items():
        levels[j] = h.level()
    for c in pending + [c_grad]:
        c.wait_send()
    for h in list(halvers.values()) + h_down:
        h.finish()
    g_out.finish()


FLAT = (2 * WIDE, SLOT)
ORDERS = ((Y, Z4), (Y, Z4), (Z, Y, ZZ), (Y, Z, ZZ))


def conv_call(bits, levels, *args):
    outs = [
        ((BLOCK, LANES), F32),
        ((CH, LANES), BF16),
        ((4,) + FLAT, BF16),
        ((LANES, D), BF16),
        ((2, D // 2, D), BF16),
    ]
    scratch = [
        pltpu.VMEM((CH, LANES), F32),
        pltpu.VMEM((2, BLOCK, LANES), F32),
        pltpu.VMEM((2, 2, BLOCK, LANES), F32),
        pltpu.VMEM((2, 2, BLOCK, LANES), F32),
        pltpu.VMEM((4, CH, LANES), BF16),
        pltpu.VMEM((WIDE, LANES), F32),
        pltpu.VMEM((2, CH, WIDE), BF16),
        pltpu.VMEM((2, 2, WIDE, LANES), BF16),
        pltpu.VMEM((CH, LANES), F32),
        pltpu.VMEM((2, BLOCK, LANES), F32),
        pltpu.VMEM((BLOCK, LANES), BF16),
        pltpu.VMEM((BLOCK, LANES), BF16),
        pltpu.VMEM((4, 2, BLOCK, LANES), BF16),
        pltpu.VMEM((4, 2, BLOCK, LANES), BF16),
        pltpu.VMEM((4,) + landing(*FLAT, bits).shape, BF16),
        pltpu.VMEM((2, D // 2, D), BF16),
        pltpu.VMEM((2,) + landing(D // 2, D, bits).shape, BF16),
        pltpu.SemaphoreType.DMA((1,)),
    ] + sems(70)
    return call(
        functools.partial(conv_kernel, levels), outs, [smem] + [vmem] * 5 + [anywhere], scratch,
        2, 9_000_000_000, args,
    )


def lift(field, joined, table, grid_rows):
    for a in grid_rows:
        here = field[:, a * GW : (a + 1) * GW]
        up, down = max(a - 1, 0), min(a + 1, GH - 1)
        for side, other in enumerate((up, down)):
            line = 0.75 * here + 0.25 * field[:, other * GW : (other + 1) * GW]
            joined[2 * a + side] = split_dot(line, table).astype(BF16)


def back_kernel(
    levels, length, tap_grad, tap_all, cot_hbm, slope, act, normed_two, w_up, w_down, hidden_own, gain_two,
    out_all_, field_, conv_hbm,
    w_out_, mixed_, q_cm_, k_tm_, v_tm_, k_cm_, lse_, normed_one_, w_qkv_, tok_hbm, gain_one,
    joined, grad_tok, conv, up, low, ot, head, gain_sum,
    out_all, field, w_out, mixed, q_cm, k_tm, v_tm, k_cm, lse, normed_one, w_qkv,
    tok, tap_tm, d_pre, mine_block, grad_hidden, branch, out_c, out_x, in_c, in_x, mine,
    conv_part, up_part, low_part, ot_part, head_part,
    conv_arrive, up_arrive, low_arrive, ot_arrive, head_arrive, gain_out, gain_arrive,
    d_mix, acc_k, acc_v, d_cm, d_tm, w_by_head, local, send, recv,
):
    p = Peers()
    links = Links(send, recv)
    clock = Clock()
    bring_conv = pltpu.make_async_copy(conv_hbm, conv_part, local.at[1])
    bring_conv.start()
    late = [
        pltpu.make_async_copy(src, dst, local.at[2 + i])
        for i, (src, dst) in enumerate(
            (
                (out_all_, out_all), (field_, field), (w_out_, w_out), (mixed_, mixed),
                (q_cm_, q_cm), (k_tm_, k_tm), (v_tm_, v_tm), (k_cm_, k_cm), (lse_, lse),
                (normed_one_, normed_one), (w_qkv_, w_qkv),
            )
        )
    ]
    bring = pltpu.make_async_copy(cot_hbm, tok.at[pl.ds(0, SLOTS), :], local.at[0])
    bring.start()
    tok[SLOTS:, :] = jnp.zeros((ROWS - SLOTS, D), BF16)
    bring_conv.wait()
    p.greet(p.bits())

    def halver(array, arrive, result, stages, after=0):
        made = Halver(links, p, clock, array, arrive, result, stages, after)
        halvers.append(made)
        return made

    halvers = []
    for j in (3, 2, 1, 0):
        halver(conv_part.at[j], conv_arrive.at[j], conv.at[j], ORDERS[j], levels[j]).step()
    half = D // 2
    h_up = [
        halver(up_part.at[i], up_arrive.at[i], up.at[i], (Y, Z4))
        for i in range(2)
    ]
    h_low = halver(low_part, low_arrive, low, (Z, Y, ZZ))
    h_ot = halver(ot_part, ot_arrive, ot, (Z, Y, ZZ))
    h_head = [
        halver(head_part.at[h], head_arrive.at[h], head.at[h], ((Y, Z4), (Y, Z4), (ALL,))[h])
        for h in range(3)
    ]
    gains = Doubler(links, p, gain_out, gain_arrive)

    tap_tm[...] = (
        cell_mask((LANES, CH), 0, 0, length[0]) * tap_grad[...].T.astype(F32)
    ).astype(BF16)
    low_part[...] = dot(act[...], tap_tm[0:ROWS, :], (0, 0)).astype(BF16)
    h_low.step()
    clock.work(1.0)
    bring.wait()

    def part(owner):
        off = pl.multiple_of(owner * PART, 16)
        rows = pl.ds(off, PART)
        block = cell_mask((PART, D), 0, off, length[0]) * (
            tok[rows, :].astype(F32) + dot(tap_tm[rows, :], tap_all[...])
        )
        mine_block[...] = block
        steep = (dot(block.astype(BF16), w_down[...], (1, 1)) * slope[rows, :].astype(F32)).astype(BF16)
        d_pre[rows, :] = steep
        return dot(steep, w_up[...], (1, 1))

    for copy in late:
        copy.start()
    sums = Scatter(links, p, out_c, out_x, in_c, in_x, mine)
    sums.far(part, clock, 1.7)
    sums.near(part, clock, 1.7)
    for i in range(2):
        cols = slice(i * half, (i + 1) * half)
        up_part[i] = dot(normed_two[0:ROWS, cols], d_pre[...], (0, 0)).astype(BF16)
        h_up[i].step()
        clock.work(0.8)
    gain = gain_two[...].reshape(1, D)
    gathers = []
    gain_part_two = jnp.zeros((1, D), F32)
    for at, piece in enumerate(PIECES):
        rows = pl.ds(*piece)
        total = sums.piece(at, clock)
        scaled, inverse = norm(hidden_own[rows, :])
        inner, add = norm_back(total, scaled, inverse, gain)
        after = mine_block[rows, :] + inner
        grad_hidden[rows, :] = after
        gain_part_two = gain_part_two + add
        branch[pl.ds(pl.multiple_of(p.t * PART + piece[0], 16), piece[1]), :] = after.astype(BF16)
        g = Gather(links, p, lambda t: piece_at(branch, t, piece))
        g.start(clock, piece[1] * D * 2)
        gathers.append(g)
        clock.work(0.6)
    sums.finish()
    bring = pltpu.make_async_copy(tok_hbm, tok.at[pl.ds(0, SLOTS), :], local.at[0])
    bring.start()
    for copy in late:
        copy.wait()
    table = upsample_table(GW).T.astype(BF16)
    for quarter in range(5):
        lift(field, joined, table, range(quarter * 6, quarter * 6 + 6))
        clock.work(0.4)
    ot_part[192:, :] = dot(
        tap_grad[pl.ds(pl.multiple_of(p.t * BLOCK, BLOCK), BLOCK), :], out_all[...]
    ).astype(BF16)
    for h in range(3):
        for part_at_ in range(3):
            w_by_head[h * 192 + part_at_ * 64 : h * 192 + part_at_ * 64 + 64, :] = w_qkv[
                part_at_ * 192 + h * 64 : part_at_ * 192 + h * 64 + 64, :
            ]
    d_mix[:, ROWS:] = jnp.zeros((192, LANES - ROWS), BF16)
    d_cm[:, ROWS:] = jnp.zeros((3 * 192, LANES - ROWS), BF16)
    clock.work(1.0)
    while any(act.__self__ in gathers for _, _, act in clock.queue if hasattr(act, "__self__")):
        clock.work(0.5)
    for g in gathers:
        g.finish()
    clock.work(1.0)
    ot_part[0:192, :] = dot(mixed[:, 0:ROWS], branch[...]).astype(BF16)
    h_ot.step()
    d_mix[:, 0:ROWS] = dot(w_out[...], branch[...], (1, 1)).astype(BF16)
    clock.work(1.5)
    for h in range(3):
        heads = slice(h * HEAD_DIM, (h + 1) * HEAD_DIM)
        for c in range(LANES // CHUNK):
            lanes = slice(c * CHUNK, (c + 1) * CHUNK)
            dm = d_mix[heads, lanes]
            inner = jnp.sum(
                dm.astype(F32) * mixed[heads, lanes].astype(F32), axis=0, keepdims=True
            )
            probs = jnp.exp(
                dot(k_tm[h, 0:ROWS, :], q_cm[h, :, lanes]) - lse[h : h + 1, lanes]
            )
            d_probs = dot(v_tm[h, 0:ROWS, :], dm)
            d_raw = (probs * (d_probs - inner)).astype(BF16)
            d_v = dot(probs.astype(BF16), dm, (1, 1))
            d_k = dot(d_raw, q_cm[h, 0:HEAD_DIM, lanes], (1, 1))
            acc_v[...] = d_v if c == 0 else acc_v[...] + d_v
            acc_k[...] = d_k if c == 0 else acc_k[...] + d_k
            d_q = dot(k_cm[heads, 0:ROWS], d_raw) * 0.125
            d_cm[h * 192 : h * 192 + 64, lanes] = d_q.astype(BF16)
            clock.work(0.85)
        d_cm[h * 192 + 64 : h * 192 + 128, 0:ROWS] = acc_k[...].T.astype(BF16)
        d_cm[h * 192 + 128 : h * 192 + 192, 0:ROWS] = acc_v[...].T.astype(BF16)
        three = dot(d_cm[h * 192 : (h + 1) * 192, :], normed_one[...]).astype(BF16)
        head_part[h, 0:192, :] = three[:, 0:384]
        head_part[h, 192:, :] = three[:, 384:]
        h_head[h].step()
        clock.work(0.7)
    d_tm[...] = d_cm[...].T
    bring.wait()

    def part_two(owner):
        rows = pl.ds(pl.multiple_of(owner * PART, 16), PART)
        return dot(d_tm[rows, :], w_by_head[...])

    sums = Scatter(links, p, out_c, out_x, in_c, in_x, mine)
    sums.far(part_two, clock, 1.0)
    sums.near(part_two, clock, 1.0)
    gain = gain_one[...].reshape(1, D)
    gathers = []
    gain_part = jnp.zeros((1, D), F32)
    for at, piece in enumerate(PIECES):
        rows = pl.ds(*piece)
        place = pl.ds(pl.multiple_of(p.t * PART + piece[0], 16), piece[1])
        total = sums.piece(at, clock)
        scaled, inverse = norm(tok[place, :].astype(F32))
        inner, add = norm_back(total, scaled, inverse, gain)
        gain_part = gain_part + add
        grad_tok[place, :] = (grad_hidden[rows, :] + inner).astype(BF16)
        g = Gather(links, p, lambda t: piece_at(grad_tok, t, piece))
        g.start(clock, piece[1] * D * 2)
        gathers.append(g)
        clock.work(0.6)
    row = lax.broadcasted_iota(jnp.int32, (8, D), 0)
    gains.start(jnp.where(row == 0, gain_part, 0.0) + jnp.where(row == 1, gain_part_two, 0.0))

    def turn():
        gains.step()
        if len(gains.copies) < len(gains.to):
            clock.later(clock.now + 3.0, turn)

    clock.later(clock.now + 3.0, turn)
    clock.drain()
    gain_sum[...] = gains.finish()
    for g in gathers:
        g.finish()
    sums.finish()
    for h in halvers:
        h.finish()


LATE = (11, 12) + tuple(range(14, 23))


def back_call(bits, levels, *args):
    outs = [
        ((2 * GH, BLOCK, 2 * GW), BF16),
        ((ROWS, D), BF16),
        ((4,) + FLAT, BF16),
        ((2, D // 2, D), BF16),
        ((D, CH), BF16),
        ((256, D), BF16),
        ((3, 384, 384), BF16),
        ((8, D), F32),
    ]
    room = lambda lead, rows, columns: pltpu.VMEM(
        lead + landing(rows, columns, bits).shape, BF16
    )
    scratch = [pltpu.VMEM(args[at].shape, args[at].dtype) for at in LATE] + [
        pltpu.VMEM((ROWS, D), BF16),
        pltpu.VMEM((LANES, CH), BF16),
        pltpu.VMEM((ROWS, D), BF16),
        pltpu.VMEM((PART, D), F32),
        pltpu.VMEM((PART, D), F32),
        pltpu.VMEM((ROWS, D), BF16),
    ] + scatter_scratch() + [
        pltpu.VMEM((4,) + FLAT, BF16),
        pltpu.VMEM((2, D // 2, D), BF16),
        pltpu.VMEM((D, CH), BF16),
        pltpu.VMEM((256, D), BF16),
        pltpu.VMEM((3, 384, 384), BF16),
        room((4,), *FLAT),
        room((2,), D // 2, D),
        room((), D, CH),
        room((), 256, D),
        room((3,), 384, 384),
        pltpu.VMEM((2 + bits, 8, D), F32),
        pltpu.VMEM((2 + bits, 8, D), F32),
        pltpu.VMEM((192, LANES), BF16),
        pltpu.VMEM((ROWS, HEAD_DIM), F32),
        pltpu.VMEM((ROWS, HEAD_DIM), F32),
        pltpu.VMEM((3 * 192, LANES), BF16),
        pltpu.VMEM((LANES, 3 * 192), BF16),
        pltpu.VMEM((3 * 192, D), BF16),
        pltpu.SemaphoreType.DMA((2 + len(LATE),)),
    ] + sems(130)
    return call(
        functools.partial(back_kernel, levels), outs,
        [
            smem if at == 0 else anywhere if at in LATE + (3, 13, 23) else vmem
            for at in range(len(args))
        ],
        scratch, 3, 20_000_000_000, args,
    )


def write_kernel(
    out_all, grad_tok, conv, up, down, low, tap_all, ot, head, gains, joined_in,
    out_tokens, grad_tokens, conv_sum, up_sum, down_sum, out_sum, tap_sum, qkv_sum, gain_one,
    gain_two, joined,
):
    out_tokens[...] = out_all[0:SLOTS, :]
    grad_tokens[...] = grad_tok[0:SLOTS, :]
    joined[...] = joined_in[...]
    gain_one[...] = gains[0]
    gain_two[...] = gains[1]
    for j in range(4):
        for side in range(2):
            conv_sum[j, :, side * SLOT : (side + 1) * SLOT] = conv[
                j, side * WIDE : (side + 1) * WIDE, :
            ].astype(F32)
    for i in range(2):
        rows = slice(i * (D // 2), (i + 1) * (D // 2))
        up_sum[rows, :] = up[i].astype(F32)
        down_sum[rows, :] = down[i].astype(F32) + dot(low[rows, :], tap_all[...])
    out_sum[...] = ot[0:192, :].astype(F32)
    tap_sum[...] = ot[192:, :].astype(F32)
    for h in range(3):
        for part in range(3):
            for side in range(2):
                rows = side * 192 + part * 64
                qkv_sum[
                    part * 192 + h * 64 : part * 192 + h * 64 + 64, side * 384 : (side + 1) * 384
                ] = head[h, rows : rows + 64, :].astype(F32)


def write_call(*args):
    outs = [
        ((SLOTS, D), BF16),
        ((SLOTS, D), BF16),
        ((4, WIDE, CH), F32),
        ((D, D), F32),
        ((D, D), F32),
        ((192, D), F32),
        ((BLOCK, D), F32),
        ((3 * 192, D), F32),
        ((D,), F32),
        ((D,), F32),
        ((2 * GH, BLOCK, 2 * GW), BF16),
    ]
    return call(write_kernel, outs, [vmem] * 11, [], None, 400_000_000, args)


def per_device(
    bits, tokens, lengths, gain_one, gain_two, w_qkv, w_out, w_up, w_down, w_tap, w_conv,
    cot_tokens, cot_joined,
):
    w_heads = w_qkv.transpose(0, 2, 1).reshape(3 * 192, D)
    conv_w = w_conv.transpose(0, 1, 2, 4, 3).reshape(4, WIDE, CH)
    levels = {}
    (
        hidden_own, normed_two, q_cm, k_tm, v_tm, k_cm, lse, mixed, normed_one, slope, act,
        tap_all, out_own, field, conv_far, grad_own, down_part,
    ) = front_call(
        bits, levels, lengths, tokens, gain_one, gain_two, w_heads, w_out, w_tap.T, conv_w, w_up, w_down,
        cot_joined[0].transpose(0, 2, 1), cot_tokens,
    )
    result, tap_grad, g_conv, out_all, down = conv_call(
        bits, levels, lengths, field, conv_w, conv_far, grad_own, out_own, down_part
    )
    joined, grad_tok, conv, up, low, ot, head, gain_sum = back_call(
        bits, levels, lengths, tap_grad, tap_all, cot_tokens, slope, act, normed_two, w_up, w_down,
        hidden_own, gain_two, out_all, result, g_conv,
        w_out, mixed, q_cm, k_tm, v_tm, k_cm, lse, normed_one, w_heads, tokens, gain_one,
    )
    (
        out_tokens, grad_tokens, conv_sum, up_sum, down_sum, out_sum, tap_sum, qkv_sum, gain_a,
        gain_b, joined,
    ) = write_call(out_all, grad_tok, conv, up, down, low, tap_all, ot, head, gain_sum, joined)
    return (
        out_tokens,
        joined.transpose(0, 2, 1)[None],
        grad_tokens,
        qkv_sum.reshape(3, 192, D).transpose(0, 2, 1),
        out_sum,
        up_sum,
        down_sum,
        tap_sum.T,
        conv_sum.reshape(4, 3, 3, BLOCK, CH).transpose(0, 1, 2, 4, 3),
        gain_a,
        gain_b,
    )


def solution(mesh):
    placed = (
        P("dp", None),
        P("dp"),
        P(),
        P(),
        P(None, None, "tensor"),
        P("tensor", None),
        P(None, "tensor"),
        P("tensor", None),
        P(None, "tensor"),
        P(None, None, None, None, "tensor"),
        P("dp", None),
        P("dp", None, None, "tensor"),
    )
    return jax.shard_map(
        functools.partial(per_device, mesh.shape["dp"].bit_length() - 1),
        mesh=mesh,
        in_specs=placed,
        out_specs=(
            P("dp", None),
            P("dp", None, None, "tensor"),
            P("dp", None),
            P(None, None, "tensor"),
            P("tensor", None),
            P(None, "tensor"),
            P("tensor", None),
            P(None, "tensor"),
            P(None, None, None, None, "tensor"),
            P(),
            P(),
        ),
        check_vma=False,
    )
```

```python
import functools

import jax
import jax.numpy as jnp
from jax import lax
from jax.experimental import pallas as pl
from jax.experimental.pallas import tpu as pltpu
from jax.sharding import PartitionSpec as P

HEAD_DIM = 64
GH = 30
GW = 40
SH = 24
SW = 24
SLOTS = GH * GW
D = 768
CH = 256
BLOCK = 64
TAPS = 9
WIDE = TAPS * BLOCK
PART = 304
ROWS = 4 * PART
LANES = 1280
CHUNK = 256
SLOT = 128
F32 = jnp.float32
BF16 = jnp.bfloat16
MESH = pl.DeviceIdType.MESH
VMEM_LIMIT = 60 * 2**20

vmem = pl.BlockSpec(memory_space=pltpu.VMEM)
smem = pl.BlockSpec(memory_space=pltpu.SMEM)
anywhere = pl.BlockSpec(memory_space=pl.ANY)


def dot(a, b, dims=(1, 0)):
    return lax.dot_general(
        a, b, (((dims[0],), (dims[1],)), ((), ())), preferred_element_type=F32
    )


def gelu(v):
    return 0.5 * v * (1.0 + lax.erf(v * 0.7071067811865476))


def gelu_and_slope(v):
    share = 0.5 * (1.0 + lax.erf(v * 0.7071067811865476))
    return v * share, share + v * jnp.exp(-0.5 * v * v) * 0.3989422804014327


def norm(v):
    centred = v - jnp.mean(v, axis=-1, keepdims=True)
    spread = jnp.mean(centred * centred, axis=-1, keepdims=True)
    inverse = lax.rsqrt(spread + 1e-06)
    return centred * inverse, inverse


def norm_back(incoming, scaled, inverse, gain):
    weighted = incoming * gain
    inner = (
        weighted
        - jnp.mean(weighted, axis=-1, keepdims=True)
        - scaled * jnp.mean(weighted * scaled, axis=-1, keepdims=True)
    )
    return inverse * inner, jnp.sum(incoming * scaled, axis=0, keepdims=True)


def grid_place(shape, axis, offset):
    index = (lax.broadcasted_iota(jnp.int32, shape, axis) + offset).astype(F32)
    row = jnp.floor((index + 0.5) * (1.0 / GW))
    return row, index - GW * row


def cell_mask(shape, axis, offset, length):
    row, col = grid_place(shape, axis, offset)
    large = length == SLOTS
    height = jnp.where(large, float(GH), float(SH))
    breadth = jnp.where(large, float(GW), float(SW))
    return jnp.where((row < height) & (col < breadth), 1.0, 0.0)


class Peers:
    def __init__(self):
        self.dp = lax.axis_index("dp")
        self.n = lax.axis_size("dp")
        self.t = lax.axis_index("tensor")
        self.sib = self.t + 1 - 2 * lax.rem(self.t, 2)
        self.xp = lax.rem(self.t + 2, 4)
        self.diag = lax.rem(self.sib + 2, 4)

    def bit(self, at):
        return lax.rem(self.dp // (1 << at), 2)

    def mate(self, at):
        return self.dp + (1 - 2 * self.bit(at)) * (1 << at)

    def bits(self):
        return self.n.bit_length() - 1

    def greet(self, bits=0):
        barrier = pltpu.get_barrier_semaphore()
        others = [(self.dp, self.sib), (self.dp, self.xp)]
        if bits >= 3:
            low = lax.rem(self.dp, 8)
            others += [
                (self.dp + lax.rem(low + k, 8) - low, self.t) for k in range(1, 8)
            ]
            bits_from = 3
        else:
            bits_from = 0
        others += [(self.mate(at), self.t) for at in range(bits_from, bits)]
        for other in others:
            pl.semaphore_signal(barrier, inc=1, device_id=other, device_id_type=MESH)
        pl.semaphore_wait(barrier, len(others))


class Links:
    def __init__(self, send, recv):
        self.send, self.recv, self.used = send, recv, 0

    def copy(self, src, dst, device):
        at = self.used
        self.used += 1
        return pltpu.make_async_remote_copy(
            src_ref=src,
            dst_ref=dst,
            send_sem=self.send.at[at],
            recv_sem=self.recv.at[at],
            device_id=device,
            device_id_type=MESH,
        )


class Gather:
    def __init__(self, links, peers, place):
        p = peers
        self.x = links.copy(place(p.t), place(p.t), (p.dp, p.xp))
        self.c = links.copy(place(p.t), place(p.t), (p.dp, p.sib))
        self.f = links.copy(place(p.xp), place(p.xp), (p.dp, p.sib))

    def start(self, clock=None, size=0):
        self.x.start()
        self.c.start()
        if clock is not None:
            clock.later(clock.flight("x", size), self.forward)

    def forward(self):
        self.x.wait_recv()
        self.f.start()

    def finish(self):
        self.c.wait_recv()
        self.f.wait_recv()
        self.x.wait_send()
        self.c.wait_send()
        self.f.wait_send()


class Swap:
    def __init__(self, links, peers, far, near, place):
        p = peers
        self.x = links.copy(far, place(p.t), (p.dp, p.xp))
        self.c = links.copy(near, place(p.t), (p.dp, p.sib))
        self.f = links.copy(place(p.xp), place(p.xp), (p.dp, p.sib))

    start, forward, finish = Gather.start, Gather.forward, Gather.finish


PIECES = ((0, 160), (160, PART - 160))


class Scatter:
    def __init__(self, links, peers, out_c, out_x, in_c, in_x, mine):
        p = peers
        self.p, self.out_c, self.out_x, self.in_c, self.in_x = p, out_c, out_x, in_c, in_x
        self.mine = mine
        self.c = [links.copy(out_c.at[i], in_c.at[i], (p.dp, p.sib)) for i in range(2)]
        self.x = [
            links.copy(out_x.at[pl.ds(*piece), :], in_x.at[pl.ds(*piece), :], (p.dp, p.xp))
            for piece in PIECES
        ]

    def far(self, part, clock=None, cost=0.0):
        p = self.p
        self.lands = []
        self.out_c[0] = part(p.diag).astype(BF16)
        self.c[0].start()
        self.mine[...] = part(p.xp)
        if clock is not None:
            clock.work(cost)
            clock.until(clock.flight("core", PART * D * 2))
        self.c[0].wait_recv()
        for copy, piece in zip(self.x, PIECES):
            rows = pl.ds(*piece)
            self.out_x[rows, :] = (self.mine[rows, :] + self.in_c[0, rows, :].astype(F32)).astype(
                BF16
            )
            copy.start()
            if clock is not None:
                self.lands.append(clock.flight("x", piece[1] * D * 2))

    def near(self, part, clock=None, cost=0.0):
        p = self.p
        self.out_c[1] = part(p.sib).astype(BF16)
        self.c[1].start()
        self.mine[...] = part(p.t)
        if clock is not None:
            clock.work(cost)
            clock.until(clock.flight("core", PART * D * 2))
        self.c[1].wait_recv()
        self.mine[...] += self.in_c[1].astype(F32)

    def piece(self, at, clock=None):
        rows = pl.ds(*PIECES[at])
        if clock is not None:
            clock.until(self.lands[at])
        self.x[at].wait_recv()
        return self.mine[rows, :] + self.in_x[rows, :].astype(F32)

    def finish(self):
        for copy in self.c + self.x:
            copy.wait_send()


class Clock:
    RATES = {"core": 400e3, "zz": 23e3, "z4": 8.7e3, "all": 4.3e3}

    def __init__(self):
        self.now, self.free, self.queue, self.count = 0.0, {}, [], 0

    def flight(self, axis, size):
        took = size / self.RATES.get(axis, 46e3)
        lines = {"zz": ("zz", "z"), "z4": ("z", "zz"), "all": ("y", "z", "zz")}.get(axis, (axis,))
        start = max(self.now, self.free.get(lines[0], 0.0))
        for line in lines:
            part = {("zz", "z"): 0.5, ("all", "y"): 0.5, ("z4", "z"): 0.75}.get(
                (axis, line), 1.0
            ) * took
            self.free[line] = max(self.now, self.free.get(line, 0.0)) + part
        return start + took + (1.0 if axis == "core" else 4.0)

    def later(self, when, act):
        self.queue.append((when, self.count, act))
        self.count += 1

    def work(self, took):
        self.now += took
        while self.queue and min(self.queue)[0] <= self.now:
            first = min(self.queue)
            self.queue.remove(first)
            first[2]()

    def until(self, when):
        while self.queue and min(self.queue)[0] <= when:
            self.work(max(min(self.queue)[0] - self.now, 0.0))
        self.now = max(self.now, when)

    def drain(self):
        while self.queue:
            self.work(max(min(self.queue)[0] - self.now, 0.0))


Y, Z, ZZ, Z4, ALL = ("y", 0, 2), ("z", 1, 2), ("zz", 2, 2), ("z4", 1, 4), ("all", 0, 8)


class Halver:
    def __init__(self, links, peers, clock, array, arrive, result, stages, after=0):
        p = self.p = peers
        self.links, self.clock, self.array, self.arrive = links, clock, array, arrive
        self.result, self.stages = result, stages
        self.rows, self.columns = array.shape
        self.at = self.fresh = after
        base, size, slot = 0, self.rows, 0
        self.keep, self.give, self.land, self.to = [], [], [], []
        for _, low, count in stages:
            size //= count
            mine = lax.rem(p.dp // (1 << low), count)
            give, land, to = [], [], []
            for k in range(1, count):
                other = lax.rem(mine + k, count)
                give.append(pl.ds(pl.multiple_of(base + other * size, 16), size))
                land.append(pl.ds(slot, size))
                to.append((p.dp + (other - mine) * (1 << low), p.t))
                slot += size
            base = base + mine * size
            self.give.append(give)
            self.land.append(land)
            self.to.append(to)
            self.keep.append(pl.ds(pl.multiple_of(base, 16), size))
        self.size, self.slot = size, slot
        self.sent, self.rs, self.ag = [], {}, {}

    def send(self, k, copies):
        for copy in copies:
            copy.start()
        self.sent.extend(copies)
        size = self.keep[k].size * self.columns * 2
        self.clock.later(self.clock.flight(self.stages[k][0], size), self.step)

    def s(self, k):
        self.rs[k] = [
            self.links.copy(self.array.at[give, :], self.arrive.at[land, :], to)
            for give, land, to in zip(self.give[k], self.land[k], self.to[k])
        ]
        self.send(k, self.rs[k])

    def add(self, lands, keep):
        total = self.array[keep, :].astype(F32)
        for land in lands:
            total = total + self.arrive[land, :].astype(F32)
        self.array[keep, :] = total.astype(BF16)

    def a(self, k):
        for copy in self.rs[k]:
            copy.wait_recv()
        self.add(self.land[k], self.keep[k])
        if k == len(self.stages) - 1:
            for extra in range(3, self.p.bits()):
                land = pl.ds(self.slot + (extra - 3) * self.size, self.size)
                copy = self.links.copy(
                    self.array.at[self.keep[k], :], self.arrive.at[land, :],
                    (self.p.mate(extra), self.p.t),
                )
                copy.start()
                copy.wait_recv()
                copy.wait_send()
                self.add([land], self.keep[k])

    def g(self, k):
        region = self.keep[k]
        if k == len(self.stages) - 1:
            self.result[region, :] = self.array[region, :]
        self.ag[k] = [
            self.links.copy(self.result.at[region, :], self.result.at[region, :], to)
            for to in self.to[k]
        ]
        self.send(k, self.ag[k])

    def step(self):
        at, last = self.at, len(self.stages)
        if at <= last:
            if at > self.fresh:
                self.a(at - 1)
                self.fresh = at
            if at < last:
                self.s(at)
            elif self.result is None:
                return
            else:
                self.g(last - 1)
        else:
            k = 2 * last - at
            for copy in self.ag[k].copy():
                copy.wait_recv()
            if k:
                self.g(k - 1)
        self.at += 1

    def done(self):
        return self.at > 2 * len(self.stages)

    def level(self):
        if self.at > self.fresh:
            self.a(self.at - 1)
            self.fresh = self.at
        return self.fresh

    def finish(self):
        for copy in self.sent:
            copy.wait_send()


class Fetch:
    def __init__(self, links, peers, clock, source, place, size, after=None):
        p = self.p = peers
        self.clock, self.size, self.after = clock, size, after
        quarter = lax.rem(p.dp, 4)
        pair = quarter - lax.rem(quarter, 2)
        self.x = links.copy(source(quarter), place(p.t, quarter, 1), (p.dp, p.xp))
        mine = place(p.xp, quarter, 1)
        self.one = links.copy(mine, mine, (p.mate(0), p.t))
        both = place(p.xp, pair, 2)
        self.two = links.copy(both, both, (p.mate(1), p.t))

    def start(self):
        self.x.start()
        self.clock.later(self.clock.flight("x", self.size), self.swap)

    def swap(self):
        self.x.wait_recv()
        self.one.start()
        self.clock.later(self.clock.flight("y", self.size), self.trade)

    def trade(self):
        self.one.wait_recv()
        self.two.start()
        self.clock.later(self.clock.flight("z", 2 * self.size), self.end)

    def end(self):
        self.two.wait_recv()
        if self.after is not None:
            self.after()

    def finish(self):
        self.x.wait_send()
        self.one.wait_send()
        self.two.wait_send()


def landing(rows, columns, bits):
    return pltpu.VMEM((rows + max(bits - 4, 0) * (rows // 8), columns), BF16)


class Doubler:
    def __init__(self, links, peers, outgoing, incoming):
        p = peers
        self.links, self.outgoing, self.incoming = links, outgoing, incoming
        self.to = [(p.dp, p.sib), (p.dp, p.xp)] + [(p.mate(at), p.t) for at in range(p.bits())]
        self.copies = []

    def start(self, value):
        self.value = value
        self.send()

    def send(self):
        at = len(self.copies)
        if at < len(self.to):
            self.outgoing[at] = self.value
            copy = self.links.copy(self.outgoing.at[at], self.incoming.at[at], self.to[at])
            copy.start()
            self.copies.append(copy)

    def step(self):
        at = len(self.copies) - 1
        self.copies[at].wait_recv()
        self.value = self.value + self.incoming[at]
        self.send()

    def finish(self):
        while len(self.copies) < len(self.to):
            self.step()
        self.copies[-1].wait_recv()
        self.value = self.value + self.incoming[len(self.to) - 1]
        for copy in self.copies:
            copy.wait_send()
        return self.value


def sems(count):
    return [pltpu.SemaphoreType.DMA((count,)), pltpu.SemaphoreType.DMA((count,))]


def part_at(ref, owner):
    return ref.at[pl.ds(pl.multiple_of(owner * PART, 16), PART), :]


def piece_at(ref, owner, piece):
    return ref.at[pl.ds(pl.multiple_of(owner * PART + piece[0], 16), piece[1]), :]


def upsample_table(count):
    shape = (2 * count, count)
    target = lax.broadcasted_iota(jnp.int32, shape, 0)
    source = lax.broadcasted_iota(jnp.int32, shape, 1)
    nearest = lax.shift_right_logical(target, 1)
    odd = target - 2 * nearest
    further = jnp.clip(nearest + 2 * odd - 1, 0, count - 1)
    return jnp.where(source == nearest, 0.75, 0.0) + jnp.where(source == further, 0.25, 0.0)


def split_dot(a, table):
    high = a.astype(BF16)
    low = (a - high.astype(F32)).astype(BF16)
    return dot(high, table) + dot(low, table)


def call(kernel, outs, ins, scratch, collective, flops, args, places=None):
    return pl.pallas_call(
        kernel,
        out_shape=[jax.ShapeDtypeStruct(*o) for o in outs],
        in_specs=ins,
        out_specs=places or [vmem] * len(outs),
        scratch_shapes=scratch,
        cost_estimate=pl.CostEstimate(
            flops=flops, bytes_accessed=20_000_000, transcendentals=0
        ),
        compiler_params=pltpu.CompilerParams(
            collective_id=collective,
            has_side_effects=True,
            vmem_limit_bytes=VMEM_LIMIT,
        )
        if collective is not None
        else pltpu.CompilerParams(vmem_limit_bytes=VMEM_LIMIT),
    )(*args)


def front_kernel(
    levels, length, tok_hbm, gain_one, gain_two, w_qkv, w_out, w_tap, w_conv, w_up_hbm, w_down_hbm,
    cot_field_hbm, cot_hbm,
    hidden_own_, normed_two_, q_cm_, k_tm_, v_tm_, k_cm_, lse_, mixed_, normed_one_, slope_, act_,
    tap_all, out_all, out_own, field, conv_all, grad_own, down_part,
    hidden_own, normed_two, q_cm, k_tm, v_tm, k_cm, lse, mixed, normed_one, slope, act, down_arrive,
    tok, hidden, mixed_all, out_heads, v_cm, w_up, w_down, cot_field, cot,
    out_c, out_x, in_c, in_x, mine, tall, local, send, recv,
):
    p = Peers()
    links = Links(send, recv)
    bring = pltpu.make_async_copy(tok_hbm, tok.at[pl.ds(0, SLOTS), :], local.at[0])
    bring.start()
    late = [
        pltpu.make_async_copy(w_up_hbm, w_up, local.at[1]),
        pltpu.make_async_copy(w_down_hbm, w_down, local.at[2]),
        pltpu.make_async_copy(cot_field_hbm, cot_field, local.at[3]),
        pltpu.make_async_copy(cot_hbm, cot.at[pl.ds(0, SLOTS), :], local.at[4]),
    ]
    tok[SLOTS:, :] = jnp.zeros((LANES - SLOTS, D), BF16)
    cot[SLOTS:, :] = jnp.zeros((ROWS - SLOTS, D), BF16)
    place_out = lambda t: out_all.at[pl.ds(pl.multiple_of(t * 192, 64), 192), :]
    place_tap = lambda t: tap_all.at[pl.ds(pl.multiple_of(t * 64, 64), 64), :]
    place_out(p.t)[...] = w_out[...]
    place_tap(p.t)[...] = w_tap[...]
    clock = Clock()
    p.greet(p.bits())
    c_near = [links.copy(place(p.t), place(p.t), (p.dp, p.sib)) for place in (place_out, place_tap)]
    c_far = [links.copy(place(p.xp), place(p.xp), (p.dp, p.sib)) for place in (place_out, place_tap)]
    f_out = Fetch(
        links, p, clock, lambda q: w_out.at[pl.ds(pl.multiple_of(q * 48, 16), 48), :],
        lambda t, q, n: out_all.at[pl.ds(pl.multiple_of(t * 192 + q * 48, 16), n * 48), :],
        48 * D * 2, c_far[0].start,
    )
    f_tap = Fetch(
        links, p, clock, lambda q: w_tap.at[pl.ds(pl.multiple_of(q * 16, 16), 16), :],
        lambda t, q, n: tap_all.at[pl.ds(pl.multiple_of(t * 64 + q * 16, 16), n * 16), :],
        16 * D * 2, c_far[1].start,
    )
    f_conv = Fetch(
        links, p, clock, lambda q: w_conv.at[pl.ds(q, 1)],
        lambda t, q, n: conv_all.at[pl.ds(q, n)], WIDE * CH * 2,
    )
    f_out.start()
    f_tap.start()
    f_conv.start()
    for c in c_near:
        c.start()
    writes = []

    def write(*arrays):
        for src, dst in arrays:
            copy = pltpu.make_async_copy(src, dst, local.at[5 + len(writes)])
            copy.start()
            writes.append(copy)

    bring.wait()
    for copy in late:
        copy.start()
    gain = gain_one[...].reshape(1, D)
    lane = lax.broadcasted_iota(jnp.int32, (CHUNK, SLOT), 1)
    one_row = jnp.where(
        lax.broadcasted_iota(jnp.int32, (HEAD_DIM, CHUNK), 0) == 0, 1.0, 0.0
    ).astype(BF16)

    def project(i, carry):
        off = pl.multiple_of(i * CHUNK, CHUNK)
        rows = pl.ds(off, CHUNK)
        scaled, _ = norm(tok[rows, :].astype(F32))
        normed = (scaled * gain).astype(BF16)
        normed_one[rows, :] = normed
        bias = jnp.where(cell_mask((CHUNK, SLOT), 0, off, length[0]) > 0.5, 0.0, -1e30)
        bias = jnp.where(lane == HEAD_DIM, bias, 0.0).astype(BF16)
        qkv = dot(w_qkv[...], normed, (1, 1)).astype(BF16)
        for h in range(3):
            near = slice(h * HEAD_DIM, (h + 1) * HEAD_DIM)
            q_cm[h, 0:HEAD_DIM, rows] = (qkv[near].astype(F32) * 0.125).astype(BF16)
            q_cm[h, HEAD_DIM:, rows] = one_row
            k = qkv[192 + h * HEAD_DIM : 192 + (h + 1) * HEAD_DIM]
            k_cm[near, rows] = k
            k_tm[h, rows, :] = bias
            k_tm[h, rows, 0:HEAD_DIM] = k.T
            v = qkv[384 + h * HEAD_DIM : 384 + (h + 1) * HEAD_DIM]
            v_cm[h, 0:HEAD_DIM, rows] = v
            v_cm[h, HEAD_DIM:, rows] = one_row[0:16]
            v_tm[h, rows, :] = v.T
        return carry

    lax.fori_loop(0, LANES // CHUNK, project, 0)
    write((q_cm, q_cm_), (k_tm, k_tm_), (v_tm, v_tm_), (k_cm, k_cm_), (normed_one, normed_one_))
    clock.work(4.0)
    chunks = [(h, c) for h in range(3) for c in range(LANES // CHUNK)]

    def scores(h, c):
        return dot(k_tm[h, 0:ROWS, :], q_cm[h, :, c * CHUNK : (c + 1) * CHUNK])

    def mixed_at(t, h, lanes):
        return mixed_all.at[
            pl.ds(pl.multiple_of(h * CH + t * HEAD_DIM, HEAD_DIM), HEAD_DIM), lanes
        ]

    def gather(h, lanes):
        g = Gather(links, p, lambda t: mixed_at(t, h, lanes))
        g.start(clock, (lanes.stop - lanes.start) * HEAD_DIM * 2)
        gathers.append(g)

    gathers = []
    ahead = scores(0, 0)
    for at, (h, c) in enumerate(chunks):
        s = ahead
        if at + 1 < len(chunks):
            ahead = scores(*chunks[at + 1])
        heads = slice(h * HEAD_DIM, (h + 1) * HEAD_DIM)
        lanes = slice(c * CHUNK, (c + 1) * CHUNK)
        top = jnp.max(s, axis=0, keepdims=True)
        out = dot(v_cm[h, :, 0:ROWS], jnp.exp(s - top).astype(BF16))
        total = out[HEAD_DIM : HEAD_DIM + 1]
        out = (out[0:HEAD_DIM] * (1.0 / total)).astype(BF16)
        lse[h : h + 1, lanes] = top + jnp.log(total)
        mixed[heads, lanes] = out
        mixed_at(p.t, h, lanes)[...] = out
        if c == 4:
            gather(h, slice(0 if h < 2 else 4 * CHUNK, LANES))
        elif h == 2 and c % 2:
            gather(h, slice((c - 1) * CHUNK, (c + 1) * CHUNK))
        clock.work(0.6)
    write((lse, lse_), (mixed, mixed_))
    while any(act_[2] in waited for act_ in clock.queue for waited in ((f_out.swap, f_out.trade, f_out.end, f_tap.swap, f_tap.trade, f_tap.end, gathers[0].forward, gathers[1].forward),)):
        clock.work(0.3)
    for c in c_near + c_far:
        c.wait_recv()
    for far in range(4):
        for k in range(3):
            out_heads[k * CH + far * HEAD_DIM : k * CH + (far + 1) * HEAD_DIM, :] = out_all[
                far * 192 + k * HEAD_DIM : far * 192 + (k + 1) * HEAD_DIM, :
            ]
    gathers[0].finish()
    gathers[1].finish()
    clock.work(0.5)

    def begin(i, carry):
        rows = pl.ds(pl.multiple_of(i * CHUNK, CHUNK), CHUNK)
        branch = dot(mixed_all[0 : 2 * CH, rows], out_heads[0 : 2 * CH, :], (0, 0))
        hidden[rows, :] = tok[rows, :].astype(F32) + branch
        return carry

    lax.fori_loop(0, LANES // CHUNK, begin, 0)
    clock.work(2.0)
    while any(act_[2] in [g.forward for g in gathers] for act_ in clock.queue):
        clock.work(0.3)
    for g in gathers[2:]:
        g.finish()
    gain_after = gain_two[...].reshape(1, D)

    def finish(i, carry):
        rows = pl.ds(pl.multiple_of(i * CHUNK, CHUNK), CHUNK)
        after = hidden[rows, :] + dot(
            mixed_all[2 * CH : 3 * CH, rows], out_heads[2 * CH : 3 * CH, :], (0, 0)
        )
        hidden[rows, :] = after
        scaled, _ = norm(after)
        normed_two[rows, :] = (scaled * gain_after).astype(BF16)
        return carry

    lax.fori_loop(0, LANES // CHUNK, finish, 0)
    hidden_own[...] = hidden[pl.ds(pl.multiple_of(p.t * PART, 16), PART), :]
    write((hidden_own, hidden_own_), (normed_two, normed_two_))
    clock.work(2.5)
    for copy in late:
        copy.wait()

    def part(owner):
        rows = pl.ds(pl.multiple_of(owner * PART, 16), PART)
        activation, steep = gelu_and_slope(dot(normed_two[rows, :], w_up[...]))
        activation = activation.astype(BF16)
        slope[rows, :] = steep.astype(BF16)
        act[rows, :] = activation
        return dot(activation, w_down[...])

    sums = Scatter(links, p, out_c, out_x, in_c, in_x, mine)
    sums.far(part, clock, 1.7)
    sums.near(part, clock, 1.7)
    write((slope, slope_), (act, act_))
    h_down = [
        Halver(links, p, clock, down_part.at[i], down_arrive.at[i], None, (Y, Z, ZZ))
        for i in range(2)
    ]
    for i in range(4):
        rows = slice(i * PART, (i + 1) * PART)
        cot[rows, :] = (
            cell_mask((PART, D), 0, i * PART, length[0]) * cot[rows, :].astype(F32)
        ).astype(BF16)
    for i in range(2):
        cols = slice(i * (D // 2), (i + 1) * (D // 2))
        down_part[i] = dot(act[:, cols], cot[...], (0, 0)).astype(BF16)
        h_down[i].step()
        clock.work(0.8)
    lower(cot_field, grad_own, tall, upsample_table(GW).astype(BF16))
    gathers = []
    for at, piece in enumerate(PIECES):
        total = sums.piece(at, clock)
        off = pl.multiple_of(p.t * PART + piece[0], 16)
        mask = cell_mask((piece[1], D), 0, off, length[0])
        out = (mask * (hidden_own[pl.ds(*piece), :] + total)).astype(BF16)
        out_own[pl.ds(*piece), :] = out
        field[pl.ds(off, piece[1]), :] = dot(out, tap_all[...], (1, 1)).astype(BF16)
        g = Gather(links, p, lambda t: piece_at(field, t, piece))
        g.start(clock, piece[1] * CH * 2)
        gathers.append(g)
        clock.work(0.5)
    while any(act_[2] in [g.forward for g in gathers] for act_ in clock.queue):
        clock.work(0.3)
    while any(act_[2] in (f_conv.swap, f_conv.trade, f_conv.end) for act_ in clock.queue):
        clock.work(0.3)
    for g in gathers:
        g.finish()
    levels["down"] = [h.level() for h in h_down]
    sums.finish()
    for c in c_near + c_far:
        c.wait_send()
    for f in (f_out, f_tap, f_conv):
        f.finish()
    for h in h_down:
        h.finish()
    for copy in writes:
        copy.wait()


def front_call(bits, levels, *args):
    kept = [
        ((PART, D), F32),
        ((LANES, D), BF16),
        ((3, SLOT, LANES), BF16),
        ((3, LANES, SLOT), BF16),
        ((3, LANES, HEAD_DIM), BF16),
        ((192, LANES), BF16),
        ((8, LANES), F32),
        ((192, LANES), BF16),
        ((LANES, D), BF16),
        ((ROWS, D), BF16),
        ((ROWS, D), BF16),
    ]
    outs = kept + [
        ((CH, D), BF16),
        ((D, D), BF16),
        ((PART, D), BF16),
        ((ROWS, CH), BF16),
        ((4, WIDE, CH), BF16),
        ((BLOCK, LANES), F32),
        ((2, D // 2, D), BF16),
    ]
    scratch = [pltpu.VMEM(*k) for k in kept] + [
        pltpu.VMEM((2,) + landing(D // 2, D, bits).shape, BF16),
        pltpu.VMEM((LANES, D), BF16),
        pltpu.VMEM((LANES, D), F32),
        pltpu.VMEM((D, LANES), BF16),
        pltpu.VMEM((D, D), BF16),
        pltpu.VMEM((3, HEAD_DIM + 16, LANES), BF16),
        pltpu.VMEM((D, D), BF16),
        pltpu.VMEM((D, D), BF16),
        pltpu.VMEM((2 * GH, BLOCK, 2 * GW), BF16),
        pltpu.VMEM((ROWS, D), BF16),
    ] + scatter_scratch() + [
        pltpu.VMEM((GH * BLOCK, 2 * GW), F32),
        pltpu.SemaphoreType.DMA((5 + len(kept),)),
    ] + sems(70)
    return call(
        functools.partial(front_kernel, levels), outs,
        [smem, anywhere] + [vmem] * 5 + [anywhere] * 5, scratch, 0, 14_000_000_000, args,
        [anywhere] * len(kept) + [vmem] * 7,
    )


def lower(cot, grad, tall, table):
    grad[:, SLOTS:] = jnp.zeros((BLOCK, LANES - SLOTS), F32)
    for a in range(GH):
        mid = 0.75 * (cot[2 * a].astype(F32) + cot[2 * a + 1].astype(F32))
        before = cot[max(2 * a - 1, 0)].astype(F32)
        after = cot[min(2 * a + 2, 2 * GH - 1)].astype(F32)
        tall[a * BLOCK : (a + 1) * BLOCK, :] = mid + 0.25 * (before + after)
    for a in range(GH):
        grad[:, a * GW : (a + 1) * GW] = split_dot(tall[a * BLOCK : (a + 1) * BLOCK, :], table)


def scatter_scratch():
    return [
        pltpu.VMEM((2, PART, D), BF16),
        pltpu.VMEM((PART, D), BF16),
        pltpu.VMEM((2, PART, D), BF16),
        pltpu.VMEM((PART, D), BF16),
        pltpu.VMEM((PART, D), F32),
    ]


def conv_kernel(
    levels, length, field, w_own, w_far, grad_own, out_own, down_hbm,
    result, tap_grad, g_conv, out_all, down,
    start_all, state, steep_first, steep_state, x_all, wide, flip, dcol, back, grad, grad_far,
    grad_near, back_out, back_in, arrive, down_part, down_arrive, local, send, recv,
):
    p = Peers()
    links = Links(send, recv)
    clock = Clock()
    bring = pltpu.make_async_copy(down_hbm, down_part, local.at[0])
    bring.start()
    p.greet(p.bits())
    weights = (w_own, w_far)
    block_of = (p.t, p.xp)
    at = lambda t: pl.ds(pl.multiple_of(t * BLOCK, BLOCK), BLOCK)

    part_at(out_all, p.t)[...] = out_own[...]
    out_all[ROWS:, :] = jnp.zeros((LANES - ROWS, D), BF16)
    g_out = Gather(links, p, lambda t: part_at(out_all, t))
    grad_near[...] = grad_own[...].astype(BF16)
    c_grad = links.copy(grad_near, grad_far, (p.dp, p.xp))
    c_grad.start()
    halvers = {
        j: Halver(links, p, clock, g_conv.at[j], arrive.at[j], None, ORDERS[j]) for j in (3, 2, 1)
    }
    h_down = [
        Halver(
            links, p, clock, down_part.at[i], down_arrive.at[i], down.at[i], (Y, Z, ZZ),
            levels["down"][i],
        )
        for i in range(2)
    ]
    bring.wait()
    for h in h_down:
        h.step()

    def masks(count):
        _, col = grid_place((count, LANES), 1, 0)
        not_first = jnp.where(col > 0.5, 1.0, 0.0)
        not_last = jnp.where(col < GW - 1.5, 1.0, 0.0)
        return cell_mask((count, LANES), 1, 0, length[0]), not_first, not_last

    _, not_first8, not_last8 = masks(8)
    cells16, not_first16, not_last16 = masks(16)
    not_first16, not_last16 = not_first16.astype(BF16), not_last16.astype(BF16)

    start_all[:, ROWS:] = jnp.zeros((CH, LANES - ROWS), F32)
    start_all[:, 0:ROWS] = field[...].astype(F32).T

    def rows_at(i):
        return pl.ds(pl.multiple_of(i * 16, 16), 16)

    def into_at(b, i):
        return pl.ds(pl.multiple_of(block_of[b] * BLOCK + i * 16, 16), 16)

    def open_rows(i, carry):
        x_all[0, rows_at(i), :] = gelu(start_all[rows_at(i), :]).astype(BF16)
        return carry

    lax.fori_loop(0, CH // 16, open_rows, 0)
    clock.work(2.0)

    def convolve(index, b, use):
        for c in range(LANES // CHUNK):
            lanes = slice(c * CHUNK, (c + 1) * CHUNK)
            wide[:, lanes] = dot(weights[b][index], x_all[index, :, lanes])

        def rows16(i, carry):
            halves = []
            for half in range(2):
                total = None
                for q in range(3):
                    tap = lambda r: wide[
                        pl.ds(pl.multiple_of((r * 3 + q) * BLOCK + i * 16 + half * 8, 8), 8), :
                    ]
                    three = (
                        tap(1)
                        + pltpu.roll(tap(0), GW, 1)
                        + pltpu.roll(tap(2), LANES - GW, 1)
                    )
                    if q == 0:
                        three = pltpu.roll(three, 1, 1) * not_first8
                    if q == 2:
                        three = pltpu.roll(three, LANES - 1, 1) * not_last8
                    total = three if total is None else total + three
                halves.append(total)
            use(i, cells16 * jnp.concatenate(halves, axis=0))
            return carry

        lax.fori_loop(0, BLOCK // 16, rows16, 0)
        clock.work(2.2)

    pending = []

    def share(array, b):
        place = array.at[at(block_of[b]), :]
        copy = links.copy(place, place, (p.dp, p.sib))
        copy.start()
        pending.append(copy)
        return copy

    def settle(copies):
        for c in copies:
            c.wait_recv()
        clock.work(1.0)

    def first_conv(unit):
        copies = []
        for b in range(2):
            def use(i, value, b=b):
                low, steep = gelu_and_slope(value)
                x_all[2 * unit + 1, into_at(b, i), :] = low.astype(BF16)
                steep_first[unit, b, rows_at(i), :] = steep

            convolve(2 * unit, b, use)
            copies.append(share(x_all.at[2 * unit + 1], b))
        return copies

    def spread(turn, b, value_of):
        def rows16(i, carry):
            value = value_of(i).astype(BF16)
            for q in range(3):
                side = value
                if q == 0:
                    side = pltpu.roll(value, LANES - 1, 1) * not_last16
                if q == 2:
                    side = pltpu.roll(value, 1, 1) * not_first16
                for r in range(3):
                    moved = side
                    if r == 0:
                        moved = pltpu.roll(side, LANES - GW, 1)
                    if r == 2:
                        moved = pltpu.roll(side, GW, 1)
                    into = pl.ds(pl.multiple_of((r * 3 + q) * BLOCK + i * 16, 16), 16)
                    dcol[turn % 2, b, into, :] = moved
            return carry

        lax.fori_loop(0, BLOCK // 16, rows16, 0)
        clock.work(0.8)

    def conv_back(turn):
        index = 3 - turn
        flip[0] = w_own[index].T
        flip[1] = w_far[index].T
        for c in range(LANES // CHUNK):
            lanes = slice(c * CHUNK, (c + 1) * CHUNK)
            back[:, lanes] = dot(flip[0], dcol[turn % 2, 0, :, lanes]) + dot(
                flip[1], dcol[turn % 2, 1, :, lanes]
            )
        copies = []
        for b, t in enumerate((p.sib, p.diag)):
            back_out[turn, b] = back[at(t), :].astype(BF16)
            c = links.copy(back_out.at[turn, b], back_in.at[turn, b], (p.dp, p.sib))
            c.start()
            copies.append(c)
        pending.extend(copies)
        clock.work(1.3)
        return copies

    def summed(turn, b, i):
        return back[into_at(b, i), :] + back_in[turn, b, rows_at(i), :].astype(F32)

    def weight_grad(turn):
        index = 3 - turn
        found = dot(dcol[turn % 2, 0], x_all[index], (1, 1)).astype(BF16)
        g_conv[index, 0:WIDE, :] = found[:, 0:SLOT]
        g_conv[index, WIDE:, :] = found[:, SLOT:]

    coming = first_conv(0)
    for b in range(2):
        def opening(i, carry, b=b):
            value = start_all[into_at(b, i), :]
            state[b, rows_at(i), :] = value
            steep_state[0, b, rows_at(i), :] = gelu_and_slope(value)[1]
            return carry

        lax.fori_loop(0, BLOCK // 16, opening, 0)
    clock.work(1.0)
    c_grad.wait_recv()
    g_out.start()
    grad[0] = grad_own[...]
    grad[1] = grad_far[...].astype(F32)
    for b in range(2):
        spread(0, b, lambda i, b=b: cells16 * grad[b, rows_at(i), :])
    settle(coming)
    coming = []
    for b in range(2):
        def use_second(i, value, b=b):
            fresh = state[b, rows_at(i), :] + value
            low, steep = gelu_and_slope(fresh)
            state[b, rows_at(i), :] = fresh
            x_all[2, into_at(b, i), :] = low.astype(BF16)
            steep_state[1, b, rows_at(i), :] = steep

        convolve(1, b, use_second)
        coming.append(share(x_all.at[2], b))
    backs = conv_back(0)
    settle(coming)
    coming = first_conv(1)
    settle(backs)
    for b in range(2):
        spread(
            1, b, lambda i, b=b: cells16 * summed(0, b, i) * steep_first[1, b, rows_at(i), :]
        )
    settle(coming)
    backs = conv_back(1)
    weight_grad(0)
    halvers[3].step()

    def use_last(i, value):
        result[rows_at(i), :] = state[0, rows_at(i), :] + value

    convolve(3, 0, use_last)
    weight_grad(1)
    halvers[2].step()
    clock.work(0.8)
    settle(backs)
    for b in range(2):
        def renewed(i, b=b):
            fresh = grad[b, rows_at(i), :] + summed(1, b, i) * steep_state[1, b, rows_at(i), :]
            grad[b, rows_at(i), :] = fresh
            return cells16 * fresh

        spread(2, b, renewed)
    backs = conv_back(2)
    weight_grad(2)
    halvers[1].step()
    clock.work(0.5)
    g_out.forward()
    settle(backs)
    for b in range(2):
        spread(
            3, b, lambda i, b=b: cells16 * summed(2, b, i) * steep_first[0, b, rows_at(i), :]
        )
    backs = conv_back(3)
    weight_grad(3)
    clock.work(0.5)
    inside16 = jnp.where(
        lax.broadcasted_iota(jnp.int32, (16, LANES), 1) < SLOTS, 1.0, 0.0
    )
    settle(backs)
    coming = []
    for b in range(2):
        def close(i, carry, b=b):
            fresh = grad[b, rows_at(i), :] + summed(3, b, i) * steep_state[0, b, rows_at(i), :]
            tap_grad[into_at(b, i), :] = (inside16 * fresh).astype(BF16)
            return carry

        lax.fori_loop(0, BLOCK // 16, close, 0)
        coming.append(share(tap_grad, b))
    settle(coming)
    while not all(h.done() for h in h_down):
        clock.work(0.5)
    levels[0] = 0
    for j, h in halvers.items():
        levels[j] = h.level()
    for c in pending + [c_grad]:
        c.wait_send()
    for h in list(halvers.values()) + h_down:
        h.finish()
    g_out.finish()


FLAT = (2 * WIDE, SLOT)
ORDERS = ((Z, Y, ZZ), (Y, Z, ZZ), (Y, Z, ZZ), (Y, Z, ZZ))


def conv_call(bits, levels, *args):
    outs = [
        ((BLOCK, LANES), F32),
        ((CH, LANES), BF16),
        ((4,) + FLAT, BF16),
        ((LANES, D), BF16),
        ((2, D // 2, D), BF16),
    ]
    scratch = [
        pltpu.VMEM((CH, LANES), F32),
        pltpu.VMEM((2, BLOCK, LANES), F32),
        pltpu.VMEM((2, 2, BLOCK, LANES), F32),
        pltpu.VMEM((2, 2, BLOCK, LANES), F32),
        pltpu.VMEM((4, CH, LANES), BF16),
        pltpu.VMEM((WIDE, LANES), F32),
        pltpu.VMEM((2, CH, WIDE), BF16),
        pltpu.VMEM((2, 2, WIDE, LANES), BF16),
        pltpu.VMEM((CH, LANES), F32),
        pltpu.VMEM((2, BLOCK, LANES), F32),
        pltpu.VMEM((BLOCK, LANES), BF16),
        pltpu.VMEM((BLOCK, LANES), BF16),
        pltpu.VMEM((4, 2, BLOCK, LANES), BF16),
        pltpu.VMEM((4, 2, BLOCK, LANES), BF16),
        pltpu.VMEM((4,) + landing(*FLAT, bits).shape, BF16),
        pltpu.VMEM((2, D // 2, D), BF16),
        pltpu.VMEM((2,) + landing(D // 2, D, bits).shape, BF16),
        pltpu.SemaphoreType.DMA((1,)),
    ] + sems(70)
    return call(
        functools.partial(conv_kernel, levels), outs, [smem] + [vmem] * 5 + [anywhere], scratch,
        2, 9_000_000_000, args,
    )


def lift(field, joined, table, grid_rows):
    for a in grid_rows:
        here = field[:, a * GW : (a + 1) * GW]
        up, down = max(a - 1, 0), min(a + 1, GH - 1)
        for side, other in enumerate((up, down)):
            line = 0.75 * here + 0.25 * field[:, other * GW : (other + 1) * GW]
            joined[2 * a + side] = split_dot(line, table).astype(BF16)


def back_kernel(
    levels, length, tap_grad, tap_all, cot_hbm, slope_, act, normed_two_, w_up_, w_down_, hidden_own_, gain_two,
    out_all_, field_, conv_hbm,
    w_out_, mixed_, q_cm_, k_tm_, v_tm_, k_cm_, lse_, normed_one_, w_qkv_, tok_hbm, gain_one,
    joined, grad_tok, conv, up, low, ot, head, gain_sum,
    slope, normed_two, w_up, w_down, hidden_own,
    out_all, field, w_out, mixed, q_cm, k_tm, v_tm, k_cm, lse, normed_one, w_qkv,
    tok, tap_tm, d_pre, mine_block, grad_hidden, branch, out_c, out_x, in_c, in_x, mine,
    conv_part, up_part, low_part, ot_part, head_part,
    conv_arrive, up_arrive, low_arrive, ot_arrive, head_arrive, gain_out, gain_arrive,
    d_out, d_mix_tm, d_mix_cm, d_mix, acc_k, acc_v, d_cm, d_tm, w_by_head, local, send, recv,
):
    p = Peers()
    links = Links(send, recv)
    clock = Clock()
    bring_conv = pltpu.make_async_copy(conv_hbm, conv_part, local.at[1])
    bring_conv.start()
    soon = [
        pltpu.make_async_copy(src, dst, local.at[2 + len(LATE) + i])
        for i, (src, dst) in enumerate(
            (
                (w_down_, w_down), (slope_, slope), (w_up_, w_up), (normed_two_, normed_two),
                (hidden_own_, hidden_own),
            )
        )
    ]
    late = [
        pltpu.make_async_copy(src, dst, local.at[2 + i])
        for i, (src, dst) in enumerate(
            (
                (out_all_, out_all), (field_, field), (w_out_, w_out), (mixed_, mixed),
                (q_cm_, q_cm), (k_tm_, k_tm), (v_tm_, v_tm), (k_cm_, k_cm), (lse_, lse),
                (normed_one_, normed_one), (w_qkv_, w_qkv),
            )
        )
    ]
    bring = pltpu.make_async_copy(cot_hbm, tok.at[pl.ds(0, SLOTS), :], local.at[0])
    bring.start()
    for copy in soon:
        copy.start()
    tok[SLOTS:, :] = jnp.zeros((ROWS - SLOTS, D), BF16)
    p.greet(p.bits())

    def halver(array, arrive, result, stages, after=0):
        made = Halver(links, p, clock, array, arrive, result, stages, after)
        halvers.append(made)
        return made

    halvers = []
    bring_conv.wait()
    for j in (3, 2, 1, 0):
        halver(conv_part.at[j], conv_arrive.at[j], conv.at[j], ORDERS[j], levels[j]).step()
    half = D // 2
    h_up = [
        halver(up_part.at[i], up_arrive.at[i], up.at[i], (Y, Z, ZZ))
        for i in range(2)
    ]
    h_low = halver(low_part, low_arrive, low, (Y, Z, ZZ))
    h_ot = halver(ot_part, ot_arrive, ot, (Z, Y, ZZ))
    h_head = [
        halver(head_part.at[h], head_arrive.at[h], head.at[h], ((Y, Z, ZZ), (Y, Z, ZZ), (Z, Y, ZZ))[h])
        for h in range(3)
    ]
    gains = Doubler(links, p, gain_out, gain_arrive)

    tap_tm[...] = (
        cell_mask((LANES, CH), 0, 0, length[0]) * tap_grad[...].T.astype(F32)
    ).astype(BF16)
    low_part[...] = dot(act[...], tap_tm[0:ROWS, :], (0, 0)).astype(BF16)
    h_low.step()
    clock.work(1.0)
    bring.wait()
    for copy in soon:
        copy.wait()

    def part(owner):
        off = pl.multiple_of(owner * PART, 16)
        rows = pl.ds(off, PART)
        block = cell_mask((PART, D), 0, off, length[0]) * (
            tok[rows, :].astype(F32) + dot(tap_tm[rows, :], tap_all[...])
        )
        mine_block[...] = block
        steep = (dot(block.astype(BF16), w_down[...], (1, 1)) * slope[rows, :].astype(F32)).astype(BF16)
        d_pre[rows, :] = steep
        return dot(steep, w_up[...], (1, 1))

    for copy in late:
        copy.start()
    sums = Scatter(links, p, out_c, out_x, in_c, in_x, mine)
    sums.far(part, clock, 1.7)
    sums.near(part, clock, 1.7)
    for i in range(2):
        cols = slice(i * half, (i + 1) * half)
        up_part[i] = dot(normed_two[0:ROWS, cols], d_pre[...], (0, 0)).astype(BF16)
        h_up[i].step()
        clock.work(0.8)
    gain = gain_two[...].reshape(1, D)
    for copy in late:
        copy.wait()
    chip = p.t // 2
    near_half = pl.ds(pl.multiple_of(chip * (D // 2), SLOT), D // 2)
    far_half = pl.ds(pl.multiple_of((1 - chip) * (D // 2), SLOT), D // 2)
    swaps = []
    gain_part_two = jnp.zeros((1, D), F32)
    for at, piece in enumerate(PIECES):
        rows = pl.ds(*piece)
        total = sums.piece(at, clock)
        scaled, inverse = norm(hidden_own[rows, :])
        inner, add = norm_back(total, scaled, inverse, gain)
        after = mine_block[rows, :] + inner
        grad_hidden[rows, :] = after
        gain_part_two = gain_part_two + add
        low_after = after.astype(BF16)
        branch[pl.ds(pl.multiple_of(p.t * PART + piece[0], 16), piece[1]), :] = low_after
        d_out[rows, :] = dot(low_after, w_out[...], (1, 1)).astype(BF16)
        piece_at(d_mix_tm, p.t, piece)[...] = d_out[rows, near_half]
        g = Swap(
            links, p, d_out.at[rows, far_half], d_out.at[rows, near_half],
            lambda t: piece_at(d_mix_tm, t, piece),
        )
        g.start(clock, piece[1] * D)
        swaps.append(g)
        clock.work(0.8)
    g_branch = Gather(links, p, lambda t: part_at(branch, t))
    g_branch.start(clock, PART * D * 2)
    sums.finish()
    bring = pltpu.make_async_copy(tok_hbm, tok.at[pl.ds(0, SLOTS), :], local.at[0])
    bring.start()
    table = upsample_table(GW).T.astype(BF16)
    for quarter in range(5):
        lift(field, joined, table, range(quarter * 6, quarter * 6 + 6))
        clock.work(0.4)
    ot_part[192:, :] = dot(
        tap_grad[pl.ds(pl.multiple_of(p.t * BLOCK, BLOCK), BLOCK), :], out_all[...]
    ).astype(BF16)
    for h in range(3):
        for part_at_ in range(3):
            w_by_head[h * 192 + part_at_ * 64 : h * 192 + part_at_ * 64 + 64, :] = w_qkv[
                part_at_ * 192 + h * 64 : part_at_ * 192 + h * 64 + 64, :
            ]
    d_mix_cm[:, ROWS:] = jnp.zeros((D // 2, LANES - ROWS), BF16)
    d_cm[:, ROWS:] = jnp.zeros((3 * 192, LANES - ROWS), BF16)
    clock.work(1.0)
    ahead = [g.forward for g in swaps]
    while any(entry[2] in ahead for entry in clock.queue):
        clock.work(0.3)
    for g in swaps:
        g.finish()
    clock.work(1.0)
    d_mix_cm[:, 0:ROWS] = d_mix_tm[...].T
    d_mix[...] = d_mix_cm[pl.ds(pl.multiple_of(lax.rem(p.t, 2) * 192, 64), 192), :]
    clock.work(0.7)

    def grad_out():
        g_branch.finish()
        ot_part[0:192, :] = dot(mixed[:, 0:ROWS], branch[...]).astype(BF16)
        h_ot.step()
        clock.work(0.5)

    for h in range(3):
        heads = slice(h * HEAD_DIM, (h + 1) * HEAD_DIM)
        for c in range(LANES // CHUNK):
            lanes = slice(c * CHUNK, (c + 1) * CHUNK)
            dm = d_mix[heads, lanes]
            inner = jnp.sum(
                dm.astype(F32) * mixed[heads, lanes].astype(F32), axis=0, keepdims=True
            )
            probs = jnp.exp(
                dot(k_tm[h, 0:ROWS, :], q_cm[h, :, lanes]) - lse[h : h + 1, lanes]
            )
            d_probs = dot(v_tm[h, 0:ROWS, :], dm)
            d_raw = (probs * (d_probs - inner)).astype(BF16)
            d_v = dot(probs.astype(BF16), dm, (1, 1))
            d_k = dot(d_raw, q_cm[h, 0:HEAD_DIM, lanes], (1, 1))
            acc_v[...] = d_v if c == 0 else acc_v[...] + d_v
            acc_k[...] = d_k if c == 0 else acc_k[...] + d_k
            d_q = dot(k_cm[heads, 0:ROWS], d_raw) * 0.125
            d_cm[h * 192 : h * 192 + 64, lanes] = d_q.astype(BF16)
            clock.work(0.85)
        d_cm[h * 192 + 64 : h * 192 + 128, 0:ROWS] = acc_k[...].T.astype(BF16)
        d_cm[h * 192 + 128 : h * 192 + 192, 0:ROWS] = acc_v[...].T.astype(BF16)
        three = dot(d_cm[h * 192 : (h + 1) * 192, :], normed_one[...]).astype(BF16)
        head_part[h, 0:192, :] = three[:, 0:384]
        head_part[h, 192:, :] = three[:, 384:]
        h_head[h].step()
        clock.work(0.7)
        if h == 0:
            while any(entry[2] == g_branch.forward for entry in clock.queue):
                clock.work(0.3)
            grad_out()
    d_tm[...] = d_cm[...].T
    bring.wait()

    def part_two(owner):
        rows = pl.ds(pl.multiple_of(owner * PART, 16), PART)
        return dot(d_tm[rows, :], w_by_head[...])

    sums = Scatter(links, p, out_c, out_x, in_c, in_x, mine)
    sums.far(part_two, clock, 1.0)
    sums.near(part_two, clock, 1.0)
    gain = gain_one[...].reshape(1, D)
    gathers = []
    gain_part = jnp.zeros((1, D), F32)
    for at, piece in enumerate(PIECES):
        rows = pl.ds(*piece)
        place = pl.ds(pl.multiple_of(p.t * PART + piece[0], 16), piece[1])
        total = sums.piece(at, clock)
        scaled, inverse = norm(tok[place, :].astype(F32))
        inner, add = norm_back(total, scaled, inverse, gain)
        gain_part = gain_part + add
        grad_tok[place, :] = (grad_hidden[rows, :] + inner).astype(BF16)
        g = Gather(links, p, lambda t: piece_at(grad_tok, t, piece))
        g.start(clock, piece[1] * D * 2)
        gathers.append(g)
        clock.work(0.6)
    row = lax.broadcasted_iota(jnp.int32, (8, D), 0)
    gains.start(jnp.where(row == 0, gain_part, 0.0) + jnp.where(row == 1, gain_part_two, 0.0))

    def turn():
        gains.step()
        if len(gains.copies) < len(gains.to):
            clock.later(clock.now + 3.0, turn)

    clock.later(clock.now + 3.0, turn)
    clock.drain()
    gain_sum[...] = gains.finish()
    for g in gathers:
        g.finish()
    sums.finish()
    for h in halvers:
        h.finish()


SOON = (4, 6, 7, 8, 9)
LATE = (11, 12) + tuple(range(14, 23))


def back_call(bits, levels, *args):
    outs = [
        ((2 * GH, BLOCK, 2 * GW), BF16),
        ((ROWS, D), BF16),
        ((4,) + FLAT, BF16),
        ((2, D // 2, D), BF16),
        ((D, CH), BF16),
        ((256, D), BF16),
        ((3, 384, 384), BF16),
        ((8, D), F32),
    ]
    room = lambda lead, rows, columns: pltpu.VMEM(
        lead + landing(rows, columns, bits).shape, BF16
    )
    scratch = [pltpu.VMEM(args[at].shape, args[at].dtype) for at in SOON + LATE] + [
        pltpu.VMEM((ROWS, D), BF16),
        pltpu.VMEM((LANES, CH), BF16),
        pltpu.VMEM((ROWS, D), BF16),
        pltpu.VMEM((PART, D), F32),
        pltpu.VMEM((PART, D), F32),
        pltpu.VMEM((ROWS, D), BF16),
    ] + scatter_scratch() + [
        pltpu.VMEM((4,) + FLAT, BF16),
        pltpu.VMEM((2, D // 2, D), BF16),
        pltpu.VMEM((D, CH), BF16),
        pltpu.VMEM((256, D), BF16),
        pltpu.VMEM((3, 384, 384), BF16),
        room((4,), *FLAT),
        room((2,), D // 2, D),
        room((), D, CH),
        room((), 256, D),
        room((3,), 384, 384),
        pltpu.VMEM((2 + bits, 8, D), F32),
        pltpu.VMEM((2 + bits, 8, D), F32),
        pltpu.VMEM((PART, D), BF16),
        pltpu.VMEM((ROWS, D // 2), BF16),
        pltpu.VMEM((D // 2, LANES), BF16),
        pltpu.VMEM((192, LANES), BF16),
        pltpu.VMEM((ROWS, HEAD_DIM), F32),
        pltpu.VMEM((ROWS, HEAD_DIM), F32),
        pltpu.VMEM((3 * 192, LANES), BF16),
        pltpu.VMEM((LANES, 3 * 192), BF16),
        pltpu.VMEM((3 * 192, D), BF16),
        pltpu.SemaphoreType.DMA((2 + len(LATE) + len(SOON),)),
    ] + sems(130)
    return call(
        functools.partial(back_kernel, levels), outs,
        [
            smem if at == 0 else anywhere if at in SOON + LATE + (3, 13, 23) else vmem
            for at in range(len(args))
        ],
        scratch, 3, 20_000_000_000, args,
    )


def write_kernel(
    out_all, grad_tok, conv, up, down, low, tap_all, ot, head, gains, joined_in,
    out_tokens, grad_tokens, conv_sum, up_sum, down_sum, out_sum, tap_sum, qkv_sum, gain_one,
    gain_two, joined,
):
    out_tokens[...] = out_all[0:SLOTS, :]
    grad_tokens[...] = grad_tok[0:SLOTS, :]
    joined[...] = joined_in[...]
    gain_one[...] = gains[0]
    gain_two[...] = gains[1]
    for j in range(4):
        for side in range(2):
            conv_sum[j, :, side * SLOT : (side + 1) * SLOT] = conv[
                j, side * WIDE : (side + 1) * WIDE, :
            ].astype(F32)
    for i in range(2):
        rows = slice(i * (D // 2), (i + 1) * (D // 2))
        up_sum[rows, :] = up[i].astype(F32)
        down_sum[rows, :] = down[i].astype(F32) + dot(low[rows, :], tap_all[...])
    out_sum[...] = ot[0:192, :].astype(F32)
    tap_sum[...] = ot[192:, :].astype(F32)
    for h in range(3):
        for part in range(3):
            for side in range(2):
                rows = side * 192 + part * 64
                qkv_sum[
                    part * 192 + h * 64 : part * 192 + h * 64 + 64, side * 384 : (side + 1) * 384
                ] = head[h, rows : rows + 64, :].astype(F32)


def write_call(*args):
    outs = [
        ((SLOTS, D), BF16),
        ((SLOTS, D), BF16),
        ((4, WIDE, CH), F32),
        ((D, D), F32),
        ((D, D), F32),
        ((192, D), F32),
        ((BLOCK, D), F32),
        ((3 * 192, D), F32),
        ((D,), F32),
        ((D,), F32),
        ((2 * GH, BLOCK, 2 * GW), BF16),
    ]
    return call(write_kernel, outs, [vmem] * 11, [], None, 400_000_000, args)


def per_device(
    bits, tokens, lengths, gain_one, gain_two, w_qkv, w_out, w_up, w_down, w_tap, w_conv,
    cot_tokens, cot_joined,
):
    w_heads = w_qkv.transpose(0, 2, 1).reshape(3 * 192, D)
    conv_w = w_conv.transpose(0, 1, 2, 4, 3).reshape(4, WIDE, CH)
    levels = {}
    (
        hidden_own, normed_two, q_cm, k_tm, v_tm, k_cm, lse, mixed, normed_one, slope, act,
        tap_all, w_out_all, out_own, field, conv_far, grad_own, down_part,
    ) = front_call(
        bits, levels, lengths, tokens, gain_one, gain_two, w_heads, w_out, w_tap.T, conv_w, w_up, w_down,
        cot_joined[0].transpose(0, 2, 1), cot_tokens,
    )
    result, tap_grad, g_conv, out_all, down = conv_call(
        bits, levels, lengths, field, conv_w, conv_far, grad_own, out_own, down_part
    )
    joined, grad_tok, conv, up, low, ot, head, gain_sum = back_call(
        bits, levels, lengths, tap_grad, tap_all, cot_tokens, slope, act, normed_two, w_up, w_down,
        hidden_own, gain_two, out_all, result, g_conv,
        w_out_all, mixed, q_cm, k_tm, v_tm, k_cm, lse, normed_one, w_heads, tokens, gain_one,
    )
    (
        out_tokens, grad_tokens, conv_sum, up_sum, down_sum, out_sum, tap_sum, qkv_sum, gain_a,
        gain_b, joined,
    ) = write_call(out_all, grad_tok, conv, up, down, low, tap_all, ot, head, gain_sum, joined)
    return (
        out_tokens,
        joined.transpose(0, 2, 1)[None],
        grad_tokens,
        qkv_sum.reshape(3, 192, D).transpose(0, 2, 1),
        out_sum,
        up_sum,
        down_sum,
        tap_sum.T,
        conv_sum.reshape(4, 3, 3, BLOCK, CH).transpose(0, 1, 2, 4, 3),
        gain_a,
        gain_b,
    )


def solution(mesh):
    placed = (
        P("dp", None),
        P("dp"),
        P(),
        P(),
        P(None, None, "tensor"),
        P("tensor", None),
        P(None, "tensor"),
        P("tensor", None),
        P(None, "tensor"),
        P(None, None, None, None, "tensor"),
        P("dp", None),
        P("dp", None, None, "tensor"),
    )
    return jax.shard_map(
        functools.partial(per_device, mesh.shape["dp"].bit_length() - 1),
        mesh=mesh,
        in_specs=placed,
        out_specs=(
            P("dp", None),
            P("dp", None, None, "tensor"),
            P("dp", None),
            P(None, None, "tensor"),
            P("tensor", None),
            P(None, "tensor"),
            P("tensor", None),
            P(None, "tensor"),
            P(None, None, None, None, "tensor"),
            P(),
            P(),
        ),
        check_vma=False,
    )
```

```python
import functools

import jax
import jax.numpy as jnp
from jax import lax
from jax.experimental import pallas as pl
from jax.experimental.pallas import tpu as pltpu
from jax.sharding import PartitionSpec as P

HEAD_DIM = 64
GH = 30
GW = 40
SH = 24
SW = 24
SLOTS = GH * GW
D = 768
CH = 256
BLOCK = 64
TAPS = 9
WIDE = TAPS * BLOCK
PART = 304
ROWS = 4 * PART
LANES = 1280
CHUNK = 256
SLOT = 128
F32 = jnp.float32
BF16 = jnp.bfloat16
MESH = pl.DeviceIdType.MESH
VMEM_LIMIT = 60 * 2**20

vmem = pl.BlockSpec(memory_space=pltpu.VMEM)
smem = pl.BlockSpec(memory_space=pltpu.SMEM)
anywhere = pl.BlockSpec(memory_space=pl.ANY)


def dot(a, b, dims=(1, 0)):
    return lax.dot_general(
        a, b, (((dims[0],), (dims[1],)), ((), ())), preferred_element_type=F32
    )


def gelu(v):
    return 0.5 * v * (1.0 + lax.erf(v * 0.7071067811865476))


def gelu_and_slope(v):
    share = 0.5 * (1.0 + lax.erf(v * 0.7071067811865476))
    return v * share, share + v * jnp.exp(-0.5 * v * v) * 0.3989422804014327


def norm(v):
    centred = v - jnp.mean(v, axis=-1, keepdims=True)
    spread = jnp.mean(centred * centred, axis=-1, keepdims=True)
    inverse = lax.rsqrt(spread + 1e-06)
    return centred * inverse, inverse


def norm_back(incoming, scaled, inverse, gain):
    weighted = incoming * gain
    inner = (
        weighted
        - jnp.mean(weighted, axis=-1, keepdims=True)
        - scaled * jnp.mean(weighted * scaled, axis=-1, keepdims=True)
    )
    return inverse * inner, jnp.sum(incoming * scaled, axis=0, keepdims=True)


def grid_place(shape, axis, offset):
    index = (lax.broadcasted_iota(jnp.int32, shape, axis) + offset).astype(F32)
    row = jnp.floor((index + 0.5) * (1.0 / GW))
    return row, index - GW * row


def cell_mask(shape, axis, offset, length):
    row, col = grid_place(shape, axis, offset)
    large = length == SLOTS
    height = jnp.where(large, float(GH), float(SH))
    breadth = jnp.where(large, float(GW), float(SW))
    return jnp.where((row < height) & (col < breadth), 1.0, 0.0)


class Peers:
    def __init__(self):
        self.dp = lax.axis_index("dp")
        self.n = lax.axis_size("dp")
        self.t = lax.axis_index("tensor")
        self.sib = self.t + 1 - 2 * lax.rem(self.t, 2)
        self.xp = lax.rem(self.t + 2, 4)
        self.diag = lax.rem(self.sib + 2, 4)

    def bit(self, at):
        return lax.rem(self.dp // (1 << at), 2)

    def mate(self, at):
        return self.dp + (1 - 2 * self.bit(at)) * (1 << at)

    def bits(self):
        return self.n.bit_length() - 1

    def greet(self, bits=0):
        barrier = pltpu.get_barrier_semaphore()
        others = [(self.dp, self.sib), (self.dp, self.xp)]
        others += [(self.mate(at), self.t) for at in range(bits)]
        for other in others:
            pl.semaphore_signal(barrier, inc=1, device_id=other, device_id_type=MESH)
        pl.semaphore_wait(barrier, len(others))


class Links:
    def __init__(self, send, recv):
        self.send, self.recv, self.used = send, recv, 0

    def copy(self, src, dst, device):
        at = self.used
        self.used += 1
        return pltpu.make_async_remote_copy(
            src_ref=src,
            dst_ref=dst,
            send_sem=self.send.at[at],
            recv_sem=self.recv.at[at],
            device_id=device,
            device_id_type=MESH,
        )


class Gather:
    def __init__(self, links, peers, place):
        p = peers
        self.x = links.copy(place(p.t), place(p.t), (p.dp, p.xp))
        self.c = links.copy(place(p.t), place(p.t), (p.dp, p.sib))
        self.f = links.copy(place(p.xp), place(p.xp), (p.dp, p.sib))

    def start(self, clock=None, size=0):
        self.x.start()
        self.c.start()
        if clock is not None:
            clock.later(clock.flight("x", size), self.forward)

    def forward(self):
        self.x.wait_recv()
        self.f.start()

    def finish(self):
        self.c.wait_recv()
        self.f.wait_recv()
        self.x.wait_send()
        self.c.wait_send()
        self.f.wait_send()


class Swap:
    def __init__(self, links, peers, far, near, place):
        p = peers
        self.x = links.copy(far, place(p.t), (p.dp, p.xp))
        self.c = links.copy(near, place(p.t), (p.dp, p.sib))
        self.f = links.copy(place(p.xp), place(p.xp), (p.dp, p.sib))

    start, forward, finish = Gather.start, Gather.forward, Gather.finish


PIECES = ((0, 160), (160, PART - 160))


class Scatter:
    def __init__(self, links, peers, out_c, out_x, in_c, in_x, mine):
        p = peers
        self.p, self.out_c, self.out_x, self.in_c, self.in_x = p, out_c, out_x, in_c, in_x
        self.mine = mine
        self.c = [
            links.copy(
                out_c.at[i, pl.ds(*piece), :], in_c.at[i, pl.ds(*piece), :], (p.dp, p.sib)
            )
            for i, piece in ((0, PIECES[0]), (0, PIECES[1]), (1, (0, PART)))
        ]
        self.x = [
            links.copy(out_x.at[pl.ds(*piece), :], in_x.at[pl.ds(*piece), :], (p.dp, p.xp))
            for piece in PIECES
        ]

    def far(self, part, clock, cost):
        p = self.p
        self.lands, core = [], []
        for copy, piece in zip(self.c, PIECES):
            self.out_c[0, pl.ds(*piece), :] = part(p.diag, *piece).astype(BF16)
            copy.start()
            clock.work(0.25 * cost)
            core.append(clock.flight("core", piece[1] * D * 2))
        for at, (copy, piece) in enumerate(zip(self.x, PIECES)):
            rows = pl.ds(*piece)
            mine = part(p.xp, *piece)
            clock.work(0.25 * cost)
            clock.until(core[at])
            self.c[at].wait_recv()
            self.out_x[rows, :] = (mine + self.in_c[0, rows, :].astype(F32)).astype(BF16)
            copy.start()
            self.lands.append(clock.flight("x", piece[1] * D * 2))

    def near(self, part, clock, cost):
        p = self.p
        self.out_c[1] = part(p.sib, 0, PART).astype(BF16)
        self.c[2].start()
        self.mine[...] = part(p.t, 0, PART)
        clock.work(cost)
        clock.until(clock.flight("core", PART * D * 2))
        self.c[2].wait_recv()
        self.mine[...] += self.in_c[1].astype(F32)

    def piece(self, at, clock=None):
        rows = pl.ds(*PIECES[at])
        if clock is not None:
            clock.until(self.lands[at])
        self.x[at].wait_recv()
        return self.mine[rows, :] + self.in_x[rows, :].astype(F32)

    def finish(self):
        for copy in self.c + self.x:
            copy.wait_send()


class Clock:
    RATES = {"core": 400e3, "zz": 23e3, "z4": 8.7e3, "all": 4.3e3}

    def __init__(self, latency=4.0):
        self.latency = latency
        self.now, self.free, self.queue, self.count = 0.0, {}, [], 0

    def flight(self, axis, size):
        took = size / self.RATES.get(axis, 46e3)
        lines = {"zz": ("zz", "z"), "z4": ("z", "zz"), "all": ("y", "z", "zz")}.get(axis, (axis,))
        start = max(self.now, self.free.get(lines[0], 0.0))
        for line in lines:
            part = {("zz", "z"): 0.5, ("all", "y"): 0.5, ("z4", "z"): 0.75}.get(
                (axis, line), 1.0
            ) * took
            self.free[line] = max(self.now, self.free.get(line, 0.0)) + part
        return start + took + (1.0 if axis == "core" else self.latency)

    def later(self, when, act):
        self.queue.append((when, self.count, act))
        self.count += 1

    def work(self, took):
        self.now += took
        while self.queue and min(self.queue)[0] <= self.now:
            first = min(self.queue)
            self.queue.remove(first)
            first[2]()

    def until(self, when):
        while self.queue and min(self.queue)[0] <= when:
            self.work(max(min(self.queue)[0] - self.now, 0.0))
        self.now = max(self.now, when)

    def drain(self):
        while self.queue:
            self.work(max(min(self.queue)[0] - self.now, 0.0))


Y, Z, ZZ, Z4, ALL = ("y", 0, 2), ("z", 1, 2), ("zz", 2, 2), ("z4", 1, 4), ("all", 0, 8)


class Halver:
    def __init__(self, links, peers, clock, array, arrive, result, stages, after=0):
        p = self.p = peers
        self.links, self.clock, self.array, self.arrive = links, clock, array, arrive
        self.result, self.stages = result, stages
        self.rows, self.columns = array.shape
        self.at = self.fresh = after
        base, size, slot = 0, self.rows, 0
        self.keep, self.give, self.land, self.to = [], [], [], []
        for _, low, count in stages:
            size //= count
            mine = lax.rem(p.dp // (1 << low), count)
            give, land, to = [], [], []
            for k in range(1, count):
                other = lax.rem(mine + k, count)
                give.append(pl.ds(pl.multiple_of(base + other * size, 16), size))
                land.append(pl.ds(slot, size))
                to.append((p.dp + (other - mine) * (1 << low), p.t))
                slot += size
            base = base + mine * size
            self.give.append(give)
            self.land.append(land)
            self.to.append(to)
            self.keep.append(pl.ds(pl.multiple_of(base, 16), size))
        self.size, self.slot = size, slot
        self.sent, self.rs, self.ag = [], {}, {}

    def send(self, k, copies):
        for copy in copies:
            copy.start()
        self.sent.extend(copies)
        size = self.keep[k].size * self.columns * 2
        self.clock.later(self.clock.flight(self.stages[k][0], size), self.step)

    def s(self, k):
        self.rs[k] = [
            self.links.copy(self.array.at[give, :], self.arrive.at[land, :], to)
            for give, land, to in zip(self.give[k], self.land[k], self.to[k])
        ]
        self.send(k, self.rs[k])

    def add(self, lands, keep):
        total = self.array[keep, :].astype(F32)
        for land in lands:
            total = total + self.arrive[land, :].astype(F32)
        self.array[keep, :] = total.astype(BF16)

    def a(self, k):
        for copy in self.rs[k]:
            copy.wait_recv()
        self.add(self.land[k], self.keep[k])
        if k == len(self.stages) - 1:
            for extra in range(3, self.p.bits()):
                land = pl.ds(self.slot + (extra - 3) * self.size, self.size)
                copy = self.links.copy(
                    self.array.at[self.keep[k], :], self.arrive.at[land, :],
                    (self.p.mate(extra), self.p.t),
                )
                copy.start()
                copy.wait_recv()
                copy.wait_send()
                self.add([land], self.keep[k])

    def g(self, k):
        region = self.keep[k]
        if k == len(self.stages) - 1:
            self.result[region, :] = self.array[region, :]
        self.ag[k] = [
            self.links.copy(self.result.at[region, :], self.result.at[region, :], to)
            for to in self.to[k]
        ]
        self.send(k, self.ag[k])

    def step(self):
        at, last = self.at, len(self.stages)
        if at <= last:
            if at > self.fresh:
                self.a(at - 1)
                self.fresh = at
            if at < last:
                self.s(at)
            elif self.result is None:
                return
            else:
                self.g(last - 1)
        else:
            k = 2 * last - at
            for copy in self.ag[k].copy():
                copy.wait_recv()
            if k:
                self.g(k - 1)
        self.at += 1

    def done(self):
        return self.at > 2 * len(self.stages)

    def level(self):
        if self.at > self.fresh:
            self.a(self.at - 1)
            self.fresh = self.at
        return self.fresh

    def finish(self):
        for copy in self.sent:
            copy.wait_send()


class Fetch:
    def __init__(self, links, peers, clock, source, place, size, after=None):
        p = self.p = peers
        self.clock, self.size, self.after = clock, size, after
        quarter = lax.rem(p.dp, 4)
        pair = quarter - lax.rem(quarter, 2)
        self.x = links.copy(source(quarter), place(p.t, quarter, 1), (p.dp, p.xp))
        mine = place(p.xp, quarter, 1)
        self.one = links.copy(mine, mine, (p.mate(0), p.t))
        both = place(p.xp, pair, 2)
        self.two = links.copy(both, both, (p.mate(1), p.t))

    def start(self):
        self.x.start()
        self.clock.later(self.clock.flight("x", self.size), self.swap)

    def swap(self):
        self.x.wait_recv()
        self.one.start()
        self.clock.later(self.clock.flight("y", self.size), self.trade)

    def trade(self):
        self.one.wait_recv()
        self.two.start()
        self.clock.later(self.clock.flight("z", 2 * self.size), self.end)

    def end(self):
        self.two.wait_recv()
        if self.after is not None:
            self.after()

    def finish(self):
        self.x.wait_send()
        self.one.wait_send()
        self.two.wait_send()


def landing(rows, columns, bits):
    return pltpu.VMEM((rows + max(bits - 4, 0) * (rows // 8), columns), BF16)


class Doubler:
    def __init__(self, links, peers, outgoing, incoming):
        p = peers
        self.links, self.outgoing, self.incoming = links, outgoing, incoming
        self.to = [(p.dp, p.sib), (p.dp, p.xp)] + [(p.mate(at), p.t) for at in range(p.bits())]
        self.copies = []

    def start(self, value):
        self.value = value
        self.send()

    def send(self):
        at = len(self.copies)
        if at < len(self.to):
            self.outgoing[at] = self.value
            copy = self.links.copy(self.outgoing.at[at], self.incoming.at[at], self.to[at])
            copy.start()
            self.copies.append(copy)

    def step(self):
        at = len(self.copies) - 1
        self.copies[at].wait_recv()
        self.value = self.value + self.incoming[at]
        self.send()

    def finish(self):
        while len(self.copies) < len(self.to):
            self.step()
        self.copies[-1].wait_recv()
        self.value = self.value + self.incoming[len(self.to) - 1]
        for copy in self.copies:
            copy.wait_send()
        return self.value


def sems(count):
    return [pltpu.SemaphoreType.DMA((count,)), pltpu.SemaphoreType.DMA((count,))]


def part_at(ref, owner):
    return ref.at[pl.ds(pl.multiple_of(owner * PART, 16), PART), :]


def piece_at(ref, owner, piece):
    return ref.at[pl.ds(pl.multiple_of(owner * PART + piece[0], 16), piece[1]), :]


def upsample_table(count):
    shape = (2 * count, count)
    target = lax.broadcasted_iota(jnp.int32, shape, 0)
    source = lax.broadcasted_iota(jnp.int32, shape, 1)
    nearest = lax.shift_right_logical(target, 1)
    odd = target - 2 * nearest
    further = jnp.clip(nearest + 2 * odd - 1, 0, count - 1)
    return jnp.where(source == nearest, 0.75, 0.0) + jnp.where(source == further, 0.25, 0.0)


def split_dot(a, table):
    high = a.astype(BF16)
    low = (a - high.astype(F32)).astype(BF16)
    return dot(high, table) + dot(low, table)


def call(kernel, outs, ins, scratch, collective, flops, args, places=None):
    return pl.pallas_call(
        kernel,
        out_shape=[jax.ShapeDtypeStruct(*o) for o in outs],
        in_specs=ins,
        out_specs=places or [vmem] * len(outs),
        scratch_shapes=scratch,
        cost_estimate=pl.CostEstimate(
            flops=flops, bytes_accessed=20_000_000, transcendentals=0
        ),
        compiler_params=pltpu.CompilerParams(
            collective_id=collective,
            has_side_effects=True,
            vmem_limit_bytes=VMEM_LIMIT,
        )
        if collective is not None
        else pltpu.CompilerParams(vmem_limit_bytes=VMEM_LIMIT),
    )(*args)


def front_kernel(
    levels, length, tok_hbm, gain_one, gain_two, w_qkv, w_out, w_tap, w_conv, w_up_hbm, w_down_hbm,
    cot_field_hbm, cot_hbm,
    hidden_own_, normed_two_, q_cm_, k_tm_, v_tm_, k_cm_, lse_, mixed_, normed_one_, slope_, act_,
    tap_all_, out_all_, conv_all_, grad_own_,
    out_own, field, down_part,
    hidden_own, normed_two, q_cm, k_tm, v_tm, k_cm, lse, mixed, normed_one, slope, act,
    tap_all, out_all, conv_all, grad_own, down_arrive,
    tok, hidden, mixed_all, out_heads, v_cm, w_up, w_down, cot_field, cot,
    out_c, out_x, in_c, in_x, mine, tall, local, send, recv,
):
    p = Peers()
    links = Links(send, recv)
    bring = pltpu.make_async_copy(tok_hbm, tok.at[pl.ds(0, SLOTS), :], local.at[0])
    bring.start()
    late = [
        pltpu.make_async_copy(w_up_hbm, w_up, local.at[1]),
        pltpu.make_async_copy(w_down_hbm, w_down, local.at[2]),
        pltpu.make_async_copy(cot_field_hbm, cot_field, local.at[3]),
        pltpu.make_async_copy(cot_hbm, cot.at[pl.ds(0, SLOTS), :], local.at[4]),
    ]
    tok[SLOTS:, :] = jnp.zeros((LANES - SLOTS, D), BF16)
    cot[SLOTS:, :] = jnp.zeros((ROWS - SLOTS, D), BF16)
    place_out = lambda t: out_all.at[pl.ds(pl.multiple_of(t * 192, 64), 192), :]
    place_tap = lambda t: tap_all.at[pl.ds(pl.multiple_of(t * 64, 64), 64), :]
    place_out(p.t)[...] = w_out[...]
    place_tap(p.t)[...] = w_tap[...]
    clock = Clock(3.3)
    p.greet(p.bits())
    c_near = [links.copy(place(p.t), place(p.t), (p.dp, p.sib)) for place in (place_out, place_tap)]
    c_far = [links.copy(place(p.xp), place(p.xp), (p.dp, p.sib)) for place in (place_out, place_tap)]
    f_out = Fetch(
        links, p, clock, lambda q: w_out.at[pl.ds(pl.multiple_of(q * 48, 16), 48), :],
        lambda t, q, n: out_all.at[pl.ds(pl.multiple_of(t * 192 + q * 48, 16), n * 48), :],
        48 * D * 2, c_far[0].start,
    )
    f_tap = Fetch(
        links, p, clock, lambda q: w_tap.at[pl.ds(pl.multiple_of(q * 16, 16), 16), :],
        lambda t, q, n: tap_all.at[pl.ds(pl.multiple_of(t * 64 + q * 16, 16), n * 16), :],
        16 * D * 2, c_far[1].start,
    )
    f_conv = Fetch(
        links, p, clock, lambda q: w_conv.at[pl.ds(q, 1)],
        lambda t, q, n: conv_all.at[pl.ds(q, n)], WIDE * CH * 2,
    )
    f_out.start()
    f_tap.start()
    f_conv.start()
    for c in c_near:
        c.start()
    writes = []

    def write(*arrays):
        for src, dst in arrays:
            copy = pltpu.make_async_copy(src, dst, local.at[5 + len(writes)])
            copy.start()
            writes.append(copy)

    bring.wait()
    for copy in late:
        copy.start()
    gain = gain_one[...].reshape(1, D)
    lane = lax.broadcasted_iota(jnp.int32, (CHUNK, SLOT), 1)
    one_row = jnp.where(
        lax.broadcasted_iota(jnp.int32, (HEAD_DIM, CHUNK), 0) == 0, 1.0, 0.0
    ).astype(BF16)

    def project(i, carry):
        off = pl.multiple_of(i * CHUNK, CHUNK)
        rows = pl.ds(off, CHUNK)
        scaled, _ = norm(tok[rows, :].astype(F32))
        normed = (scaled * gain).astype(BF16)
        normed_one[rows, :] = normed
        bias = jnp.where(cell_mask((CHUNK, SLOT), 0, off, length[0]) > 0.5, 0.0, -1e30)
        bias = jnp.where(lane == HEAD_DIM, bias, 0.0).astype(BF16)
        qkv = dot(w_qkv[...], normed, (1, 1)).astype(BF16)
        for h in range(3):
            near = slice(h * HEAD_DIM, (h + 1) * HEAD_DIM)
            q_cm[h, 0:HEAD_DIM, rows] = (qkv[near].astype(F32) * 0.125).astype(BF16)
            q_cm[h, HEAD_DIM:, rows] = one_row
            k = qkv[192 + h * HEAD_DIM : 192 + (h + 1) * HEAD_DIM]
            k_cm[near, rows] = k
            k_tm[h, rows, :] = bias
            k_tm[h, rows, 0:HEAD_DIM] = k.T
            v = qkv[384 + h * HEAD_DIM : 384 + (h + 1) * HEAD_DIM]
            v_cm[h, 0:HEAD_DIM, rows] = v
            v_cm[h, HEAD_DIM:, rows] = one_row[0:16]
            v_tm[h, rows, :] = v.T
        return carry

    lax.fori_loop(0, LANES // CHUNK, project, 0)
    write((q_cm, q_cm_), (k_tm, k_tm_), (v_tm, v_tm_), (k_cm, k_cm_), (normed_one, normed_one_))
    clock.work(4.0)
    chunks = [(h, c) for h in range(3) for c in range(LANES // CHUNK)]

    def scores(h, c):
        return dot(k_tm[h, 0:ROWS, :], q_cm[h, :, c * CHUNK : (c + 1) * CHUNK])

    def mixed_at(t, h, lanes):
        return mixed_all.at[
            pl.ds(pl.multiple_of(h * CH + t * HEAD_DIM, HEAD_DIM), HEAD_DIM), lanes
        ]

    def gather(h, lanes):
        g = Gather(links, p, lambda t: mixed_at(t, h, lanes))
        g.start(clock, (lanes.stop - lanes.start) * HEAD_DIM * 2)
        gathers.append(g)

    gathers = []
    ahead = scores(0, 0)
    for at, (h, c) in enumerate(chunks):
        s = ahead
        if at + 1 < len(chunks):
            ahead = scores(*chunks[at + 1])
        heads = slice(h * HEAD_DIM, (h + 1) * HEAD_DIM)
        lanes = slice(c * CHUNK, (c + 1) * CHUNK)
        top = jnp.max(s, axis=0, keepdims=True)
        out = dot(v_cm[h, :, 0:ROWS], jnp.exp(s - top).astype(BF16))
        total = out[HEAD_DIM : HEAD_DIM + 1]
        out = (out[0:HEAD_DIM] * (1.0 / total)).astype(BF16)
        lse[h : h + 1, lanes] = top + jnp.log(total)
        mixed[heads, lanes] = out
        mixed_at(p.t, h, lanes)[...] = out
        if c == 4:
            gather(h, slice(0 if h < 2 else 4 * CHUNK, LANES))
        elif h == 2 and c % 2:
            gather(h, slice((c - 1) * CHUNK, (c + 1) * CHUNK))
        clock.work(0.6)
    write((lse, lse_), (mixed, mixed_))
    while any(act_[2] in waited for act_ in clock.queue for waited in ((f_out.swap, f_out.trade, f_out.end, f_tap.swap, f_tap.trade, f_tap.end, gathers[0].forward, gathers[1].forward),)):
        clock.work(0.3)
    for c in c_near + c_far:
        c.wait_recv()
    for far in range(4):
        for k in range(3):
            out_heads[k * CH + far * HEAD_DIM : k * CH + (far + 1) * HEAD_DIM, :] = out_all[
                far * 192 + k * HEAD_DIM : far * 192 + (k + 1) * HEAD_DIM, :
            ]
    gathers[0].finish()
    gathers[1].finish()
    clock.work(0.5)

    def begin(i, carry):
        rows = pl.ds(pl.multiple_of(i * CHUNK, CHUNK), CHUNK)
        branch = dot(mixed_all[0 : 2 * CH, rows], out_heads[0 : 2 * CH, :], (0, 0))
        hidden[rows, :] = tok[rows, :].astype(F32) + branch
        return carry

    lax.fori_loop(0, LANES // CHUNK, begin, 0)
    clock.work(2.0)
    while any(act_[2] in [g.forward for g in gathers] for act_ in clock.queue):
        clock.work(0.3)
    for g in gathers[2:]:
        g.finish()
    gain_after = gain_two[...].reshape(1, D)

    def finish(i, carry):
        rows = pl.ds(pl.multiple_of(i * CHUNK, CHUNK), CHUNK)
        after = hidden[rows, :] + dot(
            mixed_all[2 * CH : 3 * CH, rows], out_heads[2 * CH : 3 * CH, :], (0, 0)
        )
        hidden[rows, :] = after
        scaled, _ = norm(after)
        normed_two[rows, :] = (scaled * gain_after).astype(BF16)
        return carry

    lax.fori_loop(0, LANES // CHUNK, finish, 0)
    hidden_own[...] = hidden[pl.ds(pl.multiple_of(p.t * PART, 16), PART), :]
    write((hidden_own, hidden_own_), (normed_two, normed_two_))
    write((out_all, out_all_), (tap_all, tap_all_))
    clock.work(2.5)
    for copy in late:
        copy.wait()

    def part(owner, first, count):
        rows = pl.ds(pl.multiple_of(owner * PART + first, 16), count)
        activation, steep = gelu_and_slope(dot(normed_two[rows, :], w_up[...]))
        activation = activation.astype(BF16)
        slope[rows, :] = steep.astype(BF16)
        act[rows, :] = activation
        return dot(activation, w_down[...])

    sums = Scatter(links, p, out_c, out_x, in_c, in_x, mine)
    sums.far(part, clock, 1.7)
    sums.near(part, clock, 1.7)
    write((slope, slope_), (act, act_))
    h_down = [
        Halver(links, p, clock, down_part.at[i], down_arrive.at[i], None, (Y, Z, ZZ))
        for i in range(2)
    ]
    for i in range(4):
        rows = slice(i * PART, (i + 1) * PART)
        cot[rows, :] = (
            cell_mask((PART, D), 0, i * PART, length[0]) * cot[rows, :].astype(F32)
        ).astype(BF16)
    for i in range(2):
        cols = slice(i * (D // 2), (i + 1) * (D // 2))
        down_part[i] = dot(act[:, cols], cot[...], (0, 0)).astype(BF16)
        h_down[i].step()
        clock.work(0.8)
    lower(cot_field, grad_own, tall, upsample_table(GW).astype(BF16))
    write((grad_own, grad_own_))
    gathers = []
    for at, piece in enumerate(PIECES):
        total = sums.piece(at, clock)
        off = pl.multiple_of(p.t * PART + piece[0], 16)
        mask = cell_mask((piece[1], D), 0, off, length[0])
        out = (mask * (hidden_own[pl.ds(*piece), :] + total)).astype(BF16)
        out_own[pl.ds(*piece), :] = out
        field[pl.ds(off, piece[1]), :] = dot(out, tap_all[...], (1, 1)).astype(BF16)
        g = Gather(links, p, lambda t: piece_at(field, t, piece))
        g.start(clock, piece[1] * CH * 2)
        gathers.append(g)
        clock.work(0.5)
    while any(act_[2] in [g.forward for g in gathers] for act_ in clock.queue):
        clock.work(0.3)
    while any(act_[2] in (f_conv.swap, f_conv.trade, f_conv.end) for act_ in clock.queue):
        clock.work(0.3)
    write((conv_all, conv_all_))
    for g in gathers:
        g.finish()
    levels["down"] = [h.level() for h in h_down]
    sums.finish()
    for c in c_near + c_far:
        c.wait_send()
    for f in (f_out, f_tap, f_conv):
        f.finish()
    for h in h_down:
        h.finish()
    for copy in writes:
        copy.wait()


def front_call(bits, levels, *args):
    kept = [
        ((PART, D), F32),
        ((LANES, D), BF16),
        ((3, SLOT, LANES), BF16),
        ((3, LANES, SLOT), BF16),
        ((3, LANES, HEAD_DIM), BF16),
        ((192, LANES), BF16),
        ((8, LANES), F32),
        ((192, LANES), BF16),
        ((LANES, D), BF16),
        ((ROWS, D), BF16),
        ((ROWS, D), BF16),
        ((CH, D), BF16),
        ((D, D), BF16),
        ((4, WIDE, CH), BF16),
        ((BLOCK, LANES), F32),
    ]
    outs = kept + [
        ((PART, D), BF16),
        ((ROWS, CH), BF16),
        ((2, D // 2, D), BF16),
    ]
    scratch = [pltpu.VMEM(*k) for k in kept] + [
        pltpu.VMEM((2,) + landing(D // 2, D, bits).shape, BF16),
        pltpu.VMEM((LANES, D), BF16),
        pltpu.VMEM((LANES, D), F32),
        pltpu.VMEM((D, LANES), BF16),
        pltpu.VMEM((D, D), BF16),
        pltpu.VMEM((3, HEAD_DIM + 16, LANES), BF16),
        pltpu.VMEM((D, D), BF16),
        pltpu.VMEM((D, D), BF16),
        pltpu.VMEM((2 * GH, BLOCK, 2 * GW), BF16),
        pltpu.VMEM((ROWS, D), BF16),
    ] + scatter_scratch() + [
        pltpu.VMEM((GH * BLOCK, 2 * GW), F32),
        pltpu.SemaphoreType.DMA((5 + len(kept),)),
    ] + sems(70)
    return call(
        functools.partial(front_kernel, levels), outs,
        [smem, anywhere] + [vmem] * 5 + [anywhere] * 5, scratch, 0, 14_000_000_000, args,
        [anywhere] * len(kept) + [vmem] * 3,
    )


def lower(cot, grad, tall, table):
    grad[:, SLOTS:] = jnp.zeros((BLOCK, LANES - SLOTS), F32)
    for a in range(GH):
        mid = 0.75 * (cot[2 * a].astype(F32) + cot[2 * a + 1].astype(F32))
        before = cot[max(2 * a - 1, 0)].astype(F32)
        after = cot[min(2 * a + 2, 2 * GH - 1)].astype(F32)
        tall[a * BLOCK : (a + 1) * BLOCK, :] = mid + 0.25 * (before + after)
    for a in range(GH):
        grad[:, a * GW : (a + 1) * GW] = split_dot(tall[a * BLOCK : (a + 1) * BLOCK, :], table)


def scatter_scratch():
    return [
        pltpu.VMEM((2, PART, D), BF16),
        pltpu.VMEM((PART, D), BF16),
        pltpu.VMEM((2, PART, D), BF16),
        pltpu.VMEM((PART, D), BF16),
        pltpu.VMEM((PART, D), F32),
    ]


def conv_kernel(
    levels, length, field, w_own, w_far, grad_own, out_own, down_hbm,
    result, tap_grad, g_conv, out_all, down,
    start_all, state, steep_first, steep_state, x_all, wide, flip, dcol, back, grad, grad_far,
    grad_near, back_out, back_in, arrive, down_part, down_arrive, local, send, recv,
):
    p = Peers()
    links = Links(send, recv)
    clock = Clock(3.6)
    bring = pltpu.make_async_copy(down_hbm, down_part, local.at[0])
    bring.start()
    p.greet(p.bits())
    weights = (w_own, w_far)
    block_of = (p.t, p.xp)
    at = lambda t: pl.ds(pl.multiple_of(t * BLOCK, BLOCK), BLOCK)

    part_at(out_all, p.t)[...] = out_own[...]
    out_all[ROWS:, :] = jnp.zeros((LANES - ROWS, D), BF16)
    g_out = Gather(links, p, lambda t: part_at(out_all, t))
    grad_near[...] = grad_own[...].astype(BF16)
    c_grad = links.copy(grad_near, grad_far, (p.dp, p.xp))
    c_grad.start()
    halvers = {
        j: Halver(links, p, clock, g_conv.at[j], arrive.at[j], None, ORDERS[j]) for j in (3, 2, 1)
    }
    h_down = [
        Halver(
            links, p, clock, down_part.at[i], down_arrive.at[i], down.at[i], (Y, Z, ZZ),
            levels["down"][i],
        )
        for i in range(2)
    ]
    bring.wait()
    for h in h_down:
        h.step()

    def masks(count):
        _, col = grid_place((count, LANES), 1, 0)
        not_first = jnp.where(col > 0.5, 1.0, 0.0)
        not_last = jnp.where(col < GW - 1.5, 1.0, 0.0)
        return cell_mask((count, LANES), 1, 0, length[0]), not_first, not_last

    _, not_first8, not_last8 = masks(8)
    cells16, not_first16, not_last16 = masks(16)
    not_first16, not_last16 = not_first16.astype(BF16), not_last16.astype(BF16)

    start_all[:, ROWS:] = jnp.zeros((CH, LANES - ROWS), F32)
    start_all[:, 0:ROWS] = field[...].astype(F32).T

    def rows_at(i):
        return pl.ds(pl.multiple_of(i * 16, 16), 16)

    def into_at(b, i):
        return pl.ds(pl.multiple_of(block_of[b] * BLOCK + i * 16, 16), 16)

    def open_rows(i, carry):
        x_all[0, rows_at(i), :] = gelu(start_all[rows_at(i), :]).astype(BF16)
        return carry

    lax.fori_loop(0, CH // 16, open_rows, 0)
    clock.work(2.0)

    def convolve(index, b, use):
        for c in range(LANES // CHUNK):
            lanes = slice(c * CHUNK, (c + 1) * CHUNK)
            wide[:, lanes] = dot(weights[b][index], x_all[index, :, lanes])

        def rows16(i, carry):
            halves = []
            for half in range(2):
                total = None
                for q in range(3):
                    tap = lambda r: wide[
                        pl.ds(pl.multiple_of((r * 3 + q) * BLOCK + i * 16 + half * 8, 8), 8), :
                    ]
                    three = (
                        tap(1)
                        + pltpu.roll(tap(0), GW, 1)
                        + pltpu.roll(tap(2), LANES - GW, 1)
                    )
                    if q == 0:
                        three = pltpu.roll(three, 1, 1) * not_first8
                    if q == 2:
                        three = pltpu.roll(three, LANES - 1, 1) * not_last8
                    total = three if total is None else total + three
                halves.append(total)
            use(i, cells16 * jnp.concatenate(halves, axis=0))
            return carry

        lax.fori_loop(0, BLOCK // 16, rows16, 0)
        clock.work(2.2)

    pending = []

    def share(array, b):
        place = array.at[at(block_of[b]), :]
        copy = links.copy(place, place, (p.dp, p.sib))
        copy.start()
        pending.append(copy)
        return copy

    def settle(copies):
        for c in copies:
            c.wait_recv()
        clock.work(1.0)

    def first_conv(unit):
        copies = []
        for b in range(2):
            def use(i, value, b=b):
                low, steep = gelu_and_slope(value)
                x_all[2 * unit + 1, into_at(b, i), :] = low.astype(BF16)
                steep_first[unit, b, rows_at(i), :] = steep

            convolve(2 * unit, b, use)
            copies.append(share(x_all.at[2 * unit + 1], b))
        return copies

    def spread(turn, b, value_of):
        def rows16(i, carry):
            value = value_of(i).astype(BF16)
            for q in range(3):
                side = value
                if q == 0:
                    side = pltpu.roll(value, LANES - 1, 1) * not_last16
                if q == 2:
                    side = pltpu.roll(value, 1, 1) * not_first16
                for r in range(3):
                    moved = side
                    if r == 0:
                        moved = pltpu.roll(side, LANES - GW, 1)
                    if r == 2:
                        moved = pltpu.roll(side, GW, 1)
                    into = pl.ds(pl.multiple_of((r * 3 + q) * BLOCK + i * 16, 16), 16)
                    dcol[turn % 2, b, into, :] = moved
            return carry

        lax.fori_loop(0, BLOCK // 16, rows16, 0)
        clock.work(0.8)

    def conv_back(turn):
        index = 3 - turn
        flip[0] = w_own[index].T
        flip[1] = w_far[index].T
        for c in range(LANES // CHUNK):
            lanes = slice(c * CHUNK, (c + 1) * CHUNK)
            back[:, lanes] = dot(flip[0], dcol[turn % 2, 0, :, lanes]) + dot(
                flip[1], dcol[turn % 2, 1, :, lanes]
            )
        copies = []
        for b, t in enumerate((p.sib, p.diag)):
            back_out[turn, b] = back[at(t), :].astype(BF16)
            c = links.copy(back_out.at[turn, b], back_in.at[turn, b], (p.dp, p.sib))
            c.start()
            copies.append(c)
        pending.extend(copies)
        clock.work(1.3)
        return copies

    def summed(turn, b, i):
        return back[into_at(b, i), :] + back_in[turn, b, rows_at(i), :].astype(F32)

    def weight_grad(turn):
        index = 3 - turn
        found = dot(dcol[turn % 2, 0], x_all[index], (1, 1)).astype(BF16)
        g_conv[index, 0:WIDE, :] = found[:, 0:SLOT]
        g_conv[index, WIDE:, :] = found[:, SLOT:]

    coming = first_conv(0)
    for b in range(2):
        def opening(i, carry, b=b):
            value = start_all[into_at(b, i), :]
            state[b, rows_at(i), :] = value
            steep_state[0, b, rows_at(i), :] = gelu_and_slope(value)[1]
            return carry

        lax.fori_loop(0, BLOCK // 16, opening, 0)
    clock.work(1.0)
    c_grad.wait_recv()
    g_out.start()
    grad[0] = grad_own[...]
    grad[1] = grad_far[...].astype(F32)
    for b in range(2):
        spread(0, b, lambda i, b=b: cells16 * grad[b, rows_at(i), :])
    settle(coming)
    coming = []
    for b in range(2):
        def use_second(i, value, b=b):
            fresh = state[b, rows_at(i), :] + value
            low, steep = gelu_and_slope(fresh)
            state[b, rows_at(i), :] = fresh
            x_all[2, into_at(b, i), :] = low.astype(BF16)
            steep_state[1, b, rows_at(i), :] = steep

        convolve(1, b, use_second)
        coming.append(share(x_all.at[2], b))
    backs = conv_back(0)
    settle(coming)
    coming = first_conv(1)
    settle(backs)
    for b in range(2):
        spread(
            1, b, lambda i, b=b: cells16 * summed(0, b, i) * steep_first[1, b, rows_at(i), :]
        )
    settle(coming)
    backs = conv_back(1)
    weight_grad(0)
    halvers[3].step()

    def use_last(i, value):
        result[rows_at(i), :] = state[0, rows_at(i), :] + value

    convolve(3, 0, use_last)
    weight_grad(1)
    halvers[2].step()
    clock.work(0.8)
    settle(backs)
    for b in range(2):
        def renewed(i, b=b):
            fresh = grad[b, rows_at(i), :] + summed(1, b, i) * steep_state[1, b, rows_at(i), :]
            grad[b, rows_at(i), :] = fresh
            return cells16 * fresh

        spread(2, b, renewed)
    backs = conv_back(2)
    weight_grad(2)
    halvers[1].step()
    clock.work(0.5)
    g_out.forward()
    settle(backs)
    for b in range(2):
        spread(
            3, b, lambda i, b=b: cells16 * summed(2, b, i) * steep_first[0, b, rows_at(i), :]
        )
    backs = conv_back(3)
    weight_grad(3)
    clock.work(0.5)
    inside16 = jnp.where(
        lax.broadcasted_iota(jnp.int32, (16, LANES), 1) < SLOTS, 1.0, 0.0
    )
    settle(backs)
    coming = []
    for b in range(2):
        def close(i, carry, b=b):
            fresh = grad[b, rows_at(i), :] + summed(3, b, i) * steep_state[0, b, rows_at(i), :]
            tap_grad[into_at(b, i), :] = (inside16 * fresh).astype(BF16)
            return carry

        lax.fori_loop(0, BLOCK // 16, close, 0)
        coming.append(share(tap_grad, b))
    settle(coming)
    while not all(h.done() for h in h_down):
        clock.work(0.5)
    levels[0] = 0
    for j, h in halvers.items():
        levels[j] = h.level()
    for c in pending + [c_grad]:
        c.wait_send()
    for h in list(halvers.values()) + h_down:
        h.finish()
    g_out.finish()


FLAT = (2 * WIDE, SLOT)
ORDERS = ((Z, Y, ZZ), (Y, Z, ZZ), (Y, Z, ZZ), (Y, Z, ZZ))


def conv_call(bits, levels, *args):
    outs = [
        ((BLOCK, LANES), F32),
        ((CH, LANES), BF16),
        ((4,) + FLAT, BF16),
        ((LANES, D), BF16),
        ((2, D // 2, D), BF16),
    ]
    scratch = [
        pltpu.VMEM((CH, LANES), F32),
        pltpu.VMEM((2, BLOCK, LANES), F32),
        pltpu.VMEM((2, 2, BLOCK, LANES), F32),
        pltpu.VMEM((2, 2, BLOCK, LANES), F32),
        pltpu.VMEM((4, CH, LANES), BF16),
        pltpu.VMEM((WIDE, LANES), F32),
        pltpu.VMEM((2, CH, WIDE), BF16),
        pltpu.VMEM((2, 2, WIDE, LANES), BF16),
        pltpu.VMEM((CH, LANES), F32),
        pltpu.VMEM((2, BLOCK, LANES), F32),
        pltpu.VMEM((BLOCK, LANES), BF16),
        pltpu.VMEM((BLOCK, LANES), BF16),
        pltpu.VMEM((4, 2, BLOCK, LANES), BF16),
        pltpu.VMEM((4, 2, BLOCK, LANES), BF16),
        pltpu.VMEM((4,) + landing(*FLAT, bits).shape, BF16),
        pltpu.VMEM((2, D // 2, D), BF16),
        pltpu.VMEM((2,) + landing(D // 2, D, bits).shape, BF16),
        pltpu.SemaphoreType.DMA((1,)),
    ] + sems(70)
    return call(
        functools.partial(conv_kernel, levels), outs, [smem] + [vmem] * 5 + [anywhere], scratch,
        2, 9_000_000_000, args,
    )


def lift(field, joined, table, grid_rows):
    for a in grid_rows:
        here = field[:, a * GW : (a + 1) * GW]
        up, down = max(a - 1, 0), min(a + 1, GH - 1)
        for side, other in enumerate((up, down)):
            line = 0.75 * here + 0.25 * field[:, other * GW : (other + 1) * GW]
            joined[2 * a + side] = split_dot(line, table).astype(BF16)


def back_kernel(
    levels, length, tap_grad, tap_all, cot_hbm, slope_, act, normed_two_, w_up_, w_down_, hidden_own_, gain_two,
    out_all_, field_, conv_hbm,
    w_out_, mixed_, q_cm_, k_tm_, v_tm_, k_cm_, lse_, normed_one_, w_qkv_, tok_hbm, gain_one,
    joined, grad_tok, conv, up, low, ot, head, gain_sum,
    slope, normed_two, w_up, w_down, hidden_own,
    out_all, field, w_out, mixed, q_cm, k_tm, v_tm, k_cm, lse, normed_one, w_qkv,
    tok, tap_tm, d_pre, mine_block, grad_hidden, branch, out_c, out_x, in_c, in_x, mine,
    conv_part, up_part, low_part, ot_part, head_part,
    conv_arrive, up_arrive, low_arrive, ot_arrive, head_arrive, gain_out, gain_arrive,
    d_out, d_mix_tm, d_mix_cm, d_mix, acc_k, acc_v, d_cm, d_tm, w_by_head, local, send, recv,
):
    p = Peers()
    links = Links(send, recv)
    clock = Clock()
    bring_conv = pltpu.make_async_copy(conv_hbm, conv_part, local.at[1])
    bring_conv.start()
    soon = [
        pltpu.make_async_copy(src, dst, local.at[2 + len(LATE) + i])
        for i, (src, dst) in enumerate(
            (
                (w_down_, w_down), (slope_, slope), (w_up_, w_up), (normed_two_, normed_two),
                (hidden_own_, hidden_own),
            )
        )
    ]
    late = [
        pltpu.make_async_copy(src, dst, local.at[2 + i])
        for i, (src, dst) in enumerate(
            (
                (out_all_, out_all), (field_, field), (w_out_, w_out), (mixed_, mixed),
                (q_cm_, q_cm), (k_tm_, k_tm), (v_tm_, v_tm), (k_cm_, k_cm), (lse_, lse),
                (normed_one_, normed_one), (w_qkv_, w_qkv),
            )
        )
    ]
    bring = pltpu.make_async_copy(cot_hbm, tok.at[pl.ds(0, SLOTS), :], local.at[0])
    bring.start()
    for copy in soon:
        copy.start()
    tok[SLOTS:, :] = jnp.zeros((ROWS - SLOTS, D), BF16)
    p.greet(p.bits())

    def halver(array, arrive, result, stages, after=0):
        made = Halver(links, p, clock, array, arrive, result, stages, after)
        halvers.append(made)
        return made

    halvers = []
    bring_conv.wait()
    for j in (3, 2, 1, 0):
        halver(conv_part.at[j], conv_arrive.at[j], conv.at[j], ORDERS[j], levels[j]).step()
    half = D // 2
    h_up = [
        halver(up_part.at[i], up_arrive.at[i], up.at[i], (Y, Z, ZZ))
        for i in range(2)
    ]
    h_low = halver(low_part, low_arrive, low, (Y, Z, ZZ))
    h_ot = halver(ot_part, ot_arrive, ot, (Z, Y, ZZ))
    h_head = [
        halver(head_part.at[h], head_arrive.at[h], head.at[h], ((Y, Z, ZZ), (Y, Z, ZZ), (Z, Y, ZZ))[h])
        for h in range(3)
    ]
    gains = Doubler(links, p, gain_out, gain_arrive)

    tap_tm[...] = (
        cell_mask((LANES, CH), 0, 0, length[0]) * tap_grad[...].T.astype(F32)
    ).astype(BF16)
    low_part[...] = dot(act[...], tap_tm[0:ROWS, :], (0, 0)).astype(BF16)
    h_low.step()
    clock.work(1.0)
    bring.wait()
    for copy in soon:
        copy.wait()

    def part(owner, first, count):
        off = pl.multiple_of(owner * PART + first, 16)
        rows = pl.ds(off, count)
        block = cell_mask((count, D), 0, off, length[0]) * (
            tok[rows, :].astype(F32) + dot(tap_tm[rows, :], tap_all[...])
        )
        mine_block[first : first + count, :] = block
        steep = (dot(block.astype(BF16), w_down[...], (1, 1)) * slope[rows, :].astype(F32)).astype(BF16)
        d_pre[rows, :] = steep
        return dot(steep, w_up[...], (1, 1))

    for copy in late:
        copy.start()
    sums = Scatter(links, p, out_c, out_x, in_c, in_x, mine)
    sums.far(part, clock, 1.7)
    sums.near(part, clock, 1.7)
    for i in range(2):
        cols = slice(i * half, (i + 1) * half)
        up_part[i] = dot(normed_two[0:ROWS, cols], d_pre[...], (0, 0)).astype(BF16)
        h_up[i].step()
        clock.work(0.8)
    gain = gain_two[...].reshape(1, D)
    for copy in late:
        copy.wait()
    chip = p.t // 2
    near_half = pl.ds(pl.multiple_of(chip * (D // 2), SLOT), D // 2)
    far_half = pl.ds(pl.multiple_of((1 - chip) * (D // 2), SLOT), D // 2)
    swaps = []
    gain_part_two = jnp.zeros((1, D), F32)
    for at, piece in enumerate(PIECES):
        rows = pl.ds(*piece)
        total = sums.piece(at, clock)
        scaled, inverse = norm(hidden_own[rows, :])
        inner, add = norm_back(total, scaled, inverse, gain)
        after = mine_block[rows, :] + inner
        grad_hidden[rows, :] = after
        gain_part_two = gain_part_two + add
        low_after = after.astype(BF16)
        branch[pl.ds(pl.multiple_of(p.t * PART + piece[0], 16), piece[1]), :] = low_after
        d_out[rows, :] = dot(low_after, w_out[...], (1, 1)).astype(BF16)
        piece_at(d_mix_tm, p.t, piece)[...] = d_out[rows, near_half]
        g = Swap(
            links, p, d_out.at[rows, far_half], d_out.at[rows, near_half],
            lambda t: piece_at(d_mix_tm, t, piece),
        )
        g.start(clock, piece[1] * D)
        swaps.append(g)
        clock.work(0.8)
    g_branch = Gather(links, p, lambda t: part_at(branch, t))
    g_branch.start(clock, PART * D * 2)
    sums.finish()
    bring = pltpu.make_async_copy(tok_hbm, tok.at[pl.ds(0, SLOTS), :], local.at[0])
    bring.start()
    table = upsample_table(GW).T.astype(BF16)
    for quarter in range(5):
        lift(field, joined, table, range(quarter * 6, quarter * 6 + 6))
        clock.work(0.4)
    ot_part[192:, :] = dot(
        tap_grad[pl.ds(pl.multiple_of(p.t * BLOCK, BLOCK), BLOCK), :], out_all[...]
    ).astype(BF16)
    for h in range(3):
        for part_at_ in range(3):
            w_by_head[h * 192 + part_at_ * 64 : h * 192 + part_at_ * 64 + 64, :] = w_qkv[
                part_at_ * 192 + h * 64 : part_at_ * 192 + h * 64 + 64, :
            ]
    d_mix_cm[:, ROWS:] = jnp.zeros((D // 2, LANES - ROWS), BF16)
    d_cm[:, ROWS:] = jnp.zeros((3 * 192, LANES - ROWS), BF16)
    clock.work(1.0)
    ahead = [g.forward for g in swaps]
    while any(entry[2] in ahead for entry in clock.queue):
        clock.work(0.3)
    for g in swaps:
        g.finish()
    clock.work(1.0)
    d_mix_cm[:, 0:ROWS] = d_mix_tm[...].T
    d_mix[...] = d_mix_cm[pl.ds(pl.multiple_of(lax.rem(p.t, 2) * 192, 64), 192), :]
    clock.work(0.7)

    def grad_out():
        g_branch.finish()
        ot_part[0:192, :] = dot(mixed[:, 0:ROWS], branch[...]).astype(BF16)
        h_ot.step()
        clock.work(0.5)

    for h in range(3):
        heads = slice(h * HEAD_DIM, (h + 1) * HEAD_DIM)
        for c in range(LANES // CHUNK):
            lanes = slice(c * CHUNK, (c + 1) * CHUNK)
            dm = d_mix[heads, lanes]
            inner = jnp.sum(
                dm.astype(F32) * mixed[heads, lanes].astype(F32), axis=0, keepdims=True
            )
            probs = jnp.exp(
                dot(k_tm[h, 0:ROWS, :], q_cm[h, :, lanes]) - lse[h : h + 1, lanes]
            )
            d_probs = dot(v_tm[h, 0:ROWS, :], dm)
            d_raw = (probs * (d_probs - inner)).astype(BF16)
            d_v = dot(probs.astype(BF16), dm, (1, 1))
            d_k = dot(d_raw, q_cm[h, 0:HEAD_DIM, lanes], (1, 1))
            acc_v[...] = d_v if c == 0 else acc_v[...] + d_v
            acc_k[...] = d_k if c == 0 else acc_k[...] + d_k
            d_q = dot(k_cm[heads, 0:ROWS], d_raw) * 0.125
            d_cm[h * 192 : h * 192 + 64, lanes] = d_q.astype(BF16)
            clock.work(0.85)
        d_cm[h * 192 + 64 : h * 192 + 128, 0:ROWS] = acc_k[...].T.astype(BF16)
        d_cm[h * 192 + 128 : h * 192 + 192, 0:ROWS] = acc_v[...].T.astype(BF16)
        three = dot(d_cm[h * 192 : (h + 1) * 192, :], normed_one[...]).astype(BF16)
        head_part[h, 0:192, :] = three[:, 0:384]
        head_part[h, 192:, :] = three[:, 384:]
        h_head[h].step()
        clock.work(0.7)
        if h == 0:
            while any(entry[2] == g_branch.forward for entry in clock.queue):
                clock.work(0.3)
            grad_out()
    d_tm[...] = d_cm[...].T
    bring.wait()

    def part_two(owner, first, count):
        rows = pl.ds(pl.multiple_of(owner * PART + first, 16), count)
        return dot(d_tm[rows, :], w_by_head[...])

    sums = Scatter(links, p, out_c, out_x, in_c, in_x, mine)
    sums.far(part_two, clock, 1.0)
    sums.near(part_two, clock, 1.0)
    gain = gain_one[...].reshape(1, D)
    gathers = []
    gain_part = jnp.zeros((1, D), F32)
    for at, piece in enumerate(PIECES):
        rows = pl.ds(*piece)
        place = pl.ds(pl.multiple_of(p.t * PART + piece[0], 16), piece[1])
        total = sums.piece(at, clock)
        scaled, inverse = norm(tok[place, :].astype(F32))
        inner, add = norm_back(total, scaled, inverse, gain)
        gain_part = gain_part + add
        grad_tok[place, :] = (grad_hidden[rows, :] + inner).astype(BF16)
        g = Gather(links, p, lambda t: piece_at(grad_tok, t, piece))
        g.start(clock, piece[1] * D * 2)
        gathers.append(g)
        clock.work(0.6)
    row = lax.broadcasted_iota(jnp.int32, (8, D), 0)
    gains.start(jnp.where(row == 0, gain_part, 0.0) + jnp.where(row == 1, gain_part_two, 0.0))

    def turn():
        gains.step()
        if len(gains.copies) < len(gains.to):
            clock.later(clock.now + 3.0, turn)

    clock.later(clock.now + 3.0, turn)
    clock.drain()
    gain_sum[...] = gains.finish()
    for g in gathers:
        g.finish()
    sums.finish()
    for h in halvers:
        h.finish()


SOON = (4, 6, 7, 8, 9)
LATE = (11, 12) + tuple(range(14, 23))


def back_call(bits, levels, *args):
    outs = [
        ((2 * GH, BLOCK, 2 * GW), BF16),
        ((ROWS, D), BF16),
        ((4,) + FLAT, BF16),
        ((2, D // 2, D), BF16),
        ((D, CH), BF16),
        ((256, D), BF16),
        ((3, 384, 384), BF16),
        ((8, D), F32),
    ]
    room = lambda lead, rows, columns: pltpu.VMEM(
        lead + landing(rows, columns, bits).shape, BF16
    )
    scratch = [pltpu.VMEM(args[at].shape, args[at].dtype) for at in SOON + LATE] + [
        pltpu.VMEM((ROWS, D), BF16),
        pltpu.VMEM((LANES, CH), BF16),
        pltpu.VMEM((ROWS, D), BF16),
        pltpu.VMEM((PART, D), F32),
        pltpu.VMEM((PART, D), F32),
        pltpu.VMEM((ROWS, D), BF16),
    ] + scatter_scratch() + [
        pltpu.VMEM((4,) + FLAT, BF16),
        pltpu.VMEM((2, D // 2, D), BF16),
        pltpu.VMEM((D, CH), BF16),
        pltpu.VMEM((256, D), BF16),
        pltpu.VMEM((3, 384, 384), BF16),
        room((4,), *FLAT),
        room((2,), D // 2, D),
        room((), D, CH),
        room((), 256, D),
        room((3,), 384, 384),
        pltpu.VMEM((2 + bits, 8, D), F32),
        pltpu.VMEM((2 + bits, 8, D), F32),
        pltpu.VMEM((PART, D), BF16),
        pltpu.VMEM((ROWS, D // 2), BF16),
        pltpu.VMEM((D // 2, LANES), BF16),
        pltpu.VMEM((192, LANES), BF16),
        pltpu.VMEM((ROWS, HEAD_DIM), F32),
        pltpu.VMEM((ROWS, HEAD_DIM), F32),
        pltpu.VMEM((3 * 192, LANES), BF16),
        pltpu.VMEM((LANES, 3 * 192), BF16),
        pltpu.VMEM((3 * 192, D), BF16),
        pltpu.SemaphoreType.DMA((2 + len(LATE) + len(SOON),)),
    ] + sems(130)
    return call(
        functools.partial(back_kernel, levels), outs,
        [
            smem if at == 0 else anywhere if at in SOON + LATE + (3, 13, 23) else vmem
            for at in range(len(args))
        ],
        scratch, 3, 20_000_000_000, args,
    )


def write_kernel(
    out_all, grad_tok, conv, up, down, low, tap_all, ot, head, gains, joined_in,
    out_tokens, grad_tokens, conv_sum, up_sum, down_sum, out_sum, tap_sum, qkv_sum, gain_one,
    gain_two, joined,
):
    out_tokens[...] = out_all[0:SLOTS, :]
    grad_tokens[...] = grad_tok[0:SLOTS, :]
    joined[...] = joined_in[...]
    gain_one[...] = gains[0]
    gain_two[...] = gains[1]
    for j in range(4):
        for side in range(2):
            conv_sum[j, :, side * SLOT : (side + 1) * SLOT] = conv[
                j, side * WIDE : (side + 1) * WIDE, :
            ].astype(F32)
    for i in range(2):
        rows = slice(i * (D // 2), (i + 1) * (D // 2))
        up_sum[rows, :] = up[i].astype(F32)
        down_sum[rows, :] = down[i].astype(F32) + dot(low[rows, :], tap_all[...])
    out_sum[...] = ot[0:192, :].astype(F32)
    tap_sum[...] = ot[192:, :].astype(F32)
    for h in range(3):
        for part in range(3):
            for side in range(2):
                rows = side * 192 + part * 64
                qkv_sum[
                    part * 192 + h * 64 : part * 192 + h * 64 + 64, side * 384 : (side + 1) * 384
                ] = head[h, rows : rows + 64, :].astype(F32)


def write_call(*args):
    outs = [
        ((SLOTS, D), BF16),
        ((SLOTS, D), BF16),
        ((4, WIDE, CH), F32),
        ((D, D), F32),
        ((D, D), F32),
        ((192, D), F32),
        ((BLOCK, D), F32),
        ((3 * 192, D), F32),
        ((D,), F32),
        ((D,), F32),
        ((2 * GH, BLOCK, 2 * GW), BF16),
    ]
    return call(write_kernel, outs, [vmem] * 11, [], None, 400_000_000, args)


def per_device(
    bits, tokens, lengths, gain_one, gain_two, w_qkv, w_out, w_up, w_down, w_tap, w_conv,
    cot_tokens, cot_joined,
):
    w_heads = w_qkv.transpose(0, 2, 1).reshape(3 * 192, D)
    conv_w = w_conv.transpose(0, 1, 2, 4, 3).reshape(4, WIDE, CH)
    levels = {}
    (
        hidden_own, normed_two, q_cm, k_tm, v_tm, k_cm, lse, mixed, normed_one, slope, act,
        tap_all, w_out_all, conv_far, grad_own, out_own, field, down_part,
    ) = front_call(
        bits, levels, lengths, tokens, gain_one, gain_two, w_heads, w_out, w_tap.T, conv_w, w_up, w_down,
        cot_joined[0].transpose(0, 2, 1), cot_tokens,
    )
    result, tap_grad, g_conv, out_all, down = conv_call(
        bits, levels, lengths, field, conv_w, conv_far, grad_own, out_own, down_part
    )
    joined, grad_tok, conv, up, low, ot, head, gain_sum = back_call(
        bits, levels, lengths, tap_grad, tap_all, cot_tokens, slope, act, normed_two, w_up, w_down,
        hidden_own, gain_two, out_all, result, g_conv,
        w_out_all, mixed, q_cm, k_tm, v_tm, k_cm, lse, normed_one, w_heads, tokens, gain_one,
    )
    (
        out_tokens, grad_tokens, conv_sum, up_sum, down_sum, out_sum, tap_sum, qkv_sum, gain_a,
        gain_b, joined,
    ) = write_call(out_all, grad_tok, conv, up, down, low, tap_all, ot, head, gain_sum, joined)
    return (
        out_tokens,
        joined.transpose(0, 2, 1)[None],
        grad_tokens,
        qkv_sum.reshape(3, 192, D).transpose(0, 2, 1),
        out_sum,
        up_sum,
        down_sum,
        tap_sum.T,
        conv_sum.reshape(4, 3, 3, BLOCK, CH).transpose(0, 1, 2, 4, 3),
        gain_a,
        gain_b,
    )


def solution(mesh):
    placed = (
        P("dp", None),
        P("dp"),
        P(),
        P(),
        P(None, None, "tensor"),
        P("tensor", None),
        P(None, "tensor"),
        P("tensor", None),
        P(None, "tensor"),
        P(None, None, None, None, "tensor"),
        P("dp", None),
        P("dp", None, None, "tensor"),
    )
    return jax.shard_map(
        functools.partial(per_device, mesh.shape["dp"].bit_length() - 1),
        mesh=mesh,
        in_specs=placed,
        out_specs=(
            P("dp", None),
            P("dp", None, None, "tensor"),
            P("dp", None),
            P(None, None, "tensor"),
            P("tensor", None),
            P(None, "tensor"),
            P("tensor", None),
            P(None, "tensor"),
            P(None, None, None, None, "tensor"),
            P(),
            P(),
        ),
        check_vma=False,
    )
```

```python
import functools

import jax
import jax.numpy as jnp
from jax import lax
from jax.experimental import pallas as pl
from jax.experimental.pallas import tpu as pltpu
from jax.sharding import PartitionSpec as P

HEAD_DIM = 64
GH = 30
GW = 40
SH = 24
SW = 24
SLOTS = GH * GW
D = 768
CH = 256
BLOCK = 64
TAPS = 9
WIDE = TAPS * BLOCK
PART = 304
ROWS = 4 * PART
LANES = 1280
CHUNK = 256
SLOT = 128
F32 = jnp.float32
BF16 = jnp.bfloat16
MESH = pl.DeviceIdType.MESH
VMEM_LIMIT = 60 * 2**20

vmem = pl.BlockSpec(memory_space=pltpu.VMEM)
smem = pl.BlockSpec(memory_space=pltpu.SMEM)
anywhere = pl.BlockSpec(memory_space=pl.ANY)


def dot(a, b, dims=(1, 0)):
    return lax.dot_general(
        a, b, (((dims[0],), (dims[1],)), ((), ())), preferred_element_type=F32
    )


def gelu(v):
    return 0.5 * v * (1.0 + lax.erf(v * 0.7071067811865476))


def gelu_and_slope(v):
    share = 0.5 * (1.0 + lax.erf(v * 0.7071067811865476))
    return v * share, share + v * jnp.exp(-0.5 * v * v) * 0.3989422804014327


def norm(v):
    centred = v - jnp.mean(v, axis=-1, keepdims=True)
    spread = jnp.mean(centred * centred, axis=-1, keepdims=True)
    inverse = lax.rsqrt(spread + 1e-06)
    return centred * inverse, inverse


def norm_back(incoming, scaled, inverse, gain):
    weighted = incoming * gain
    inner = (
        weighted
        - jnp.mean(weighted, axis=-1, keepdims=True)
        - scaled * jnp.mean(weighted * scaled, axis=-1, keepdims=True)
    )
    return inverse * inner, jnp.sum(incoming * scaled, axis=0, keepdims=True)


def grid_place(shape, axis, offset):
    index = (lax.broadcasted_iota(jnp.int32, shape, axis) + offset).astype(F32)
    row = jnp.floor((index + 0.5) * (1.0 / GW))
    return row, index - GW * row


def cell_mask(shape, axis, offset, length):
    row, col = grid_place(shape, axis, offset)
    large = length == SLOTS
    height = jnp.where(large, float(GH), float(SH))
    breadth = jnp.where(large, float(GW), float(SW))
    return jnp.where((row < height) & (col < breadth), 1.0, 0.0)


class Peers:
    def __init__(self):
        self.dp = lax.axis_index("dp")
        self.n = lax.axis_size("dp")
        self.t = lax.axis_index("tensor")
        self.sib = self.t + 1 - 2 * lax.rem(self.t, 2)
        self.xp = lax.rem(self.t + 2, 4)
        self.diag = lax.rem(self.sib + 2, 4)

    def bit(self, at):
        return lax.rem(self.dp // (1 << at), 2)

    def mate(self, at):
        return self.dp + (1 - 2 * self.bit(at)) * (1 << at)

    def bits(self):
        return self.n.bit_length() - 1

    def greet(self, bits=0):
        barrier = pltpu.get_barrier_semaphore()
        others = [(self.dp, self.sib), (self.dp, self.xp)]
        others += [(self.mate(at), self.t) for at in range(bits)]
        for other in others:
            pl.semaphore_signal(barrier, inc=1, device_id=other, device_id_type=MESH)
        pl.semaphore_wait(barrier, len(others))


class Links:
    def __init__(self, send, recv):
        self.send, self.recv, self.used = send, recv, 0

    def copy(self, src, dst, device):
        at = self.used
        self.used += 1
        return pltpu.make_async_remote_copy(
            src_ref=src,
            dst_ref=dst,
            send_sem=self.send.at[at],
            recv_sem=self.recv.at[at],
            device_id=device,
            device_id_type=MESH,
        )


class Gather:
    def __init__(self, links, peers, place):
        p = peers
        self.x = links.copy(place(p.t), place(p.t), (p.dp, p.xp))
        self.c = links.copy(place(p.t), place(p.t), (p.dp, p.sib))
        self.f = links.copy(place(p.xp), place(p.xp), (p.dp, p.sib))

    def start(self, clock=None, size=0):
        self.x.start()
        self.c.start()
        if clock is not None:
            clock.later(clock.flight("x", size), self.forward)

    def forward(self):
        self.x.wait_recv()
        self.f.start()

    def finish(self):
        self.c.wait_recv()
        self.f.wait_recv()
        self.x.wait_send()
        self.c.wait_send()
        self.f.wait_send()


class Swap:
    def __init__(self, links, peers, far, near, place):
        p = peers
        self.x = links.copy(far, place(p.t), (p.dp, p.xp))
        self.c = links.copy(near, place(p.t), (p.dp, p.sib))
        self.f = links.copy(place(p.xp), place(p.xp), (p.dp, p.sib))

    start, forward, finish = Gather.start, Gather.forward, Gather.finish


PIECES = ((0, 160), (160, PART - 160))


class Scatter:
    def __init__(self, links, peers, out_c, out_x, in_c, in_x, mine):
        p = peers
        self.p, self.out_c, self.out_x, self.in_c, self.in_x = p, out_c, out_x, in_c, in_x
        self.mine = mine
        self.c = [
            links.copy(
                out_c.at[i, pl.ds(*piece), :], in_c.at[i, pl.ds(*piece), :], (p.dp, p.sib)
            )
            for i, piece in ((0, PIECES[0]), (0, PIECES[1]), (1, (0, PART)))
        ]
        self.x = [
            links.copy(out_x.at[pl.ds(*piece), :], in_x.at[pl.ds(*piece), :], (p.dp, p.xp))
            for piece in PIECES
        ]

    def far(self, part, clock, cost):
        p = self.p
        self.lands, core = [], []
        for copy, piece in zip(self.c, PIECES):
            self.out_c[0, pl.ds(*piece), :] = part(p.diag, *piece).astype(BF16)
            copy.start()
            clock.work(0.25 * cost)
            core.append(clock.flight("core", piece[1] * D * 2))
        for at, (copy, piece) in enumerate(zip(self.x, PIECES)):
            rows = pl.ds(*piece)
            mine = part(p.xp, *piece)
            clock.work(0.25 * cost)
            clock.until(core[at])
            self.c[at].wait_recv()
            self.out_x[rows, :] = (mine + self.in_c[0, rows, :].astype(F32)).astype(BF16)
            copy.start()
            self.lands.append(clock.flight("x", piece[1] * D * 2))

    def near(self, part, clock, cost):
        p = self.p
        self.out_c[1] = part(p.sib, 0, PART).astype(BF16)
        self.c[2].start()
        self.mine[...] = part(p.t, 0, PART)
        clock.work(cost)
        clock.until(clock.flight("core", PART * D * 2))
        self.c[2].wait_recv()
        self.mine[...] += self.in_c[1].astype(F32)

    def piece(self, at, clock=None):
        rows = pl.ds(*PIECES[at])
        if clock is not None:
            clock.until(self.lands[at])
        self.x[at].wait_recv()
        return self.mine[rows, :] + self.in_x[rows, :].astype(F32)

    def finish(self):
        for copy in self.c + self.x:
            copy.wait_send()


class Clock:
    RATES = {"core": 400e3, "zz": 23e3, "z4": 8.7e3, "all": 4.3e3}

    def __init__(self, latency=4.0):
        self.latency = latency
        self.now, self.free, self.queue, self.count = 0.0, {}, [], 0

    def flight(self, axis, size):
        took = size / self.RATES.get(axis, 46e3)
        lines = {"zz": ("zz", "z"), "z4": ("z", "zz"), "all": ("y", "z", "zz")}.get(axis, (axis,))
        start = max(self.now, self.free.get(lines[0], 0.0))
        for line in lines:
            part = {("zz", "z"): 0.5, ("all", "y"): 0.5, ("z4", "z"): 0.75}.get(
                (axis, line), 1.0
            ) * took
            self.free[line] = max(self.now, self.free.get(line, 0.0)) + part
        return start + took + (1.0 if axis == "core" else self.latency)

    def later(self, when, act):
        self.queue.append((when, self.count, act))
        self.count += 1

    def work(self, took):
        self.now += took
        while self.queue and min(self.queue)[0] <= self.now:
            first = min(self.queue)
            self.queue.remove(first)
            first[2]()

    def until(self, when):
        while self.queue and min(self.queue)[0] <= when:
            self.work(max(min(self.queue)[0] - self.now, 0.0))
        self.now = max(self.now, when)

    def drain(self):
        while self.queue:
            self.work(max(min(self.queue)[0] - self.now, 0.0))


Y, Z, ZZ, Z4, ALL = ("y", 0, 2), ("z", 1, 2), ("zz", 2, 2), ("z4", 1, 4), ("all", 0, 8)


class Halver:
    def __init__(self, links, peers, clock, array, arrive, result, stages, after=0):
        p = self.p = peers
        self.links, self.clock, self.array, self.arrive = links, clock, array, arrive
        self.result, self.stages = result, stages
        self.rows, self.columns = array.shape
        self.at = self.fresh = after
        base, size, slot = 0, self.rows, 0
        self.keep, self.give, self.land, self.to = [], [], [], []
        for _, low, count in stages:
            size //= count
            mine = lax.rem(p.dp // (1 << low), count)
            give, land, to = [], [], []
            for k in range(1, count):
                other = lax.rem(mine + k, count)
                give.append(pl.ds(pl.multiple_of(base + other * size, 16), size))
                land.append(pl.ds(slot, size))
                to.append((p.dp + (other - mine) * (1 << low), p.t))
                slot += size
            base = base + mine * size
            self.give.append(give)
            self.land.append(land)
            self.to.append(to)
            self.keep.append(pl.ds(pl.multiple_of(base, 16), size))
        self.size, self.slot = size, slot
        self.sent, self.rs, self.ag = [], {}, {}

    def send(self, k, copies):
        for copy in copies:
            copy.start()
        self.sent.extend(copies)
        size = self.keep[k].size * self.columns * 2
        self.clock.later(self.clock.flight(self.stages[k][0], size), self.step)

    def s(self, k):
        self.rs[k] = [
            self.links.copy(self.array.at[give, :], self.arrive.at[land, :], to)
            for give, land, to in zip(self.give[k], self.land[k], self.to[k])
        ]
        self.send(k, self.rs[k])

    def add(self, lands, keep):
        total = self.array[keep, :].astype(F32)
        for land in lands:
            total = total + self.arrive[land, :].astype(F32)
        self.array[keep, :] = total.astype(BF16)

    def a(self, k):
        for copy in self.rs[k]:
            copy.wait_recv()
        self.add(self.land[k], self.keep[k])
        if k == len(self.stages) - 1:
            for extra in range(3, self.p.bits()):
                land = pl.ds(self.slot + (extra - 3) * self.size, self.size)
                copy = self.links.copy(
                    self.array.at[self.keep[k], :], self.arrive.at[land, :],
                    (self.p.mate(extra), self.p.t),
                )
                copy.start()
                copy.wait_recv()
                copy.wait_send()
                self.add([land], self.keep[k])

    def g(self, k):
        region = self.keep[k]
        if k == len(self.stages) - 1:
            self.result[region, :] = self.array[region, :]
        self.ag[k] = [
            self.links.copy(self.result.at[region, :], self.result.at[region, :], to)
            for to in self.to[k]
        ]
        self.send(k, self.ag[k])

    def step(self):
        at, last = self.at, len(self.stages)
        if at <= last:
            if at > self.fresh:
                self.a(at - 1)
                self.fresh = at
            if at < last:
                self.s(at)
            elif self.result is None:
                return
            else:
                self.g(last - 1)
        else:
            k = 2 * last - at
            for copy in self.ag[k].copy():
                copy.wait_recv()
            if k:
                self.g(k - 1)
        self.at += 1

    def done(self):
        return self.at > 2 * len(self.stages)

    def level(self):
        if self.at > self.fresh:
            self.a(self.at - 1)
            self.fresh = self.at
        return self.fresh

    def finish(self):
        for copy in self.sent:
            copy.wait_send()


class Fetch:
    def __init__(self, links, peers, clock, source, place, size, after=None):
        p = self.p = peers
        self.clock, self.size, self.after = clock, size, after
        quarter = lax.rem(p.dp, 4)
        pair = quarter - lax.rem(quarter, 2)
        self.x = links.copy(source(quarter), place(p.t, quarter, 1), (p.dp, p.xp))
        mine = place(p.xp, quarter, 1)
        self.one = links.copy(mine, mine, (p.mate(0), p.t))
        both = place(p.xp, pair, 2)
        self.two = links.copy(both, both, (p.mate(1), p.t))

    def start(self):
        self.x.start()
        self.clock.later(self.clock.flight("x", self.size), self.swap)

    def swap(self):
        self.x.wait_recv()
        self.one.start()
        self.clock.later(self.clock.flight("y", self.size), self.trade)

    def trade(self):
        self.one.wait_recv()
        self.two.start()
        self.clock.later(self.clock.flight("z", 2 * self.size), self.end)

    def end(self):
        self.two.wait_recv()
        if self.after is not None:
            self.after()

    def finish(self):
        self.x.wait_send()
        self.one.wait_send()
        self.two.wait_send()


def landing(rows, columns, bits):
    return pltpu.VMEM((rows + max(bits - 4, 0) * (rows // 8), columns), BF16)


class Doubler:
    def __init__(self, links, peers, outgoing, incoming):
        p = peers
        self.links, self.outgoing, self.incoming = links, outgoing, incoming
        self.to = [(p.dp, p.sib), (p.dp, p.xp)] + [(p.mate(at), p.t) for at in range(p.bits())]
        self.copies = []

    def start(self, value):
        self.value = value
        self.send()

    def send(self):
        at = len(self.copies)
        if at < len(self.to):
            self.outgoing[at] = self.value
            copy = self.links.copy(self.outgoing.at[at], self.incoming.at[at], self.to[at])
            copy.start()
            self.copies.append(copy)

    def step(self):
        at = len(self.copies) - 1
        self.copies[at].wait_recv()
        self.value = self.value + self.incoming[at]
        self.send()

    def finish(self):
        while len(self.copies) < len(self.to):
            self.step()
        self.copies[-1].wait_recv()
        self.value = self.value + self.incoming[len(self.to) - 1]
        for copy in self.copies:
            copy.wait_send()
        return self.value


def sems(count):
    return [pltpu.SemaphoreType.DMA((count,)), pltpu.SemaphoreType.DMA((count,))]


def part_at(ref, owner):
    return ref.at[pl.ds(pl.multiple_of(owner * PART, 16), PART), :]


def piece_at(ref, owner, piece):
    return ref.at[pl.ds(pl.multiple_of(owner * PART + piece[0], 16), piece[1]), :]


def upsample_table(count):
    shape = (2 * count, count)
    target = lax.broadcasted_iota(jnp.int32, shape, 0)
    source = lax.broadcasted_iota(jnp.int32, shape, 1)
    nearest = lax.shift_right_logical(target, 1)
    odd = target - 2 * nearest
    further = jnp.clip(nearest + 2 * odd - 1, 0, count - 1)
    return jnp.where(source == nearest, 0.75, 0.0) + jnp.where(source == further, 0.25, 0.0)


def split_dot(a, table):
    high = a.astype(BF16)
    low = (a - high.astype(F32)).astype(BF16)
    return dot(high, table) + dot(low, table)


def call(kernel, outs, ins, scratch, collective, flops, args, places=None):
    return pl.pallas_call(
        kernel,
        out_shape=[jax.ShapeDtypeStruct(*o) for o in outs],
        in_specs=ins,
        out_specs=places or [vmem] * len(outs),
        scratch_shapes=scratch,
        cost_estimate=pl.CostEstimate(
            flops=flops, bytes_accessed=20_000_000, transcendentals=0
        ),
        compiler_params=pltpu.CompilerParams(
            collective_id=collective,
            has_side_effects=True,
            vmem_limit_bytes=VMEM_LIMIT,
        )
        if collective is not None
        else pltpu.CompilerParams(vmem_limit_bytes=VMEM_LIMIT),
    )(*args)


def front_kernel(
    levels, length, tok_hbm, gain_one, gain_two, w_qkv, w_out, w_tap, w_conv, w_up_hbm, w_down_hbm,
    cot_field_hbm, cot_hbm,
    hidden_own_, normed_two_, q_cm_, k_tm_, v_tm_, k_cm_, lse_, mixed_, normed_one_, slope_, act_,
    tap_all_, out_all_, conv_all_, grad_own_,
    out_own, field, down_part,
    hidden_own, normed_two, q_cm, k_tm, v_tm, k_cm, lse, mixed, normed_one, slope, act,
    tap_all, out_all, conv_all, grad_own, down_arrive,
    tok, hidden, mixed_all, out_heads, v_cm, w_up, w_down, cot_field, cot,
    out_c, out_x, in_c, in_x, mine, tall, local, send, recv,
):
    p = Peers()
    links = Links(send, recv)
    bring = pltpu.make_async_copy(tok_hbm, tok.at[pl.ds(0, SLOTS), :], local.at[0])
    bring.start()
    late = [
        pltpu.make_async_copy(w_up_hbm, w_up, local.at[1]),
        pltpu.make_async_copy(w_down_hbm, w_down, local.at[2]),
        pltpu.make_async_copy(cot_field_hbm, cot_field, local.at[3]),
        pltpu.make_async_copy(cot_hbm, cot.at[pl.ds(0, SLOTS), :], local.at[4]),
    ]
    tok[SLOTS:, :] = jnp.zeros((LANES - SLOTS, D), BF16)
    cot[SLOTS:, :] = jnp.zeros((ROWS - SLOTS, D), BF16)
    place_out = lambda t: out_all.at[pl.ds(pl.multiple_of(t * 192, 64), 192), :]
    place_tap = lambda t: tap_all.at[pl.ds(pl.multiple_of(t * 64, 64), 64), :]
    place_out(p.t)[...] = w_out[...]
    place_tap(p.t)[...] = w_tap[...]
    clock = Clock(3.3)
    p.greet(p.bits())
    c_near = [links.copy(place(p.t), place(p.t), (p.dp, p.sib)) for place in (place_out, place_tap)]
    c_far = [links.copy(place(p.xp), place(p.xp), (p.dp, p.sib)) for place in (place_out, place_tap)]
    f_out = Fetch(
        links, p, clock, lambda q: w_out.at[pl.ds(pl.multiple_of(q * 48, 16), 48), :],
        lambda t, q, n: out_all.at[pl.ds(pl.multiple_of(t * 192 + q * 48, 16), n * 48), :],
        48 * D * 2, c_far[0].start,
    )
    f_tap = Fetch(
        links, p, clock, lambda q: w_tap.at[pl.ds(pl.multiple_of(q * 16, 16), 16), :],
        lambda t, q, n: tap_all.at[pl.ds(pl.multiple_of(t * 64 + q * 16, 16), n * 16), :],
        16 * D * 2, c_far[1].start,
    )
    f_conv = Fetch(
        links, p, clock, lambda q: w_conv.at[pl.ds(q, 1)],
        lambda t, q, n: conv_all.at[pl.ds(q, n)], WIDE * CH * 2,
    )
    f_out.start()
    f_tap.start()
    f_conv.start()
    for c in c_near:
        c.start()
    writes = []

    def write(*arrays):
        for src, dst in arrays:
            copy = pltpu.make_async_copy(src, dst, local.at[5 + len(writes)])
            copy.start()
            writes.append(copy)

    bring.wait()
    for copy in late:
        copy.start()
    gain = gain_one[...].reshape(1, D)
    lane = lax.broadcasted_iota(jnp.int32, (CHUNK, SLOT), 1)
    one_row = jnp.where(
        lax.broadcasted_iota(jnp.int32, (HEAD_DIM, CHUNK), 0) == 0, 1.0, 0.0
    ).astype(BF16)

    def project(i, carry):
        off = pl.multiple_of(i * CHUNK, CHUNK)
        rows = pl.ds(off, CHUNK)
        scaled, _ = norm(tok[rows, :].astype(F32))
        normed = (scaled * gain).astype(BF16)
        normed_one[rows, :] = normed
        bias = jnp.where(cell_mask((CHUNK, SLOT), 0, off, length[0]) > 0.5, 0.0, -1e30)
        bias = jnp.where(lane == HEAD_DIM, bias, 0.0).astype(BF16)
        qkv = dot(w_qkv[...], normed, (1, 1)).astype(BF16)
        for h in range(3):
            near = slice(h * HEAD_DIM, (h + 1) * HEAD_DIM)
            q_cm[h, 0:HEAD_DIM, rows] = (qkv[near].astype(F32) * 0.125).astype(BF16)
            q_cm[h, HEAD_DIM:, rows] = one_row
            k = qkv[192 + h * HEAD_DIM : 192 + (h + 1) * HEAD_DIM]
            k_cm[near, rows] = k
            k_tm[h, rows, :] = bias
            k_tm[h, rows, 0:HEAD_DIM] = k.T
            v = qkv[384 + h * HEAD_DIM : 384 + (h + 1) * HEAD_DIM]
            v_cm[h, 0:HEAD_DIM, rows] = v
            v_cm[h, HEAD_DIM:, rows] = one_row[0:16]
            v_tm[h, rows, :] = v.T
        return carry

    lax.fori_loop(0, LANES // CHUNK, project, 0)
    write((q_cm, q_cm_), (k_tm, k_tm_), (v_tm, v_tm_), (k_cm, k_cm_), (normed_one, normed_one_))
    clock.work(4.0)
    chunks = [(h, c) for h in range(3) for c in range(LANES // CHUNK)]

    def scores(h, c):
        return dot(k_tm[h, 0:ROWS, :], q_cm[h, :, c * CHUNK : (c + 1) * CHUNK])

    def mixed_at(t, h, lanes):
        return mixed_all.at[
            pl.ds(pl.multiple_of(h * CH + t * HEAD_DIM, HEAD_DIM), HEAD_DIM), lanes
        ]

    def gather(h, lanes):
        g = Gather(links, p, lambda t: mixed_at(t, h, lanes))
        g.start(clock, (lanes.stop - lanes.start) * HEAD_DIM * 2)
        gathers.append(g)

    gathers = []
    ahead = scores(0, 0)
    for at, (h, c) in enumerate(chunks):
        s = ahead
        if at + 1 < len(chunks):
            ahead = scores(*chunks[at + 1])
        heads = slice(h * HEAD_DIM, (h + 1) * HEAD_DIM)
        lanes = slice(c * CHUNK, (c + 1) * CHUNK)
        top = jnp.max(s, axis=0, keepdims=True)
        out = dot(v_cm[h, :, 0:ROWS], jnp.exp(s - top).astype(BF16))
        total = out[HEAD_DIM : HEAD_DIM + 1]
        out = (out[0:HEAD_DIM] * (1.0 / total)).astype(BF16)
        lse[h : h + 1, lanes] = top + jnp.log(total)
        mixed[heads, lanes] = out
        mixed_at(p.t, h, lanes)[...] = out
        if c == 4:
            gather(h, slice(0 if h < 2 else 4 * CHUNK, LANES))
        elif h == 2 and c % 2:
            gather(h, slice((c - 1) * CHUNK, (c + 1) * CHUNK))
        clock.work(0.6)
    write((lse, lse_), (mixed, mixed_))
    while any(act_[2] in waited for act_ in clock.queue for waited in ((f_out.swap, f_out.trade, f_out.end, f_tap.swap, f_tap.trade, f_tap.end, gathers[0].forward, gathers[1].forward),)):
        clock.work(0.3)
    for c in c_near + c_far:
        c.wait_recv()
    for far in range(4):
        for k in range(3):
            out_heads[k * CH + far * HEAD_DIM : k * CH + (far + 1) * HEAD_DIM, :] = out_all[
                far * 192 + k * HEAD_DIM : far * 192 + (k + 1) * HEAD_DIM, :
            ]
    gathers[0].finish()
    gathers[1].finish()
    clock.work(0.5)

    def begin(i, carry):
        rows = pl.ds(pl.multiple_of(i * CHUNK, CHUNK), CHUNK)
        branch = dot(mixed_all[0 : 2 * CH, rows], out_heads[0 : 2 * CH, :], (0, 0))
        hidden[rows, :] = tok[rows, :].astype(F32) + branch
        return carry

    lax.fori_loop(0, LANES // CHUNK, begin, 0)
    clock.work(2.0)
    while any(act_[2] in [g.forward for g in gathers] for act_ in clock.queue):
        clock.work(0.3)
    for g in gathers[2:]:
        g.finish()
    gain_after = gain_two[...].reshape(1, D)

    def finish(i, carry):
        rows = pl.ds(pl.multiple_of(i * CHUNK, CHUNK), CHUNK)
        after = hidden[rows, :] + dot(
            mixed_all[2 * CH : 3 * CH, rows], out_heads[2 * CH : 3 * CH, :], (0, 0)
        )
        hidden[rows, :] = after
        scaled, _ = norm(after)
        normed_two[rows, :] = (scaled * gain_after).astype(BF16)
        return carry

    lax.fori_loop(0, LANES // CHUNK, finish, 0)
    hidden_own[...] = hidden[pl.ds(pl.multiple_of(p.t * PART, 16), PART), :]
    write((hidden_own, hidden_own_), (normed_two, normed_two_))
    write((out_all, out_all_), (tap_all, tap_all_))
    clock.work(2.5)
    for copy in late:
        copy.wait()

    def part(owner, first, count):
        rows = pl.ds(pl.multiple_of(owner * PART + first, 16), count)
        activation, steep = gelu_and_slope(dot(normed_two[rows, :], w_up[...]))
        activation = activation.astype(BF16)
        slope[rows, :] = steep.astype(BF16)
        act[rows, :] = activation
        return dot(activation, w_down[...])

    sums = Scatter(links, p, out_c, out_x, in_c, in_x, mine)
    sums.far(part, clock, 1.7)
    sums.near(part, clock, 1.7)
    write((slope, slope_), (act, act_))
    h_down = [
        Halver(links, p, clock, down_part.at[i], down_arrive.at[i], None, (Y, Z, ZZ))
        for i in range(2)
    ]
    for i in range(4):
        rows = slice(i * PART, (i + 1) * PART)
        cot[rows, :] = (
            cell_mask((PART, D), 0, i * PART, length[0]) * cot[rows, :].astype(F32)
        ).astype(BF16)
    for i in range(2):
        cols = slice(i * (D // 2), (i + 1) * (D // 2))
        down_part[i] = dot(act[:, cols], cot[...], (0, 0)).astype(BF16)
        h_down[i].step()
        clock.work(0.8)
    lower(cot_field, grad_own, tall, upsample_table(GW).astype(BF16))
    write((grad_own, grad_own_))
    gathers = []
    for at, piece in enumerate(PIECES):
        total = sums.piece(at, clock)
        off = pl.multiple_of(p.t * PART + piece[0], 16)
        mask = cell_mask((piece[1], D), 0, off, length[0])
        out = (mask * (hidden_own[pl.ds(*piece), :] + total)).astype(BF16)
        out_own[pl.ds(*piece), :] = out
        field[pl.ds(off, piece[1]), :] = dot(out, tap_all[...], (1, 1)).astype(BF16)
        g = Gather(links, p, lambda t: piece_at(field, t, piece))
        g.start(clock, piece[1] * CH * 2)
        gathers.append(g)
        clock.work(0.5)
    while any(act_[2] in [g.forward for g in gathers] for act_ in clock.queue):
        clock.work(0.3)
    while any(act_[2] in (f_conv.swap, f_conv.trade, f_conv.end) for act_ in clock.queue):
        clock.work(0.3)
    write((conv_all, conv_all_))
    for g in gathers:
        g.finish()
    levels["down"] = [h.level() for h in h_down]
    sums.finish()
    for c in c_near + c_far:
        c.wait_send()
    for f in (f_out, f_tap, f_conv):
        f.finish()
    for h in h_down:
        h.finish()
    for copy in writes:
        copy.wait()


def front_call(bits, levels, *args):
    kept = [
        ((PART, D), F32),
        ((LANES, D), BF16),
        ((3, SLOT, LANES), BF16),
        ((3, LANES, SLOT), BF16),
        ((3, LANES, HEAD_DIM), BF16),
        ((192, LANES), BF16),
        ((8, LANES), F32),
        ((192, LANES), BF16),
        ((LANES, D), BF16),
        ((ROWS, D), BF16),
        ((ROWS, D), BF16),
        ((CH, D), BF16),
        ((D, D), BF16),
        ((4, WIDE, CH), BF16),
        ((BLOCK, LANES), F32),
    ]
    outs = kept + [
        ((PART, D), BF16),
        ((ROWS, CH), BF16),
        ((2, D // 2, D), BF16),
    ]
    scratch = [pltpu.VMEM(*k) for k in kept] + [
        pltpu.VMEM((2,) + landing(D // 2, D, bits).shape, BF16),
        pltpu.VMEM((LANES, D), BF16),
        pltpu.VMEM((LANES, D), F32),
        pltpu.VMEM((D, LANES), BF16),
        pltpu.VMEM((D, D), BF16),
        pltpu.VMEM((3, HEAD_DIM + 16, LANES), BF16),
        pltpu.VMEM((D, D), BF16),
        pltpu.VMEM((D, D), BF16),
        pltpu.VMEM((2 * GH, BLOCK, 2 * GW), BF16),
        pltpu.VMEM((ROWS, D), BF16),
    ] + scatter_scratch() + [
        pltpu.VMEM((GH * BLOCK, 2 * GW), F32),
        pltpu.SemaphoreType.DMA((5 + len(kept),)),
    ] + sems(70)
    return call(
        functools.partial(front_kernel, levels), outs,
        [smem, anywhere] + [vmem] * 5 + [anywhere] * 5, scratch, 0, 14_000_000_000, args,
        [anywhere] * len(kept) + [vmem] * 3,
    )


def lower(cot, grad, tall, table):
    grad[:, SLOTS:] = jnp.zeros((BLOCK, LANES - SLOTS), F32)
    for a in range(GH):
        mid = 0.75 * (cot[2 * a].astype(F32) + cot[2 * a + 1].astype(F32))
        before = cot[max(2 * a - 1, 0)].astype(F32)
        after = cot[min(2 * a + 2, 2 * GH - 1)].astype(F32)
        tall[a * BLOCK : (a + 1) * BLOCK, :] = mid + 0.25 * (before + after)
    for a in range(GH):
        grad[:, a * GW : (a + 1) * GW] = split_dot(tall[a * BLOCK : (a + 1) * BLOCK, :], table)


def scatter_scratch():
    return [
        pltpu.VMEM((2, PART, D), BF16),
        pltpu.VMEM((PART, D), BF16),
        pltpu.VMEM((2, PART, D), BF16),
        pltpu.VMEM((PART, D), BF16),
        pltpu.VMEM((PART, D), F32),
    ]


def conv_kernel(
    levels, length, field, w_own_, w_far_, grad_own, out_own, down_hbm,
    result, tap_grad, g_conv, out_all_, down,
    w_own, w_far, out_all,
    start_all, state, steep_first, steep_state, x_all, wide, flip, dcol, back, grad, grad_far,
    grad_near, back_out, back_in, arrive, down_part, down_arrive, local, send, recv,
):
    p = Peers()
    links = Links(send, recv)
    clock = Clock(3.6)
    bring = pltpu.make_async_copy(down_hbm, down_part, local.at[0])
    bring.start()
    brings = [
        pltpu.make_async_copy(src, dst, local.at[1 + i])
        for i, (src, dst) in enumerate(((w_own_, w_own), (w_far_, w_far)))
    ]
    for copy in brings:
        copy.start()
    p.greet(p.bits())
    weights = (w_own, w_far)
    block_of = (p.t, p.xp)
    at = lambda t: pl.ds(pl.multiple_of(t * BLOCK, BLOCK), BLOCK)

    part_at(out_all, p.t)[...] = out_own[...]
    out_all[ROWS:, :] = jnp.zeros((LANES - ROWS, D), BF16)
    g_out = Gather(links, p, lambda t: part_at(out_all, t))
    grad_near[...] = grad_own[...].astype(BF16)
    c_grad = links.copy(grad_near, grad_far, (p.dp, p.xp))
    c_grad.start()
    halvers = {
        j: Halver(links, p, clock, g_conv.at[j], arrive.at[j], None, ORDERS[j]) for j in (3, 2, 1)
    }
    h_down = [
        Halver(
            links, p, clock, down_part.at[i], down_arrive.at[i], down.at[i], (Y, Z, ZZ),
            levels["down"][i],
        )
        for i in range(2)
    ]
    bring.wait()
    for h in h_down:
        h.step()

    def masks(count):
        _, col = grid_place((count, LANES), 1, 0)
        not_first = jnp.where(col > 0.5, 1.0, 0.0)
        not_last = jnp.where(col < GW - 1.5, 1.0, 0.0)
        return cell_mask((count, LANES), 1, 0, length[0]), not_first, not_last

    _, not_first8, not_last8 = masks(8)
    cells16, not_first16, not_last16 = masks(16)
    not_first16, not_last16 = not_first16.astype(BF16), not_last16.astype(BF16)

    start_all[:, ROWS:] = jnp.zeros((CH, LANES - ROWS), F32)
    start_all[:, 0:ROWS] = field[...].astype(F32).T

    def rows_at(i):
        return pl.ds(pl.multiple_of(i * 16, 16), 16)

    def into_at(b, i):
        return pl.ds(pl.multiple_of(block_of[b] * BLOCK + i * 16, 16), 16)

    def open_rows(i, carry):
        x_all[0, rows_at(i), :] = gelu(start_all[rows_at(i), :]).astype(BF16)
        return carry

    lax.fori_loop(0, CH // 16, open_rows, 0)
    clock.work(2.0)

    def convolve(index, b, use):
        for c in range(LANES // CHUNK):
            lanes = slice(c * CHUNK, (c + 1) * CHUNK)
            wide[:, lanes] = dot(weights[b][index], x_all[index, :, lanes])

        def rows16(i, carry):
            halves = []
            for half in range(2):
                total = None
                for q in range(3):
                    tap = lambda r: wide[
                        pl.ds(pl.multiple_of((r * 3 + q) * BLOCK + i * 16 + half * 8, 8), 8), :
                    ]
                    three = (
                        tap(1)
                        + pltpu.roll(tap(0), GW, 1)
                        + pltpu.roll(tap(2), LANES - GW, 1)
                    )
                    if q == 0:
                        three = pltpu.roll(three, 1, 1) * not_first8
                    if q == 2:
                        three = pltpu.roll(three, LANES - 1, 1) * not_last8
                    total = three if total is None else total + three
                halves.append(total)
            use(i, cells16 * jnp.concatenate(halves, axis=0))
            return carry

        lax.fori_loop(0, BLOCK // 16, rows16, 0)
        clock.work(2.2)

    pending = []

    def share(array, b):
        place = array.at[at(block_of[b]), :]
        copy = links.copy(place, place, (p.dp, p.sib))
        copy.start()
        pending.append(copy)
        return copy

    def settle(copies):
        for c in copies:
            c.wait_recv()
        clock.work(1.0)

    def first_conv(unit):
        copies = []
        for b in range(2):
            def use(i, value, b=b):
                low, steep = gelu_and_slope(value)
                x_all[2 * unit + 1, into_at(b, i), :] = low.astype(BF16)
                steep_first[unit, b, rows_at(i), :] = steep

            convolve(2 * unit, b, use)
            copies.append(share(x_all.at[2 * unit + 1], b))
        return copies

    def spread(turn, b, value_of):
        def rows16(i, carry):
            value = value_of(i).astype(BF16)
            for q in range(3):
                side = value
                if q == 0:
                    side = pltpu.roll(value, LANES - 1, 1) * not_last16
                if q == 2:
                    side = pltpu.roll(value, 1, 1) * not_first16
                for r in range(3):
                    moved = side
                    if r == 0:
                        moved = pltpu.roll(side, LANES - GW, 1)
                    if r == 2:
                        moved = pltpu.roll(side, GW, 1)
                    into = pl.ds(pl.multiple_of((r * 3 + q) * BLOCK + i * 16, 16), 16)
                    dcol[turn % 2, b, into, :] = moved
            return carry

        lax.fori_loop(0, BLOCK // 16, rows16, 0)
        clock.work(0.8)

    def conv_back(turn):
        index = 3 - turn
        flip[0] = w_own[index].T
        flip[1] = w_far[index].T
        for c in range(LANES // CHUNK):
            lanes = slice(c * CHUNK, (c + 1) * CHUNK)
            back[:, lanes] = dot(flip[0], dcol[turn % 2, 0, :, lanes]) + dot(
                flip[1], dcol[turn % 2, 1, :, lanes]
            )
        copies = []
        for b, t in enumerate((p.sib, p.diag)):
            back_out[turn, b] = back[at(t), :].astype(BF16)
            c = links.copy(back_out.at[turn, b], back_in.at[turn, b], (p.dp, p.sib))
            c.start()
            copies.append(c)
        pending.extend(copies)
        clock.work(1.3)
        return copies

    def summed(turn, b, i):
        return back[into_at(b, i), :] + back_in[turn, b, rows_at(i), :].astype(F32)

    def weight_grad(turn):
        index = 3 - turn
        found = dot(dcol[turn % 2, 0], x_all[index], (1, 1)).astype(BF16)
        g_conv[index, 0:WIDE, :] = found[:, 0:SLOT]
        g_conv[index, WIDE:, :] = found[:, SLOT:]

    for copy in brings:
        copy.wait()
    coming = first_conv(0)
    for b in range(2):
        def opening(i, carry, b=b):
            value = start_all[into_at(b, i), :]
            state[b, rows_at(i), :] = value
            steep_state[0, b, rows_at(i), :] = gelu_and_slope(value)[1]
            return carry

        lax.fori_loop(0, BLOCK // 16, opening, 0)
    clock.work(1.0)
    c_grad.wait_recv()
    g_out.start()
    grad[0] = grad_own[...]
    grad[1] = grad_far[...].astype(F32)
    for b in range(2):
        spread(0, b, lambda i, b=b: cells16 * grad[b, rows_at(i), :])
    settle(coming)
    coming = []
    for b in range(2):
        def use_second(i, value, b=b):
            fresh = state[b, rows_at(i), :] + value
            low, steep = gelu_and_slope(fresh)
            state[b, rows_at(i), :] = fresh
            x_all[2, into_at(b, i), :] = low.astype(BF16)
            steep_state[1, b, rows_at(i), :] = steep

        convolve(1, b, use_second)
        coming.append(share(x_all.at[2], b))
    backs = conv_back(0)
    settle(coming)
    coming = first_conv(1)
    settle(backs)
    for b in range(2):
        spread(
            1, b, lambda i, b=b: cells16 * summed(0, b, i) * steep_first[1, b, rows_at(i), :]
        )
    settle(coming)
    backs = conv_back(1)
    weight_grad(0)
    halvers[3].step()

    def use_last(i, value):
        result[rows_at(i), :] = state[0, rows_at(i), :] + value

    convolve(3, 0, use_last)
    weight_grad(1)
    halvers[2].step()
    clock.work(0.8)
    settle(backs)
    for b in range(2):
        def renewed(i, b=b):
            fresh = grad[b, rows_at(i), :] + summed(1, b, i) * steep_state[1, b, rows_at(i), :]
            grad[b, rows_at(i), :] = fresh
            return cells16 * fresh

        spread(2, b, renewed)
    backs = conv_back(2)
    weight_grad(2)
    halvers[1].step()
    clock.work(0.5)
    g_out.forward()
    settle(backs)
    for b in range(2):
        spread(
            3, b, lambda i, b=b: cells16 * summed(2, b, i) * steep_first[0, b, rows_at(i), :]
        )
    backs = conv_back(3)
    weight_grad(3)
    clock.work(0.5)
    inside16 = jnp.where(
        lax.broadcasted_iota(jnp.int32, (16, LANES), 1) < SLOTS, 1.0, 0.0
    )
    settle(backs)
    g_out.finish()
    keep = pltpu.make_async_copy(out_all, out_all_, local.at[3])
    keep.start()
    coming = []
    for b in range(2):
        def close(i, carry, b=b):
            fresh = grad[b, rows_at(i), :] + summed(3, b, i) * steep_state[0, b, rows_at(i), :]
            tap_grad[into_at(b, i), :] = (inside16 * fresh).astype(BF16)
            return carry

        lax.fori_loop(0, BLOCK // 16, close, 0)
        coming.append(share(tap_grad, b))
    settle(coming)
    while not all(h.done() for h in h_down):
        clock.work(0.5)
    levels[0] = 0
    for j, h in halvers.items():
        levels[j] = h.level()
    for c in pending + [c_grad]:
        c.wait_send()
    for h in list(halvers.values()) + h_down:
        h.finish()
    keep.wait()


FLAT = (2 * WIDE, SLOT)
ORDERS = ((Z, Y, ZZ), (Y, Z, ZZ), (Y, Z, ZZ), (Y, Z, ZZ))


def conv_call(bits, levels, *args):
    outs = [
        ((BLOCK, LANES), F32),
        ((CH, LANES), BF16),
        ((4,) + FLAT, BF16),
        ((LANES, D), BF16),
        ((2, D // 2, D), BF16),
    ]
    scratch = [
        pltpu.VMEM((4, WIDE, CH), BF16),
        pltpu.VMEM((4, WIDE, CH), BF16),
        pltpu.VMEM((LANES, D), BF16),
        pltpu.VMEM((CH, LANES), F32),
        pltpu.VMEM((2, BLOCK, LANES), F32),
        pltpu.VMEM((2, 2, BLOCK, LANES), F32),
        pltpu.VMEM((2, 2, BLOCK, LANES), F32),
        pltpu.VMEM((4, CH, LANES), BF16),
        pltpu.VMEM((WIDE, LANES), F32),
        pltpu.VMEM((2, CH, WIDE), BF16),
        pltpu.VMEM((2, 2, WIDE, LANES), BF16),
        pltpu.VMEM((CH, LANES), F32),
        pltpu.VMEM((2, BLOCK, LANES), F32),
        pltpu.VMEM((BLOCK, LANES), BF16),
        pltpu.VMEM((BLOCK, LANES), BF16),
        pltpu.VMEM((4, 2, BLOCK, LANES), BF16),
        pltpu.VMEM((4, 2, BLOCK, LANES), BF16),
        pltpu.VMEM((4,) + landing(*FLAT, bits).shape, BF16),
        pltpu.VMEM((2, D // 2, D), BF16),
        pltpu.VMEM((2,) + landing(D // 2, D, bits).shape, BF16),
        pltpu.SemaphoreType.DMA((4,)),
    ] + sems(70)
    return call(
        functools.partial(conv_kernel, levels), outs, [smem, vmem, anywhere, anywhere, vmem, vmem, anywhere],
        scratch, 2, 9_000_000_000, args, [vmem, vmem, vmem, anywhere, vmem],
    )


def lift(field, joined, table, grid_rows):
    for a in grid_rows:
        here = field[:, a * GW : (a + 1) * GW]
        up, down = max(a - 1, 0), min(a + 1, GH - 1)
        for side, other in enumerate((up, down)):
            line = 0.75 * here + 0.25 * field[:, other * GW : (other + 1) * GW]
            joined[2 * a + side] = split_dot(line, table).astype(BF16)


def back_kernel(
    levels, length, tap_grad, tap_all, cot_hbm, slope_, act, normed_two_, w_up_, w_down_, hidden_own_, gain_two,
    out_all_, field_, conv_hbm,
    w_out_, mixed_, q_cm_, k_tm_, v_tm_, k_cm_, lse_, normed_one_, w_qkv_, tok_hbm, gain_one,
    joined, grad_tok, conv, up, low, ot, head, gain_sum,
    slope, normed_two, w_up, w_down, hidden_own,
    out_all, field, w_out, mixed, q_cm, k_tm, v_tm, k_cm, lse, normed_one, w_qkv,
    tok, tap_tm, d_pre, mine_block, grad_hidden, branch, out_c, out_x, in_c, in_x, mine,
    conv_part, up_part, low_part, ot_part, head_part,
    conv_arrive, up_arrive, low_arrive, ot_arrive, head_arrive, gain_out, gain_arrive,
    d_out, d_mix_tm, d_mix_cm, d_mix, acc_k, acc_v, d_cm, d_tm, w_by_head, local, send, recv,
):
    p = Peers()
    links = Links(send, recv)
    clock = Clock()
    bring_conv = pltpu.make_async_copy(conv_hbm, conv_part, local.at[1])
    bring_conv.start()
    soon = [
        pltpu.make_async_copy(src, dst, local.at[2 + len(LATE) + i])
        for i, (src, dst) in enumerate(
            (
                (w_down_, w_down), (slope_, slope), (w_up_, w_up), (normed_two_, normed_two),
                (hidden_own_, hidden_own),
            )
        )
    ]
    late = [
        pltpu.make_async_copy(src, dst, local.at[2 + i])
        for i, (src, dst) in enumerate(
            (
                (out_all_, out_all), (field_, field), (w_out_, w_out), (mixed_, mixed),
                (q_cm_, q_cm), (k_tm_, k_tm), (v_tm_, v_tm), (k_cm_, k_cm), (lse_, lse),
                (normed_one_, normed_one), (w_qkv_, w_qkv),
            )
        )
    ]
    bring = pltpu.make_async_copy(cot_hbm, tok.at[pl.ds(0, SLOTS), :], local.at[0])
    bring.start()
    for copy in soon:
        copy.start()
    tok[SLOTS:, :] = jnp.zeros((ROWS - SLOTS, D), BF16)
    p.greet(p.bits())

    def halver(array, arrive, result, stages, after=0):
        made = Halver(links, p, clock, array, arrive, result, stages, after)
        halvers.append(made)
        return made

    halvers = []
    bring_conv.wait()
    for j in (3, 2, 1, 0):
        halver(conv_part.at[j], conv_arrive.at[j], conv.at[j], ORDERS[j], levels[j]).step()
    half = D // 2
    h_up = [
        halver(up_part.at[i], up_arrive.at[i], up.at[i], (Y, Z, ZZ))
        for i in range(2)
    ]
    h_low = halver(low_part, low_arrive, low, (Y, Z, ZZ))
    h_ot = halver(ot_part, ot_arrive, ot, (Z, Y, ZZ))
    h_head = [
        halver(head_part.at[h], head_arrive.at[h], head.at[h], ((Y, Z, ZZ), (Y, Z, ZZ), (Z, Y, ZZ))[h])
        for h in range(3)
    ]
    gains = Doubler(links, p, gain_out, gain_arrive)

    tap_tm[...] = (
        cell_mask((LANES, CH), 0, 0, length[0]) * tap_grad[...].T.astype(F32)
    ).astype(BF16)
    low_part[...] = dot(act[...], tap_tm[0:ROWS, :], (0, 0)).astype(BF16)
    h_low.step()
    clock.work(1.0)
    bring.wait()
    for copy in soon:
        copy.wait()

    def part(owner, first, count):
        off = pl.multiple_of(owner * PART + first, 16)
        rows = pl.ds(off, count)
        block = cell_mask((count, D), 0, off, length[0]) * (
            tok[rows, :].astype(F32) + dot(tap_tm[rows, :], tap_all[...])
        )
        mine_block[first : first + count, :] = block
        steep = (dot(block.astype(BF16), w_down[...], (1, 1)) * slope[rows, :].astype(F32)).astype(BF16)
        d_pre[rows, :] = steep
        return dot(steep, w_up[...], (1, 1))

    for copy in late:
        copy.start()
    sums = Scatter(links, p, out_c, out_x, in_c, in_x, mine)
    sums.far(part, clock, 1.7)
    sums.near(part, clock, 1.7)
    for i in range(2):
        cols = slice(i * half, (i + 1) * half)
        up_part[i] = dot(normed_two[0:ROWS, cols], d_pre[...], (0, 0)).astype(BF16)
        h_up[i].step()
        clock.work(0.8)
    gain = gain_two[...].reshape(1, D)
    for copy in late:
        copy.wait()
    chip = p.t // 2
    near_half = pl.ds(pl.multiple_of(chip * (D // 2), SLOT), D // 2)
    far_half = pl.ds(pl.multiple_of((1 - chip) * (D // 2), SLOT), D // 2)
    swaps = []
    gain_part_two = jnp.zeros((1, D), F32)
    for at, piece in enumerate(PIECES):
        rows = pl.ds(*piece)
        total = sums.piece(at, clock)
        scaled, inverse = norm(hidden_own[rows, :])
        inner, add = norm_back(total, scaled, inverse, gain)
        after = mine_block[rows, :] + inner
        grad_hidden[rows, :] = after
        gain_part_two = gain_part_two + add
        low_after = after.astype(BF16)
        branch[pl.ds(pl.multiple_of(p.t * PART + piece[0], 16), piece[1]), :] = low_after
        d_out[rows, :] = dot(low_after, w_out[...], (1, 1)).astype(BF16)
        piece_at(d_mix_tm, p.t, piece)[...] = d_out[rows, near_half]
        g = Swap(
            links, p, d_out.at[rows, far_half], d_out.at[rows, near_half],
            lambda t: piece_at(d_mix_tm, t, piece),
        )
        g.start(clock, piece[1] * D)
        swaps.append(g)
        clock.work(0.8)
    g_branch = Gather(links, p, lambda t: part_at(branch, t))
    g_branch.start(clock, PART * D * 2)
    sums.finish()
    bring = pltpu.make_async_copy(tok_hbm, tok.at[pl.ds(0, SLOTS), :], local.at[0])
    bring.start()
    table = upsample_table(GW).T.astype(BF16)
    for quarter in range(5):
        lift(field, joined, table, range(quarter * 6, quarter * 6 + 6))
        clock.work(0.4)
    ot_part[192:, :] = dot(
        tap_grad[pl.ds(pl.multiple_of(p.t * BLOCK, BLOCK), BLOCK), :], out_all[...]
    ).astype(BF16)
    for h in range(3):
        for part_at_ in range(3):
            w_by_head[h * 192 + part_at_ * 64 : h * 192 + part_at_ * 64 + 64, :] = w_qkv[
                part_at_ * 192 + h * 64 : part_at_ * 192 + h * 64 + 64, :
            ]
    d_mix_cm[:, ROWS:] = jnp.zeros((D // 2, LANES - ROWS), BF16)
    d_cm[:, ROWS:] = jnp.zeros((3 * 192, LANES - ROWS), BF16)
    clock.work(1.0)
    ahead = [g.forward for g in swaps]
    while any(entry[2] in ahead for entry in clock.queue):
        clock.work(0.3)
    for g in swaps:
        g.finish()
    clock.work(1.0)
    d_mix_cm[:, 0:ROWS] = d_mix_tm[...].T
    d_mix[...] = d_mix_cm[pl.ds(pl.multiple_of(lax.rem(p.t, 2) * 192, 64), 192), :]
    clock.work(0.7)

    def grad_out():
        g_branch.finish()
        ot_part[0:192, :] = dot(mixed[:, 0:ROWS], branch[...]).astype(BF16)
        h_ot.step()
        clock.work(0.5)

    for h in range(3):
        heads = slice(h * HEAD_DIM, (h + 1) * HEAD_DIM)
        for c in range(LANES // CHUNK):
            lanes = slice(c * CHUNK, (c + 1) * CHUNK)
            dm = d_mix[heads, lanes]
            inner = jnp.sum(
                dm.astype(F32) * mixed[heads, lanes].astype(F32), axis=0, keepdims=True
            )
            probs = jnp.exp(
                dot(k_tm[h, 0:ROWS, :], q_cm[h, :, lanes]) - lse[h : h + 1, lanes]
            )
            d_probs = dot(v_tm[h, 0:ROWS, :], dm)
            d_raw = (probs * (d_probs - inner)).astype(BF16)
            d_v = dot(probs.astype(BF16), dm, (1, 1))
            d_k = dot(d_raw, q_cm[h, 0:HEAD_DIM, lanes], (1, 1))
            acc_v[...] = d_v if c == 0 else acc_v[...] + d_v
            acc_k[...] = d_k if c == 0 else acc_k[...] + d_k
            d_q = dot(k_cm[heads, 0:ROWS], d_raw) * 0.125
            d_cm[h * 192 : h * 192 + 64, lanes] = d_q.astype(BF16)
            clock.work(0.85)
        d_cm[h * 192 + 64 : h * 192 + 128, 0:ROWS] = acc_k[...].T.astype(BF16)
        d_cm[h * 192 + 128 : h * 192 + 192, 0:ROWS] = acc_v[...].T.astype(BF16)
        three = dot(d_cm[h * 192 : (h + 1) * 192, :], normed_one[...]).astype(BF16)
        head_part[h, 0:192, :] = three[:, 0:384]
        head_part[h, 192:, :] = three[:, 384:]
        h_head[h].step()
        clock.work(0.7)
        if h == 0:
            while any(entry[2] == g_branch.forward for entry in clock.queue):
                clock.work(0.3)
            grad_out()
    d_tm[...] = d_cm[...].T
    bring.wait()

    def part_two(owner, first, count):
        rows = pl.ds(pl.multiple_of(owner * PART + first, 16), count)
        return dot(d_tm[rows, :], w_by_head[...])

    sums = Scatter(links, p, out_c, out_x, in_c, in_x, mine)
    sums.far(part_two, clock, 1.0)
    sums.near(part_two, clock, 1.0)
    gain = gain_one[...].reshape(1, D)
    gathers = []
    gain_part = jnp.zeros((1, D), F32)
    for at, piece in enumerate(PIECES):
        rows = pl.ds(*piece)
        place = pl.ds(pl.multiple_of(p.t * PART + piece[0], 16), piece[1])
        total = sums.piece(at, clock)
        scaled, inverse = norm(tok[place, :].astype(F32))
        inner, add = norm_back(total, scaled, inverse, gain)
        gain_part = gain_part + add
        grad_tok[place, :] = (grad_hidden[rows, :] + inner).astype(BF16)
        g = Gather(links, p, lambda t: piece_at(grad_tok, t, piece))
        g.start(clock, piece[1] * D * 2)
        gathers.append(g)
        clock.work(0.6)
    row = lax.broadcasted_iota(jnp.int32, (8, D), 0)
    gains.start(jnp.where(row == 0, gain_part, 0.0) + jnp.where(row == 1, gain_part_two, 0.0))

    def turn():
        gains.step()
        if len(gains.copies) < len(gains.to):
            clock.later(clock.now + 3.0, turn)

    clock.later(clock.now + 3.0, turn)
    clock.drain()
    gain_sum[...] = gains.finish()
    for g in gathers:
        g.finish()
    sums.finish()
    for h in halvers:
        h.finish()


SOON = (4, 6, 7, 8, 9)
LATE = (11, 12) + tuple(range(14, 23))


def back_call(bits, levels, *args):
    outs = [
        ((2 * GH, BLOCK, 2 * GW), BF16),
        ((ROWS, D), BF16),
        ((4,) + FLAT, BF16),
        ((2, D // 2, D), BF16),
        ((D, CH), BF16),
        ((256, D), BF16),
        ((3, 384, 384), BF16),
        ((8, D), F32),
    ]
    room = lambda lead, rows, columns: pltpu.VMEM(
        lead + landing(rows, columns, bits).shape, BF16
    )
    scratch = [pltpu.VMEM(args[at].shape, args[at].dtype) for at in SOON + LATE] + [
        pltpu.VMEM((ROWS, D), BF16),
        pltpu.VMEM((LANES, CH), BF16),
        pltpu.VMEM((ROWS, D), BF16),
        pltpu.VMEM((PART, D), F32),
        pltpu.VMEM((PART, D), F32),
        pltpu.VMEM((ROWS, D), BF16),
    ] + scatter_scratch() + [
        pltpu.VMEM((4,) + FLAT, BF16),
        pltpu.VMEM((2, D // 2, D), BF16),
        pltpu.VMEM((D, CH), BF16),
        pltpu.VMEM((256, D), BF16),
        pltpu.VMEM((3, 384, 384), BF16),
        room((4,), *FLAT),
        room((2,), D // 2, D),
        room((), D, CH),
        room((), 256, D),
        room((3,), 384, 384),
        pltpu.VMEM((2 + bits, 8, D), F32),
        pltpu.VMEM((2 + bits, 8, D), F32),
        pltpu.VMEM((PART, D), BF16),
        pltpu.VMEM((ROWS, D // 2), BF16),
        pltpu.VMEM((D // 2, LANES), BF16),
        pltpu.VMEM((192, LANES), BF16),
        pltpu.VMEM((ROWS, HEAD_DIM), F32),
        pltpu.VMEM((ROWS, HEAD_DIM), F32),
        pltpu.VMEM((3 * 192, LANES), BF16),
        pltpu.VMEM((LANES, 3 * 192), BF16),
        pltpu.VMEM((3 * 192, D), BF16),
        pltpu.SemaphoreType.DMA((2 + len(LATE) + len(SOON),)),
    ] + sems(130)
    return call(
        functools.partial(back_kernel, levels), outs,
        [
            smem if at == 0 else anywhere if at in SOON + LATE + (3, 13, 23) else vmem
            for at in range(len(args))
        ],
        scratch, 3, 20_000_000_000, args,
    )


def write_kernel(
    out_all, grad_tok, conv, up, down, low, tap_all, ot, head, gains, joined_in,
    out_tokens, grad_tokens, conv_sum, up_sum, down_sum, out_sum, tap_sum, qkv_sum, gain_one,
    gain_two, joined,
):
    out_tokens[...] = out_all[0:SLOTS, :]
    grad_tokens[...] = grad_tok[0:SLOTS, :]
    joined[...] = joined_in[...]
    gain_one[...] = gains[0]
    gain_two[...] = gains[1]
    for j in range(4):
        for side in range(2):
            conv_sum[j, :, side * SLOT : (side + 1) * SLOT] = conv[
                j, side * WIDE : (side + 1) * WIDE, :
            ].astype(F32)
    for i in range(2):
        rows = slice(i * (D // 2), (i + 1) * (D // 2))
        up_sum[rows, :] = up[i].astype(F32)
        down_sum[rows, :] = down[i].astype(F32) + dot(low[rows, :], tap_all[...])
    out_sum[...] = ot[0:192, :].astype(F32)
    tap_sum[...] = ot[192:, :].astype(F32)
    for h in range(3):
        for part in range(3):
            for side in range(2):
                rows = side * 192 + part * 64
                qkv_sum[
                    part * 192 + h * 64 : part * 192 + h * 64 + 64, side * 384 : (side + 1) * 384
                ] = head[h, rows : rows + 64, :].astype(F32)


def write_call(*args):
    outs = [
        ((SLOTS, D), BF16),
        ((SLOTS, D), BF16),
        ((4, WIDE, CH), F32),
        ((D, D), F32),
        ((D, D), F32),
        ((192, D), F32),
        ((BLOCK, D), F32),
        ((3 * 192, D), F32),
        ((D,), F32),
        ((D,), F32),
        ((2 * GH, BLOCK, 2 * GW), BF16),
    ]
    return call(write_kernel, outs, [vmem] * 11, [], None, 400_000_000, args)


def per_device(
    bits, tokens, lengths, gain_one, gain_two, w_qkv, w_out, w_up, w_down, w_tap, w_conv,
    cot_tokens, cot_joined,
):
    w_heads = w_qkv.transpose(0, 2, 1).reshape(3 * 192, D)
    conv_w = w_conv.transpose(0, 1, 2, 4, 3).reshape(4, WIDE, CH)
    levels = {}
    (
        hidden_own, normed_two, q_cm, k_tm, v_tm, k_cm, lse, mixed, normed_one, slope, act,
        tap_all, w_out_all, conv_far, grad_own, out_own, field, down_part,
    ) = front_call(
        bits, levels, lengths, tokens, gain_one, gain_two, w_heads, w_out, w_tap.T, conv_w, w_up, w_down,
        cot_joined[0].transpose(0, 2, 1), cot_tokens,
    )
    result, tap_grad, g_conv, out_all, down = conv_call(
        bits, levels, lengths, field, conv_w, conv_far, grad_own, out_own, down_part
    )
    joined, grad_tok, conv, up, low, ot, head, gain_sum = back_call(
        bits, levels, lengths, tap_grad, tap_all, cot_tokens, slope, act, normed_two, w_up, w_down,
        hidden_own, gain_two, out_all, result, g_conv,
        w_out_all, mixed, q_cm, k_tm, v_tm, k_cm, lse, normed_one, w_heads, tokens, gain_one,
    )
    (
        out_tokens, grad_tokens, conv_sum, up_sum, down_sum, out_sum, tap_sum, qkv_sum, gain_a,
        gain_b, joined,
    ) = write_call(out_all, grad_tok, conv, up, down, low, tap_all, ot, head, gain_sum, joined)
    return (
        out_tokens,
        joined.transpose(0, 2, 1)[None],
        grad_tokens,
        qkv_sum.reshape(3, 192, D).transpose(0, 2, 1),
        out_sum,
        up_sum,
        down_sum,
        tap_sum.T,
        conv_sum.reshape(4, 3, 3, BLOCK, CH).transpose(0, 1, 2, 4, 3),
        gain_a,
        gain_b,
    )


def solution(mesh):
    placed = (
        P("dp", None),
        P("dp"),
        P(),
        P(),
        P(None, None, "tensor"),
        P("tensor", None),
        P(None, "tensor"),
        P("tensor", None),
        P(None, "tensor"),
        P(None, None, None, None, "tensor"),
        P("dp", None),
        P("dp", None, None, "tensor"),
    )
    return jax.shard_map(
        functools.partial(per_device, mesh.shape["dp"].bit_length() - 1),
        mesh=mesh,
        in_specs=placed,
        out_specs=(
            P("dp", None),
            P("dp", None, None, "tensor"),
            P("dp", None),
            P(None, None, "tensor"),
            P("tensor", None),
            P(None, "tensor"),
            P("tensor", None),
            P(None, "tensor"),
            P(None, None, None, None, "tensor"),
            P(),
            P(),
        ),
        check_vma=False,
    )
```
